32 devices in a mesh: leaf: 32 (over z, y, x, core).
Axes of the slice: x: 2, y: 2, z: 4, core: 2. Of those that a mesh axis runs over, the one named last changes fastest.
Arguments:
- points: float32 [16, 65536], P(None, 'leaf'), may hold values from -6 to 6
- order: int32 [65536], P('leaf'), may hold values from 0 to 65535, as said below
- bases: float32 [256, 256, 64], P('leaf'), may hold values from -0.375 to 0.375
- lift: float32 [256, 64, 64], P('leaf'), may hold values from -0.25 to 0.25
- near_ids: int32 [256, 3], P('leaf'), may hold values from 0 to 255, as said below
- near_blocks: float32 [256, 3, 256, 256], P('leaf'), may hold values from -0.21875 to 0.21875
- far_ids: int32 [256, 8], P('leaf'), may hold values from 0 to 255, as said below
- far_count: int32 [256], P('leaf'), may hold values from 1 to 8
- far_blocks: float32 [256, 8, 64, 64], P('leaf'), may hold values from -0.25 to 0.25
- transfer: float32 [4, 2, 64, 64], replicated, may hold values from -0.5 to 0.5
- couple: float32 [4, 4, 64, 64], replicated, may hold values from -0.375 to 0.375
- links: int32 [32, 4, 4], P('leaf'), may hold values from 0 to 1, as said below
- top_couple: float32 [64, 64], replicated, may hold values from -0.75 to 0.75
Outputs:
- product: float32 [16, 65536], P(None, 'leaf')
The draws below stay inside these ranges and needn't reach their ends.
Inputs may be any that keep to these rules, and one draw needn't show every extreme that they name: `order`: each subtree's 2048 entries are a permutation of that subtree's positions. `near_ids`: the first entry of a leaf is the leaf itself; the others lie at most one leaf away. `far_ids`: a coupled leaf lies in a subtree at most 4 subtrees away from the leaf's own; slots at or beyond far_count are padding. links[d, l, k] is the same for all d in one aligned block of 2^l subtrees.
All inputs are finite; a program needn't handle non-finite values.
Results may differ from the reference program's by a relative error of at most 0.0001.
Values sent between devices are 32-bit elements; how exact they have to be, the bound alone decides.
No kernel may reach another device: no remote copies, remote signals or barrier semaphores. Data moves between devices by JAX's collectives and lax.ppermute only.
A program may use at most 64 MiB of HBM per device.

```python
import jax
import jax.numpy as jnp
from jax import lax

LEAF = 256
RANK = 64
RHS = 16
LEAF_DEV = 8
NEAR = 3
CPL = 8
REACH = 4
DEPTH = 4
PTS_DEV = 2048
LEAVES = 256
POINTS = 65536
N_LEAF = 32


def draw_order(key, part):
    subkeys = jax.random.split(key, N_LEAF)
    shuffles = jax.vmap(lambda k: jax.random.permutation(k, PTS_DEV))(subkeys)
    offsets_dev = jnp.arange(N_LEAF, dtype=jnp.int32)[:, None] * PTS_DEV
    return (shuffles.astype(jnp.int32) + offsets_dev).reshape(-1)


def draw_near_ids(key, part):
    own_leaf = jnp.arange(LEAVES, dtype=jnp.int32)
    jumps = jax.random.randint(key, (LEAVES, NEAR - 1), -1, 2, dtype=jnp.int32)
    others = jnp.clip(own_leaf[:, None] + jumps, 0, LEAVES - 1)
    return jnp.concatenate([own_leaf[:, None], others], axis=1)


def draw_far_ids(key, part):
    own_device = jnp.arange(LEAVES, dtype=jnp.int32) // LEAF_DEV
    first_key, second_key = jax.random.split(jax.random.fold_in(key, 11))
    device_moves = jax.random.randint(first_key, (LEAVES, CPL), -REACH, REACH + 1, dtype=jnp.int32)
    target = jnp.clip(own_device[:, None] + device_moves, 0, N_LEAF - 1)
    within = jax.random.randint(second_key, (LEAVES, CPL), 0, LEAF_DEV, dtype=jnp.int32)
    partner = target * LEAF_DEV + within
    return partner.at[0, 0].set(REACH * LEAF_DEV)


def draw_far_count(key, part):
    counted = jax.random.randint(jax.random.fold_in(key, 23), (LEAVES,), 1, CPL + 1, dtype=jnp.int32)
    return counted.at[0].set(CPL).at[LEAVES - 1].set(1)


def draw_links(key, part):
    raw_bits = jax.random.randint(jax.random.fold_in(key, 37), (N_LEAF, DEPTH, 4), 0, 2, dtype=jnp.int32)
    devices = jnp.arange(N_LEAF, dtype=jnp.int32)[:, None]
    shifts = jnp.arange(DEPTH, dtype=jnp.int32)[None, :]
    block_start = jnp.left_shift(jnp.right_shift(devices, shifts), shifts)
    return raw_bits[block_start, shifts, :]


def block_levels(key, shape, pieces, low, high):
    loudness, own = 1.0, jax.random.fold_in(key, 6)
    for axis_at, blocks in pieces:
        heights = jnp.exp(jax.random.uniform(jax.random.fold_in(own, axis_at), (blocks,), jnp.float32, low / len(pieces), high / len(pieces)))
        loudness = loudness * jnp.repeat(heights, shape[axis_at] // blocks).reshape([-1 if axis == axis_at else 1 for axis in range(len(shape))])
    return loudness


def gaussian(stream_key, shape, scale, reach, shards=(), kind=jnp.bfloat16):
    factor_of = block_levels(stream_key, shape, shards, -0.22, 0.18) if shards else 1.0
    result = jax.random.normal(stream_key, shape, jnp.float32) * scale * factor_of
    return jnp.minimum(jnp.maximum(result, -reach), reach).astype(kind)


def setup_inputs(seed: int = 0) -> dict:
    arg_keys = jax.random.split(jax.random.key(seed), 14)
    return {
        "points": gaussian(arg_keys[0], (RHS, POINTS), 1.0, 6.0, ((1, 32),), jnp.float32),
        "order": draw_order(jax.random.fold_in(arg_keys[13], 71), 0),
        "bases": gaussian(arg_keys[2], (LEAVES, LEAF, RANK), LEAF ** -0.5, 0.375, ((0, 32),), jnp.float32),
        "lift": gaussian(arg_keys[3], (LEAVES, RANK, RANK), (RANK * LEAF_DEV) ** -0.5, 0.25, ((0, 32),), jnp.float32),
        "near_ids": draw_near_ids(jax.random.fold_in(arg_keys[13], 71), 0),
        "near_blocks": gaussian(arg_keys[5], (LEAVES, NEAR, LEAF, LEAF), (NEAR * LEAF) ** -0.5, 0.21875, ((0, 32),), jnp.float32),
        "far_ids": draw_far_ids(jax.random.fold_in(arg_keys[13], 71), 0),
        "far_count": draw_far_count(jax.random.fold_in(arg_keys[13], 71), 0),
        "far_blocks": gaussian(arg_keys[8], (LEAVES, CPL, RANK, RANK), (RANK * CPL) ** -0.5, 0.25, ((0, 32),), jnp.float32),
        "transfer": gaussian(arg_keys[9], (DEPTH, 2, RANK, RANK), (2 * RANK) ** -0.5, 0.5, (), jnp.float32),
        "couple": gaussian(arg_keys[10], (DEPTH, 4, RANK, RANK), (4 * RANK) ** -0.5, 0.375, (), jnp.float32),
        "links": draw_links(jax.random.fold_in(arg_keys[13], 71), 0),
        "top_couple": gaussian(arg_keys[12], (RANK, RANK), RANK ** -0.5, 0.75, (), jnp.float32),
    }


HIGHEST_PRECISION = lax.Precision.HIGHEST
OFFSETS = (-3, -2, 2, 3)


def full_tree(node_zero, link_table, transfer, couple, top_couple):
    levels = [node_zero]
    for level in range(DEPTH):
        current = levels[-1]
        paired = current.reshape(current.shape[0] // 2, 2, current.shape[1], current.shape[2])
        parent = jnp.einsum('rq,nrs->nqs', transfer[level, 0], paired[:, 0], precision=HIGHEST_PRECISION)
        parent = parent + jnp.einsum('rq,nrs->nqs', transfer[level, 1], paired[:, 1], precision=HIGHEST_PRECISION)
        levels.append(parent)
    couplings = []
    for level in range(DEPTH):
        current = levels[level]
        node_count = current.shape[0]
        chosen_links = link_table[::(1 << level), level, :].astype(jnp.float32)
        padded = jnp.pad(current, ((3, 3), (0, 0), (0, 0)))
        summed = jnp.zeros_like(current)
        for column, offset in enumerate(OFFSETS):
            partner = padded[3 + offset:3 + offset + node_count]
            term = jnp.einsum('qr,nrs->nqs', couple[level, column], partner, precision=HIGHEST_PRECISION)
            summed = summed + chosen_links[:, column][:, None, None] * term
        couplings.append(summed)
    top_nodes = levels[DEPTH]
    top_count = top_nodes.shape[0]
    spots = jnp.arange(top_count, dtype=jnp.int32)
    distance = jnp.abs(spots[:, None] - spots[None, :])
    weight = jnp.where(distance >= 2, 1.0 / jnp.maximum(distance, 1).astype(jnp.float32), 0.0).astype(jnp.float32)
    blended = jnp.einsum('nm,mrs->nrs', weight, top_nodes, precision=HIGHEST_PRECISION)
    downward = jnp.einsum('qr,nrs->nqs', top_couple, blended, precision=HIGHEST_PRECISION)
    for level in reversed(range(DEPTH)):
        even_part = jnp.einsum('rq,nqs->nrs', transfer[level, 0], downward, precision=HIGHEST_PRECISION)
        odd_part = jnp.einsum('rq,nqs->nrs', transfer[level, 1], downward, precision=HIGHEST_PRECISION)
        spread = jnp.stack([even_part, odd_part], axis=1).reshape(-1, downward.shape[1], downward.shape[2])
        downward = couplings[level] + spread
    return downward


def reference(points, order, bases, lift, near_ids, near_blocks, far_ids, far_count, far_blocks, transfer, couple, links, top_couple):
    vectors = points.shape[0]
    leaves = bases.shape[0]
    tree_x = jnp.take(points, order, axis=1)
    blocks = tree_x.reshape(vectors, leaves, LEAF)
    leaf_coef = jnp.einsum('lpr,slp->lrs', bases, blocks, precision=HIGHEST_PRECISION)
    lifted = jnp.einsum('lrq,lrs->lqs', lift, leaf_coef, precision=HIGHEST_PRECISION)
    node_zero = lifted.reshape(N_LEAF, LEAF_DEV, RANK, vectors).sum(axis=1)
    down_zero = full_tree(node_zero, links, transfer, couple, top_couple)
    down_leaf = jnp.repeat(down_zero, LEAF_DEV, axis=0)
    picked = jnp.take(leaf_coef, far_ids, axis=0)
    active = (jnp.arange(CPL, dtype=jnp.int32)[None, :] < far_count[:, None]).astype(jnp.float32)
    picked = picked * active[:, :, None, None]
    far_part = jnp.einsum('lkrq,lkqs->lrs', far_blocks, picked, precision=HIGHEST_PRECISION)
    leaf_out = jnp.einsum('lrq,lqs->lrs', lift, down_leaf, precision=HIGHEST_PRECISION) + far_part
    gathered = jnp.take(blocks, near_ids, axis=1)
    near_part = jnp.einsum('lkpq,slkq->slp', near_blocks, gathered, precision=HIGHEST_PRECISION)
    tree_y = near_part + jnp.einsum('lpr,lrs->slp', bases, leaf_out, precision=HIGHEST_PRECISION)
    tree_y = tree_y.reshape(vectors, -1)
    return jnp.zeros_like(points).at[:, order].set(tree_y)
```

```python
import functools

import jax
import jax.numpy as jnp
from jax import lax
from jax.experimental import pallas as pl
from jax.experimental.pallas import tpu as pltpu
from jax.sharding import PartitionSpec as P

REACH = 4
DEPTH = 4
OFFSETS = (-3, -2, 2, 3)
GROUP = 2 * REACH
LANES = 128
VMEM_LIMIT = 48 * 1024 * 1024

NN = (((1,), (0,)), ((), ()))
NT = (((1,), (1,)), ((), ()))

VMEM = pl.BlockSpec(memory_space=pltpu.VMEM)
SMEM = pl.BlockSpec(memory_space=pltpu.SMEM)


def halves(x):
    high = x.astype(jnp.bfloat16)
    low = (x - high.astype(jnp.float32)).astype(jnp.bfloat16)
    return high, low


def dot3(a, b, dims):
    a_high, a_low = halves(a)
    b_high, b_low = halves(b)
    rows = a.shape[0]
    both = lax.dot_general(
        jnp.concatenate([a_high, a_low], axis=0), b_high, dims, preferred_element_type=jnp.float32
    )
    cross = lax.dot_general(a_high, b_low, dims, preferred_element_type=jnp.float32)
    return both[:rows] + (both[rows:] + cross)


def fold(x):
    return jnp.concatenate([x[:8], x[8:]], axis=1)


def beside(p, q):
    rank = p.shape[1] // 2
    left = lax.broadcasted_iota(jnp.int32, p.shape, 1) < rank
    return jnp.concatenate(
        [
            jnp.where(left, p, pltpu.roll(q, rank, 1)),
            jnp.where(left, pltpu.roll(p, rank, 1), q),
        ],
        axis=0,
    )


def lane_gather(x, high, low):
    rows, columns = x.shape
    high = jnp.broadcast_to(high, (rows, LANES))
    low = jnp.broadcast_to(low, (rows, LANES))
    result = jnp.zeros((rows, LANES), x.dtype)
    for source in range(columns // LANES):
        tile = x[:, source * LANES : (source + 1) * LANES]
        moved = jnp.take_along_axis(tile, low, axis=1, mode="promise_in_bounds")
        result = jnp.where(high == source, moved, result)
    return result


def up_kernel(me_ref, points_ref, order_ref, bases_ref, lift_ref, near_out, wide_out, node_out, x_out):
    me = me_ref[0]
    leaf_dev, rank, leaf_size = bases_ref.shape
    vectors, points_dev = points_ref.shape
    tiles = points_dev // LANES
    points = points_ref[...]
    base = me * points_dev
    for t in range(tiles):
        spot = order_ref[t : t + 1, :] - base
        x_out[:, t * LANES : (t + 1) * LANES] = lane_gather(
            points, lax.shift_right_logical(spot, 7), spot & (LANES - 1)
        )
    coefs = []
    for leaf in range(leaf_dev):
        x_leaf = x_out[:, leaf * leaf_size : (leaf + 1) * leaf_size]
        coefs.append(dot3(x_leaf, bases_ref[leaf], NT))
    for leaf in range(leaf_dev):
        tile = fold(coefs[leaf])
        for peer in range(GROUP):
            near_out[peer, leaf * 8 : (leaf + 1) * 8, :] = tile
            wide_out[peer, leaf * 8 : (leaf + 1) * 8, :] = tile
    node = dot3(jnp.concatenate(coefs, axis=1), lift_ref[...].reshape(leaf_dev * rank, rank), NN)
    tile = fold(node)
    for peer in range(node_out.shape[0]):
        node_out[peer] = tile
    top = leaf_dev * 8
    half = leaf_size // LANES
    for out, place in ((near_out, lax.rem(me, GROUP)), (wide_out, lax.rem(me + REACH, GROUP))):
        for peer in range(GROUP):
            for part in range(half):
                first = x_out[:, part * LANES : (part + 1) * LANES]
                start = points_dev - leaf_size + part * LANES
                last = x_out[:, start : start + LANES]
                out[peer, top + part * vectors : top + (part + 1) * vectors, :] = jnp.where(
                    place < peer, last, first
                )


def inverse_kernel(me_ref, order_ref, inverse_out):
    points_dev = order_ref.shape[1]
    tiles = points_dev // LANES
    spot = order_ref[...] - me_ref[0] * points_dev
    high = lax.shift_right_logical(spot, 7)
    low = spot & (LANES - 1)
    times = lax.broadcasted_iota(jnp.int32, (1, points_dev), 1)
    shape = (tiles, points_dev)
    match = lax.broadcasted_iota(jnp.int32, shape, 0) == jnp.broadcast_to(high, shape)
    coarse = lax.shift_right_logical(times, 4).astype(jnp.float32)
    fine = (times & 15).astype(jnp.float32)
    left = jnp.concatenate(
        [
            jnp.where(match, jnp.broadcast_to(coarse, shape), 0.0),
            jnp.where(match, jnp.broadcast_to(fine, shape), 0.0),
        ],
        axis=0,
    ).astype(jnp.bfloat16)
    shape = (LANES, points_dev)
    right = jnp.where(
        lax.broadcasted_iota(jnp.int32, shape, 0) == jnp.broadcast_to(low, shape), 1.0, 0.0
    ).astype(jnp.bfloat16)
    both = lax.dot_general(left, right, NT, preferred_element_type=jnp.float32)
    inverse_out[...] = (both[:tiles] * 16.0 + both[tiles:]).astype(jnp.int32)


def near_kernel(me_ref, ids_ref, x_ref, blocks_ref, out_ref):
    leaf = pl.program_id(0)
    _, slots, leaf_size, _ = blocks_ref.shape
    leaf_dev = pl.num_programs(0)
    first = me_ref[0] * leaf_dev
    total = jnp.zeros(out_ref.shape[1:], jnp.float32)
    for slot in range(slots):
        local = ids_ref[leaf, slot] - first
        here = (local >= 0) & (local < leaf_dev)
        x_leaf = x_ref[jnp.clip(local, 0, leaf_dev - 1)]
        x_leaf = jnp.where(here, x_leaf, 0.0)
        total = total + dot3(x_leaf, blocks_ref[0, slot], NT)
    out_ref[0] = total


def down_kernel(
    me_ref,
    near_ids_ref,
    far_ids_ref,
    far_count_ref,
    links_ref,
    near_in,
    wide_in,
    nodes_in,
    near_part,
    inverse_ref,
    bases_ref,
    lift_ref,
    first_ref,
    last_ref,
    far_ref,
    transfer_ref,
    couple_ref,
    top_ref,
    out_ref,
    window,
    edges,
    y_tree,
    *levels,
):
    me = me_ref[0]
    leaf_dev, rank, leaf_size = bases_ref.shape
    slots = far_ids_ref.shape[1]
    vectors, points_dev = out_ref.shape
    count = nodes_in.shape[0]
    coef_rows = leaf_dev * 8
    parts = leaf_size // LANES
    place = lax.rem(me, GROUP)
    place_wide = lax.rem(me + REACH, GROUP)

    for index in range(2 * REACH + 1):
        offset = index - REACH
        inside = (place + offset >= 0) & (place + offset < GROUP)
        narrow = near_in[jnp.clip(place + offset, 0, GROUP - 1), :coef_rows]
        wide = wide_in[jnp.clip(place_wide + offset, 0, GROUP - 1), :coef_rows]
        window[index * leaf_dev : (index + 1) * leaf_dev] = jnp.where(inside, narrow, wide).reshape(
            leaf_dev, 8, LANES
        )
    window[(2 * REACH + 1) * leaf_dev] = jnp.zeros((8, LANES), jnp.float32)
    for index, offset in ((0, -1), (1, 1)):
        inside = (place + offset >= 0) & (place + offset < GROUP)
        narrow = near_in[jnp.clip(place + offset, 0, GROUP - 1), coef_rows:]
        wide = wide_in[jnp.clip(place_wide + offset, 0, GROUP - 1), coef_rows:]
        chosen = jnp.where(inside, narrow, wide)
        edges[index] = jnp.concatenate(
            [chosen[part * vectors : (part + 1) * vectors] for part in range(parts)], axis=1
        )

    for level in range(DEPTH):
        half = count >> (level + 1)
        source = nodes_in if level == 0 else levels[level - 1]
        pairs = [beside(source[2 * n], source[2 * n + 1]) for n in range(half)]
        weights = transfer_ref[level].reshape(2 * rank, rank)
        parents = dot3(jnp.concatenate(pairs, axis=0), weights, NN)
        for n in range(half):
            levels[level][n] = fold(parents[n * vectors : (n + 1) * vectors])

    top_count = count >> DEPTH
    node = lax.shift_right_logical(me, DEPTH)
    blended = jnp.zeros((8, LANES), jnp.float32)
    for other in range(top_count):
        distance = jnp.abs(node - other)
        weight = jnp.where(
            distance >= 2, 1.0 / jnp.maximum(distance, 1).astype(jnp.float32), 0.0
        )
        blended = blended + weight * levels[DEPTH - 1][other]
    down = dot3(beside(blended, blended)[:, :rank], top_ref[...], NT)
    for level in reversed(range(DEPTH)):
        node = lax.shift_right_logical(me, level)
        size = count >> level
        source = nodes_in if level == 0 else levels[level - 1]
        partners = []
        for column, offset in enumerate(OFFSETS):
            other = node + offset
            used = (other >= 0) & (other < size)
            weight = jnp.where(used, links_ref[level, column], 0).astype(jnp.float32)
            partners.append(weight * source[jnp.clip(other, 0, size - 1)])
        left = jnp.concatenate(
            [beside(partners[0], partners[1]), beside(partners[2], partners[3])], axis=1
        )
        weights = jnp.concatenate([couple_ref[level, column] for column in range(4)], axis=1)
        out = dot3(left, weights, NT)
        down = out + dot3(down, transfer_ref[level, lax.rem(node, 2)], NT)

    zero_slot = (2 * REACH + 1) * leaf_dev
    for leaf in range(leaf_dev):
        picked = []
        for slot in range(slots):
            spot = far_ids_ref[leaf, slot] - (me - REACH) * leaf_dev
            used = (slot < far_count_ref[leaf]) & (spot >= 0) & (spot < zero_slot)
            picked.append(window[jnp.where(used, spot, zero_slot)])
        left = jnp.concatenate(
            [beside(picked[slot], picked[slot + 1]) for slot in range(0, slots, 2)] + [down], axis=1
        )
        weights = jnp.concatenate(
            [far_ref[leaf, slot] for slot in range(slots)] + [lift_ref[leaf]], axis=1
        )
        leaf_out = dot3(left, weights, NT)
        y_leaf = near_part[leaf] + dot3(leaf_out, bases_ref[leaf], NN)
        y_tree[:, leaf * leaf_size : (leaf + 1) * leaf_size] = y_leaf
    for leaf, outside, index, blocks in (
        (0, -1, 0, first_ref),
        (leaf_dev - 1, leaf_dev, 1, last_ref),
    ):
        total = jnp.zeros((vectors, leaf_size), jnp.float32)
        for slot in range(1, blocks.shape[1]):
            remote = near_ids_ref[leaf, slot] - me * leaf_dev == outside
            total = total + dot3(jnp.where(remote, edges[index], 0.0), blocks[0, slot], NT)
        start = leaf * leaf_size
        y_tree[:, start : start + leaf_size] = y_tree[:, start : start + leaf_size] + total

    y = y_tree[...]
    for tile in range(points_dev // LANES):
        spot = inverse_ref[tile : tile + 1, :]
        out_ref[:, tile * LANES : (tile + 1) * LANES] = lane_gather(
            y, lax.shift_right_logical(spot, 7), spot & (LANES - 1)
        )


def local(
    devices,
    points,
    order,
    bases,
    lift,
    near_ids,
    near_blocks,
    far_ids,
    far_count,
    far_blocks,
    transfer,
    couple,
    links,
    top_couple,
):
    me = lax.axis_index("leaf").astype(jnp.int32).reshape(1)
    vectors, points_dev = points.shape
    leaf_dev, leaf_size, rank = bases.shape
    slots = near_ids.shape[1]
    bases_t = jnp.swapaxes(bases, 1, 2)
    tiles = points_dev // LANES
    rows = leaf_dev * 8 + vectors * (leaf_size // LANES)
    params = pltpu.CompilerParams(vmem_limit_bytes=VMEM_LIMIT)
    f32 = jnp.float32

    near_out, wide_out, node_out, tree_x = pl.pallas_call(
        up_kernel,
        out_shape=[
            jax.ShapeDtypeStruct((GROUP, rows, LANES), f32),
            jax.ShapeDtypeStruct((GROUP, rows, LANES), f32),
            jax.ShapeDtypeStruct((devices, 8, LANES), f32),
            jax.ShapeDtypeStruct((vectors, points_dev), f32),
        ],
        in_specs=[SMEM] + [VMEM] * 4,
        out_specs=[VMEM] * 4,
        compiler_params=params,
        name="up",
    )(me, points, order.reshape(tiles, LANES), bases_t, lift)

    narrow_groups = [[g * GROUP + i for i in range(GROUP)] for g in range(devices // GROUP)]
    wide_groups = [
        [(g * GROUP - REACH + i) % devices for i in range(GROUP)] for g in range(devices // GROUP)
    ]
    nodes_in = lax.all_to_all(node_out, "leaf", 0, 0, tiled=True)
    near_in = lax.all_to_all(near_out, "leaf", 0, 0, axis_index_groups=narrow_groups, tiled=True)
    wide_in = lax.all_to_all(wide_out, "leaf", 0, 0, axis_index_groups=wide_groups, tiled=True)

    inverse = pl.pallas_call(
        inverse_kernel,
        out_shape=jax.ShapeDtypeStruct((tiles, LANES), jnp.int32),
        in_specs=[SMEM, VMEM],
        out_specs=VMEM,
        compiler_params=params,
        name="inverse",
    )(me, order.reshape(1, points_dev))

    x_leaves = tree_x.reshape(vectors, leaf_dev, leaf_size).swapaxes(0, 1)
    near_part = pl.pallas_call(
        near_kernel,
        grid=(leaf_dev,),
        out_shape=jax.ShapeDtypeStruct((leaf_dev, vectors, leaf_size), f32),
        in_specs=[
            SMEM,
            SMEM,
            pl.BlockSpec((leaf_dev, vectors, leaf_size), lambda i: (0, 0, 0)),
            pl.BlockSpec((1, slots, leaf_size, leaf_size), lambda i: (i, 0, 0, 0)),
        ],
        out_specs=pl.BlockSpec((1, vectors, leaf_size), lambda i: (i, 0, 0)),
        compiler_params=params,
        cost_estimate=pl.CostEstimate(
            flops=6 * vectors * near_blocks.size, bytes_accessed=4 * near_blocks.size, transcendentals=0
        ),
        name="near",
    )(me, near_ids, x_leaves, near_blocks)

    def edge(block):
        return pl.BlockSpec((1, slots, leaf_size, leaf_size), lambda i: (block, 0, 0, 0))

    def whole(shape):
        return pl.BlockSpec(shape, lambda i: (0,) * len(shape))

    operands = (near_in, wide_in, nodes_in, near_part, inverse, bases_t, lift)
    after = (far_blocks, transfer, couple, top_couple)
    return pl.pallas_call(
        down_kernel,
        grid=(1,),
        out_shape=jax.ShapeDtypeStruct((vectors, points_dev), f32),
        in_specs=[SMEM] * 5
        + [whole(x.shape) for x in operands]
        + [edge(0), edge(leaf_dev - 1)]
        + [whole(x.shape) for x in after],
        out_specs=whole((vectors, points_dev)),
        scratch_shapes=[
            pltpu.VMEM(((2 * REACH + 1) * leaf_dev + 1, 8, LANES), f32),
            pltpu.VMEM((2, vectors, leaf_size), f32),
            pltpu.VMEM((vectors, points_dev), f32),
        ]
        + [pltpu.VMEM((devices >> (level + 1), 8, LANES), f32) for level in range(DEPTH)],
        compiler_params=params,
        name="down",
    )(
        me,
        near_ids,
        far_ids,
        far_count,
        links.reshape(links.shape[1:]),
        *operands,
        near_blocks,
        near_blocks,
        *after,
    )


def solution(mesh):
    in_specs = (
        P(None, "leaf"),
        P("leaf"),
        P("leaf", None, None),
        P("leaf", None, None),
        P("leaf", None),
        P("leaf", None, None, None),
        P("leaf", None),
        P("leaf"),
        P("leaf", None, None, None),
        P(),
        P(),
        P("leaf", None, None),
        P(),
    )
    return jax.shard_map(
        functools.partial(local, mesh.shape["leaf"]),
        mesh=mesh,
        in_specs=in_specs,
        out_specs=P(None, "leaf"),
        check_vma=False,
    )
```

```python
import functools

import jax
import jax.numpy as jnp
from jax import lax
from jax.experimental import pallas as pl
from jax.experimental.pallas import tpu as pltpu
from jax.sharding import PartitionSpec as P

REACH = 4
DEPTH = 4
OFFSETS = (-3, -2, 2, 3)
GROUP = 2 * REACH
LANES = 128
TILE = 8
VMEM_LIMIT = 24 * 1024 * 1024

NN = (((1,), (0,)), ((), ()))
NT = (((1,), (1,)), ((), ()))

VMEM = pl.BlockSpec(memory_space=pltpu.VMEM)
SMEM = pl.BlockSpec(memory_space=pltpu.SMEM)
HBM = pl.BlockSpec(memory_space=pltpu.HBM)
PARAMS = pltpu.CompilerParams(vmem_limit_bytes=VMEM_LIMIT)
F32 = jnp.float32
BF16 = jnp.bfloat16


def halves(x):
    high = x.astype(BF16)
    low = (x - high.astype(F32)).astype(BF16)
    return high, low


def dot_halves(a, b_high, b_low, dims):
    a_high, a_low = halves(a)
    rows = a.shape[0]
    both = lax.dot_general(
        jnp.concatenate([a_high, a_low], axis=0), b_high, dims, preferred_element_type=F32
    )
    cross = lax.dot_general(a_high, b_low, dims, preferred_element_type=F32)
    return both[:rows] + (both[rows:] + cross)


def dot3(a, b, dims):
    return dot_halves(a, *halves(b), dims)


def fold(x):
    return jnp.concatenate([x[:TILE], x[TILE:]], axis=1)


def beside(p, q):
    rank = p.shape[1] // 2
    left = lax.broadcasted_iota(jnp.int32, p.shape, 1) < rank
    return jnp.concatenate(
        [
            jnp.where(left, p, pltpu.roll(q, rank, 1)),
            jnp.where(left, pltpu.roll(p, rank, 1), q),
        ],
        axis=0,
    )


def row_of(tiles):
    return jnp.concatenate([beside(*tiles[k : k + 2]) for k in range(0, len(tiles), 2)], axis=1)


def lane_gather(x, high, low):
    rows, columns = x.shape
    high = jnp.broadcast_to(high, (rows, LANES))
    low = jnp.broadcast_to(low, (rows, LANES))
    result = jnp.zeros((rows, LANES), x.dtype)
    for source in range(columns // LANES):
        tile = x[:, source * LANES : (source + 1) * LANES]
        moved = jnp.take_along_axis(tile, low, axis=1, mode="promise_in_bounds")
        result = jnp.where(high == source, moved, result)
    return result


def fetch(pairs, sems):
    copies = [
        pltpu.make_async_copy(source, target, sems.at[index])
        for index, (source, target) in enumerate(pairs)
    ]
    for copy in copies:
        copy.start()
    return copies


def up_kernel(
    me_ref, points_hbm, order_hbm, bases_hbm, lift_hbm, out, x_out, points_v, order_v, bases_v, lift_v, sems
):
    copies = fetch(
        [(order_hbm, order_v), (points_hbm, points_v), (bases_hbm, bases_v), (lift_hbm, lift_v)], sems
    )
    me = me_ref[0]
    leaf_dev, rank, leaf_size = bases_v.shape
    vectors, points_dev = points_v.shape
    copies[0].wait()
    copies[1].wait()
    points = points_v[...]
    per_leaf = leaf_size // LANES
    for t in range(points_dev // LANES):
        spot = order_v[t : t + 1, :] - me * points_dev
        column = t % per_leaf * LANES
        x_out[t // per_leaf, :, column : column + LANES] = lane_gather(
            points, lax.shift_right_logical(spot, 7), spot & (LANES - 1)
        )
    copies[2].wait()
    coefs = [dot3(x_out[leaf], bases_v[leaf], NT) for leaf in range(leaf_dev)]
    tiles = [fold(coef) for coef in coefs]
    copies[3].wait()
    weights = lift_v[...].reshape(leaf_dev * rank, rank)
    tiles.append(fold(dot3(jnp.concatenate(coefs, axis=1), weights, NN)))
    for peer in range(GROUP):
        for index, tile in enumerate(tiles):
            out[peer, index * TILE : (index + 1) * TILE, :] = tile
    place = lax.rem(me, GROUP)
    start = len(tiles) * TILE
    for part in range(per_leaf):
        first = x_out[0, :, part * LANES : (part + 1) * LANES]
        last = x_out[leaf_dev - 1, :, part * LANES : (part + 1) * LANES]
        rows = slice(start + part * vectors, start + (part + 1) * vectors)
        for peer in range(GROUP):
            above = lax.rem(place + 1, GROUP) == peer
            out[peer, rows, :] = jnp.where(above, last, first)


def side_kernel(
    me_ref,
    x_ref,
    order_hbm,
    ids_hbm,
    links_hbm,
    blocks_hbm,
    bases_hbm,
    lift_hbm,
    far_hbm,
    transfer_hbm,
    couple_hbm,
    top_hbm,
    near_out,
    inverse_out,
    edge_high,
    edge_low,
    leaf_high,
    leaf_low,
    bases_high,
    bases_low,
    up_high,
    up_low,
    path_high,
    path_low,
    order_v,
    ids_s,
    links_s,
    blocks_v,
    bases_v,
    lift_v,
    far_v,
    transfer_v,
    couple_v,
    top_v,
    sems,
    block_sems,
):
    me = me_ref[0]
    leaf_dev, slots, leaf_size, _ = blocks_v.shape
    _, rank, _ = bases_v.shape
    small = fetch(
        [
            (ids_hbm, ids_s),
            (links_hbm, links_s),
            (order_hbm, order_v),
            (transfer_hbm, transfer_v),
            (couple_hbm, couple_v),
            (top_hbm, top_v),
            (lift_hbm, lift_v),
            (far_hbm, far_v),
            (bases_hbm, bases_v),
        ],
        sems,
    )
    blocks = fetch([(blocks_hbm.at[leaf], blocks_v.at[leaf]) for leaf in range(leaf_dev)], block_sems)
    for copy in small:
        copy.wait()

    points_dev = order_v.shape[1]
    tiles = points_dev // LANES
    spot = order_v[...] - me * points_dev
    times = lax.broadcasted_iota(jnp.int32, (1, points_dev), 1)
    shape = (tiles, points_dev)
    match = lax.broadcasted_iota(jnp.int32, shape, 0) == lax.shift_right_logical(spot, 7)
    digits = [
        jnp.where(match, jnp.broadcast_to(digit.astype(F32), shape), 0.0)
        for digit in (lax.shift_right_logical(times, 4), times & 15)
    ]
    shape = (LANES, points_dev)
    match = lax.broadcasted_iota(jnp.int32, shape, 0) == (spot & (LANES - 1))
    both = lax.dot_general(
        jnp.concatenate(digits, axis=0).astype(BF16),
        jnp.where(match, 1.0, 0.0).astype(BF16),
        NT,
        preferred_element_type=F32,
    )
    inverse_out[...] = (both[:tiles] * 16.0 + both[tiles:]).astype(jnp.int32)

    composed = transfer_v[0].reshape(2 * rank, rank)
    row = 0
    for level in range(1, DEPTH):
        rows = composed.shape[0]
        up_high[row : row + rows], up_low[row : row + rows] = halves(composed)
        row += rows
        if level < DEPTH - 1:
            composed = jnp.concatenate(
                [dot3(composed, transfer_v[level, side], NN) for side in range(2)], axis=0
            )

    path = None
    for level in range(DEPTH):
        weights = []
        for column in range(len(OFFSETS)):
            link = links_s[level, column].astype(F32)
            weights.append(link * couple_v[level, column])
        weights = jnp.concatenate(weights, axis=1)
        step = transfer_v[level, lax.shift_right_logical(me, level) & 1]
        if path is not None:
            weights = dot3(path, weights, NN)
            step = dot3(path, step, NN)
        path = step
        column = level * len(OFFSETS) * rank
        span = slice(column, column + weights.shape[1])
        path_high[:, span], path_low[:, span] = halves(weights)
    top = dot3(path, top_v[...], NN)
    last = jnp.concatenate(
        [dot3(top, transfer_v[DEPTH - 1, side], NT) for side in range(2)], axis=1
    )
    column = DEPTH * len(OFFSETS) * rank
    span = slice(column, column + 2 * rank)
    path_high[:, span], path_low[:, span] = halves(last)

    for leaf in range(leaf_dev):
        row = [far_v[leaf, slot] for slot in range(far_v.shape[1])] + [lift_v[leaf]]
        leaf_high[leaf], leaf_low[leaf] = halves(jnp.concatenate(row, axis=1))
        bases_high[leaf], bases_low[leaf] = halves(bases_v[leaf])

    for copy in blocks:
        copy.wait()

    def near(leaf, carry):
        total = jnp.zeros(near_out.shape[1:], F32)
        for slot in range(slots):
            local = ids_s[slot, leaf] - me * leaf_dev
            here = (local >= 0) & (local < leaf_dev)
            x_leaf = jnp.where(here, x_ref[jnp.clip(local, 0, leaf_dev - 1)], 0.0)
            total = total + dot3(x_leaf, blocks_v[leaf, slot], NT)
        near_out[leaf] = total
        return carry

    lax.fori_loop(0, leaf_dev, near, 0)

    for index, leaf, outside in ((0, 0, -1), (1, leaf_dev - 1, leaf_dev)):
        total = jnp.zeros((leaf_size, leaf_size), F32)
        for slot in range(1, slots):
            remote = ids_s[slot, leaf] - me * leaf_dev == outside
            total = total + jnp.where(remote, blocks_v[leaf, slot], 0.0)
        edge_high[index], edge_low[index] = halves(total)


def middle_kernel(me_ref, group_ref, up_high, up_low, nodes_out, half_out):
    place = lax.rem(me_ref[0], GROUP)
    roots = [group_ref[peer, 8 * TILE : 9 * TILE, :] for peer in range(GROUP)]
    start, index = 0, 0
    for level in range(1, DEPTH):
        width = 1 << level
        count = GROUP // width
        left = jnp.concatenate(
            [row_of(roots[n * width : (n + 1) * width]) for n in range(count)], axis=0
        )
        size = left.shape[1]
        nodes = dot_halves(left, up_high[start : start + size], up_low[start : start + size], NN)
        start += size
        for n in range(count):
            nodes_out[index] = fold(nodes[n * 2 * TILE : (n + 1) * 2 * TILE])
            index += 1
    nodes_out[index] = jnp.zeros((TILE, LANES), F32)
    low = place < REACH
    for part in range(REACH):
        chosen = group_ref[jnp.where(low, REACH, 0) + part, : 9 * TILE]
        half_out[part * 9 * TILE : (part + 1) * 9 * TILE] = chosen
    half_out[REACH * 9 * TILE :] = group_ref[jnp.where(low, GROUP - 1, 0), 9 * TILE :]


def down_kernel(
    me_ref,
    group_ref,
    half_ref,
    nodes_ref,
    near_ref,
    inverse_ref,
    edge_high,
    edge_low,
    leaf_high,
    leaf_low,
    bases_high,
    bases_low,
    path_high,
    path_low,
    far_ids_hbm,
    far_count_hbm,
    out_ref,
    far_ids_s,
    far_count_s,
    y_tree,
    sems,
):
    copies = fetch([(far_ids_hbm, far_ids_s), (far_count_hbm, far_count_s)], sems)
    me = me_ref[0]
    leaf_dev, vectors, leaf_size = near_ref.shape
    points_dev = out_ref.shape[1]
    groups = nodes_ref.shape[0]
    slots = far_ids_s.shape[1]
    group = lax.shift_right_logical(me, 3)
    place = me & (GROUP - 1)
    low = place < REACH
    per_leaf = leaf_size // LANES
    start = (leaf_dev + 1) * TILE

    def tile_of(subtree, index):
        other = subtree & (GROUP - 1)
        inside = lax.shift_right_arithmetic(subtree, 3) == group
        row = pl.multiple_of(index * TILE, TILE)
        near_row = jnp.clip(other - jnp.where(low, REACH, 0), 0, REACH - 1) * start
        here = group_ref[other, pl.ds(row, TILE), :]
        there = half_ref[pl.ds(pl.multiple_of(near_row + row, TILE), TILE), :]
        return jnp.where(inside, here, there)

    partners = []
    for level in range(DEPTH):
        node = lax.shift_right_logical(me, level)
        size = (groups * GROUP) >> level
        for offset in OFFSETS:
            other = node + offset
            used = (other >= 0) & (other < size)
            other = jnp.clip(other, 0, size - 1)
            if level == 0:
                tile = tile_of(other, leaf_dev)
            else:
                shift = DEPTH - 1 - level
                first = GROUP - (2 << shift)
                tile = nodes_ref[
                    lax.shift_right_logical(other, shift), first + (other & ((1 << shift) - 1))
                ]
            partners.append(jnp.where(used, tile, 0.0))
    top = lax.shift_right_logical(me, DEPTH)
    for side in range(2):
        blended = jnp.zeros((TILE, LANES), F32)
        for other in range(groups // 2):
            distance = jnp.abs(top - other)
            weight = jnp.where(distance >= 2, 1.0 / jnp.maximum(distance, 1).astype(F32), 0.0)
            blended = blended + weight * nodes_ref[2 * other + side, GROUP - 2]
        partners.append(blended)
    down = dot_halves(row_of(partners), path_high[...], path_low[...], NT)

    edges = []
    for index, offset in ((0, -1), (1, 1)):
        other = me + offset
        inside = lax.shift_right_arithmetic(other, 3) == group
        here = group_ref[other & (GROUP - 1), start:, :]
        chosen = jnp.where(inside, here, half_ref[REACH * start :, :])
        edges.append(
            jnp.concatenate(
                [chosen[part * vectors : (part + 1) * vectors] for part in range(per_leaf)], axis=1
            )
        )
    edge_parts = [
        dot_halves(edges[index], edge_high[index], edge_low[index], NT) for index in range(2)
    ]

    for copy in copies:
        copy.wait()
    for leaf in range(leaf_dev):
        picked = []
        for slot in range(slots):
            used = slot < far_count_s[leaf]
            spot = far_ids_s[leaf, slot]
            tile = tile_of(lax.shift_right_logical(spot, 3), spot & (leaf_dev - 1))
            picked.append(jnp.where(used, tile, 0.0))
        left = jnp.concatenate([row_of(picked), down], axis=1)
        leaf_out = dot_halves(left, leaf_high[leaf], leaf_low[leaf], NT)
        y_leaf = near_ref[leaf] + dot_halves(leaf_out, bases_high[leaf], bases_low[leaf], NN)
        if leaf == 0:
            y_leaf = y_leaf + edge_parts[0]
        if leaf == leaf_dev - 1:
            y_leaf = y_leaf + edge_parts[1]
        y_tree[:, leaf * leaf_size : (leaf + 1) * leaf_size] = y_leaf

    y = y_tree[...]
    for tile in range(points_dev // LANES):
        spot = inverse_ref[tile : tile + 1, :]
        out_ref[:, tile * LANES : (tile + 1) * LANES] = lane_gather(
            y, lax.shift_right_logical(spot, 7), spot & (LANES - 1)
        )


def local(
    devices,
    points,
    order,
    bases,
    lift,
    near_ids,
    near_blocks,
    far_ids,
    far_count,
    far_blocks,
    transfer,
    couple,
    links,
    top_couple,
):
    me = lax.axis_index("leaf").astype(jnp.int32).reshape(1)
    vectors, points_dev = points.shape
    leaf_dev, leaf_size, rank = bases.shape
    slots = near_ids.shape[1]
    far_slots = far_ids.shape[1]
    bases_t = jnp.swapaxes(bases, 1, 2)
    tiles = points_dev // LANES
    edge_rows = vectors * (leaf_size // LANES)
    rows = (leaf_dev + 1) * TILE
    groups = devices // GROUP
    order_tiles = order.reshape(tiles, LANES)
    shape = jax.ShapeDtypeStruct

    group_out, tree_x = pl.pallas_call(
        up_kernel,
        out_shape=[
            shape((GROUP, rows + edge_rows, LANES), F32),
            shape((leaf_dev, vectors, leaf_size), F32),
        ],
        in_specs=[SMEM] + [HBM] * 4,
        out_specs=[VMEM] * 2,
        scratch_shapes=[
            pltpu.VMEM(points.shape, F32),
            pltpu.VMEM((tiles, LANES), jnp.int32),
            pltpu.VMEM(bases_t.shape, F32),
            pltpu.VMEM(lift.shape, F32),
            pltpu.SemaphoreType.DMA((4,)),
        ],
        compiler_params=PARAMS,
        name="up",
    )(me, points, order_tiles, bases_t, lift)

    aligned = [[g * GROUP + i for i in range(GROUP)] for g in range(groups)]
    group_in = lax.all_to_all(group_out, "leaf", 0, 0, axis_index_groups=aligned, tiled=True)

    ids_t = near_ids.T
    links_own = links.reshape(links.shape[1:])
    composed_rows = (2 + 4 + 8) * rank
    path_columns = (DEPTH * len(OFFSETS) + 2) * rank
    leaf_columns = (far_slots + 1) * rank
    both = lambda *size: [shape(size, BF16)] * 2
    operands = (
        order.reshape(1, points_dev),
        ids_t,
        links_own,
        near_blocks,
        bases_t,
        lift,
        far_blocks,
        transfer,
        couple,
        top_couple,
    )
    (
        near_part,
        inverse,
        edge_high,
        edge_low,
        leaf_high,
        leaf_low,
        bases_high,
        bases_low,
        up_high,
        up_low,
        path_high,
        path_low,
    ) = pl.pallas_call(
        side_kernel,
        out_shape=[shape(tree_x.shape, F32), shape((tiles, LANES), jnp.int32)]
        + both(2, leaf_size, leaf_size)
        + both(leaf_dev, rank, leaf_columns)
        + both(leaf_dev, rank, leaf_size)
        + both(composed_rows, rank)
        + both(rank, path_columns),
        in_specs=[SMEM, VMEM] + [HBM] * len(operands),
        out_specs=[VMEM] * 12,
        scratch_shapes=[
            (pltpu.SMEM if x is ids_t or x is links_own else pltpu.VMEM)(x.shape, x.dtype)
            for x in operands
        ]
        + [pltpu.SemaphoreType.DMA((len(operands) - 1,)), pltpu.SemaphoreType.DMA((leaf_dev,))],
        compiler_params=PARAMS,
        cost_estimate=pl.CostEstimate(
            flops=6 * vectors * near_blocks.size,
            bytes_accessed=4 * near_blocks.size,
            transcendentals=0,
        ),
        name="side",
    )(me, tree_x, *operands)

    nodes_out, half_out = pl.pallas_call(
        middle_kernel,
        out_shape=[shape((GROUP, TILE, LANES), F32), shape((REACH * rows + edge_rows, LANES), F32)],
        in_specs=[SMEM] + [VMEM] * 3,
        out_specs=[VMEM] * 2,
        compiler_params=PARAMS,
        name="middle",
    )(me, group_in, up_high, up_low)

    pairs = []
    for device in range(devices):
        target = device + GROUP if device % GROUP < REACH else device - GROUP
        if 0 <= target < devices:
            pairs.append((device, target))
    half_in = lax.ppermute(half_out, "leaf", pairs)
    across = [[g * GROUP + i for g in range(groups)] for i in range(GROUP)]
    nodes_in = lax.all_gather(nodes_out, "leaf", axis=0, axis_index_groups=across)

    return pl.pallas_call(
        down_kernel,
        out_shape=shape((vectors, points_dev), F32),
        in_specs=[SMEM] + [VMEM] * 13 + [HBM] * 2,
        out_specs=VMEM,
        scratch_shapes=[
            pltpu.SMEM(far_ids.shape, jnp.int32),
            pltpu.SMEM(far_count.shape, jnp.int32),
            pltpu.VMEM((vectors, points_dev), F32),
            pltpu.SemaphoreType.DMA((2,)),
        ],
        compiler_params=PARAMS,
        name="down",
    )(
        me,
        group_in,
        half_in,
        nodes_in,
        near_part,
        inverse,
        edge_high,
        edge_low,
        leaf_high,
        leaf_low,
        bases_high,
        bases_low,
        path_high,
        path_low,
        far_ids,
        far_count,
    )


def solution(mesh):
    in_specs = (
        P(None, "leaf"),
        P("leaf"),
        P("leaf", None, None),
        P("leaf", None, None),
        P("leaf", None),
        P("leaf", None, None, None),
        P("leaf", None),
        P("leaf"),
        P("leaf", None, None, None),
        P(),
        P(),
        P("leaf", None, None),
        P(),
    )
    return jax.shard_map(
        functools.partial(local, mesh.shape["leaf"]),
        mesh=mesh,
        in_specs=in_specs,
        out_specs=P(None, "leaf"),
        check_vma=False,
    )
```

```python
import functools

import jax
import jax.numpy as jnp
from jax import lax
from jax.experimental import pallas as pl
from jax.experimental.pallas import tpu as pltpu
from jax.sharding import PartitionSpec as P

REACH = 4
DEPTH = 4
OFFSETS = (-3, -2, 2, 3)
GROUP = 2 * REACH
LANES = 128
TILE = 8
VMEM_LIMIT = 64 * 1024 * 1024

NN = (((1,), (0,)), ((), ()))
NT = (((1,), (1,)), ((), ()))

VMEM = pl.BlockSpec(memory_space=pltpu.VMEM)
SMEM = pl.BlockSpec(memory_space=pltpu.SMEM)
HBM = pl.BlockSpec(memory_space=pltpu.HBM)
PARAMS = pltpu.CompilerParams(vmem_limit_bytes=VMEM_LIMIT)
F32 = jnp.float32
BF16 = jnp.bfloat16


def halves(x):
    high = x.astype(BF16)
    low = (x - high.astype(F32)).astype(BF16)
    return high, low


def dot_halves(a, b_high, b_low, dims):
    a_high, a_low = halves(a)
    rows = a.shape[0]
    both = lax.dot_general(
        jnp.concatenate([a_high, a_low], axis=0), b_high, dims, preferred_element_type=F32
    )
    cross = lax.dot_general(a_high, b_low, dims, preferred_element_type=F32)
    return both[:rows] + (both[rows:] + cross)


def dot3(a, b, dims):
    return dot_halves(a, *halves(b), dims)


def fold(x):
    return jnp.concatenate([x[:TILE], x[TILE:]], axis=1)


def beside(p, q):
    rank = p.shape[1] // 2
    left = lax.broadcasted_iota(jnp.int32, p.shape, 1) < rank
    return jnp.concatenate(
        [
            jnp.where(left, p, pltpu.roll(q, rank, 1)),
            jnp.where(left, pltpu.roll(p, rank, 1), q),
        ],
        axis=0,
    )


def row_of(tiles):
    return jnp.concatenate([beside(*tiles[k : k + 2]) for k in range(0, len(tiles), 2)], axis=1)


def lane_gather(x, high, low):
    rows, columns = x.shape
    high = jnp.broadcast_to(high, (rows, LANES))
    low = jnp.broadcast_to(low, (rows, LANES))
    result = jnp.zeros((rows, LANES), x.dtype)
    for source in range(columns // LANES):
        tile = x[:, source * LANES : (source + 1) * LANES]
        moved = jnp.take_along_axis(tile, low, axis=1, mode="promise_in_bounds")
        result = jnp.where(high == source, moved, result)
    return result


def fetch(pairs, sems):
    copies = [
        pltpu.make_async_copy(source, target, sems.at[index])
        for index, (source, target) in enumerate(pairs)
    ]
    for copy in copies:
        copy.start()
    return copies


def up_kernel(
    me_ref, points_hbm, order_hbm, bases_hbm, lift_hbm, out, x_out, points_v, order_v, bases_v, lift_v, sems
):
    copies = fetch(
        [(order_hbm, order_v), (points_hbm, points_v), (bases_hbm, bases_v), (lift_hbm, lift_v)], sems
    )
    me = me_ref[0]
    leaf_dev, rank, leaf_size = bases_v.shape
    vectors, points_dev = points_v.shape
    copies[0].wait()
    copies[1].wait()
    points = points_v[...]
    per_leaf = leaf_size // LANES
    for t in range(points_dev // LANES):
        spot = order_v[t : t + 1, :] - me * points_dev
        column = t % per_leaf * LANES
        x_out[t // per_leaf, :, column : column + LANES] = lane_gather(
            points, lax.shift_right_logical(spot, 7), spot & (LANES - 1)
        )
    copies[2].wait()
    coefs = [dot3(x_out[leaf], bases_v[leaf], NT) for leaf in range(leaf_dev)]
    tiles = [fold(coef) for coef in coefs]
    copies[3].wait()
    weights = lift_v[...].reshape(leaf_dev * rank, rank)
    tiles.append(fold(dot3(jnp.concatenate(coefs, axis=1), weights, NN)))
    for peer in range(GROUP):
        for index, tile in enumerate(tiles):
            out[peer, index * TILE : (index + 1) * TILE, :] = tile
    place = lax.rem(me, GROUP)
    start = len(tiles) * TILE
    for part in range(per_leaf):
        first = x_out[0, :, part * LANES : (part + 1) * LANES]
        last = x_out[leaf_dev - 1, :, part * LANES : (part + 1) * LANES]
        rows = slice(start + part * vectors, start + (part + 1) * vectors)
        for peer in range(GROUP):
            above = lax.rem(place + 1, GROUP) == peer
            out[peer, rows, :] = jnp.where(above, last, first)


def side_kernel(
    me_ref,
    x_hbm,
    order_hbm,
    ids_hbm,
    links_hbm,
    blocks_hbm,
    bases_hbm,
    lift_hbm,
    far_hbm,
    transfer_hbm,
    couple_hbm,
    top_hbm,
    near_out,
    inverse_out,
    edge_high,
    edge_low,
    leaf_high,
    leaf_low,
    bases_high,
    bases_low,
    up_high,
    up_low,
    path_high,
    path_low,
    x_ref,
    order_v,
    ids_s,
    links_s,
    blocks_v,
    bases_v,
    lift_v,
    far_v,
    transfer_v,
    couple_v,
    top_v,
    sems,
    block_sems,
):
    me = me_ref[0]
    leaf_dev, slots, leaf_size, _ = blocks_v.shape
    _, rank, _ = bases_v.shape
    small = fetch(
        [
            (ids_hbm, ids_s),
            (links_hbm, links_s),
            (x_hbm, x_ref),
            (order_hbm, order_v),
            (transfer_hbm, transfer_v),
            (couple_hbm, couple_v),
            (top_hbm, top_v),
            (lift_hbm, lift_v),
            (far_hbm, far_v),
            (bases_hbm, bases_v),
        ],
        sems,
    )
    blocks = fetch([(blocks_hbm.at[leaf], blocks_v.at[leaf]) for leaf in range(leaf_dev)], block_sems)
    for copy in small:
        copy.wait()

    points_dev = order_v.shape[1]
    tiles = points_dev // LANES
    spot = order_v[...] - me * points_dev
    times = lax.broadcasted_iota(jnp.int32, (1, points_dev), 1)
    shape = (tiles, points_dev)
    match = lax.broadcasted_iota(jnp.int32, shape, 0) == lax.shift_right_logical(spot, 7)
    digits = [
        jnp.where(match, jnp.broadcast_to(digit.astype(F32), shape), 0.0)
        for digit in (lax.shift_right_logical(times, 4), times & 15)
    ]
    shape = (LANES, points_dev)
    match = lax.broadcasted_iota(jnp.int32, shape, 0) == (spot & (LANES - 1))
    both = lax.dot_general(
        jnp.concatenate(digits, axis=0).astype(BF16),
        jnp.where(match, 1.0, 0.0).astype(BF16),
        NT,
        preferred_element_type=F32,
    )
    inverse_out[...] = (both[:tiles] * 16.0 + both[tiles:]).astype(jnp.int32)

    composed = transfer_v[0].reshape(2 * rank, rank)
    row = 0
    for level in range(1, DEPTH):
        rows = composed.shape[0]
        up_high[row : row + rows], up_low[row : row + rows] = halves(composed)
        row += rows
        if level < DEPTH - 1:
            composed = jnp.concatenate(
                [dot3(composed, transfer_v[level, side], NN) for side in range(2)], axis=0
            )

    path = None
    for level in range(DEPTH):
        weights = []
        for column in range(len(OFFSETS)):
            link = links_s[level, column].astype(F32)
            weights.append(link * couple_v[level, column])
        weights = jnp.concatenate(weights, axis=1)
        step = transfer_v[level, lax.shift_right_logical(me, level) & 1]
        if path is not None:
            weights = dot3(path, weights, NN)
            step = dot3(path, step, NN)
        path = step
        column = level * len(OFFSETS) * rank
        span = slice(column, column + weights.shape[1])
        path_high[:, span], path_low[:, span] = halves(weights)
    top = dot3(path, top_v[...], NN)
    last = jnp.concatenate(
        [dot3(top, transfer_v[DEPTH - 1, side], NT) for side in range(2)], axis=1
    )
    column = DEPTH * len(OFFSETS) * rank
    span = slice(column, column + 2 * rank)
    path_high[:, span], path_low[:, span] = halves(last)

    for leaf in range(leaf_dev):
        row = [far_v[leaf, slot] for slot in range(far_v.shape[1])] + [lift_v[leaf]]
        leaf_high[leaf], leaf_low[leaf] = halves(jnp.concatenate(row, axis=1))
        bases_high[leaf], bases_low[leaf] = halves(bases_v[leaf])

    for copy in blocks:
        copy.wait()

    def near(leaf, carry):
        total = jnp.zeros(near_out.shape[1:], F32)
        for slot in range(slots):
            local = ids_s[slot, leaf] - me * leaf_dev
            here = (local >= 0) & (local < leaf_dev)
            x_leaf = jnp.where(here, x_ref[jnp.clip(local, 0, leaf_dev - 1)], 0.0)
            total = total + dot3(x_leaf, blocks_v[leaf, slot], NT)
        near_out[leaf] = total
        return carry

    lax.fori_loop(0, leaf_dev, near, 0)

    for index, leaf, outside in ((0, 0, -1), (1, leaf_dev - 1, leaf_dev)):
        total = jnp.zeros((leaf_size, leaf_size), F32)
        for slot in range(1, slots):
            remote = ids_s[slot, leaf] - me * leaf_dev == outside
            total = total + jnp.where(remote, blocks_v[leaf, slot], 0.0)
        edge_high[index], edge_low[index] = halves(total)


def middle_kernel(
    leaf_dev,
    me_ref,
    group_hbm,
    up_high_hbm,
    up_low_hbm,
    nodes_out,
    half_hbm,
    roots_v,
    up_high,
    up_low,
    sems,
    half_sems,
):
    low = lax.rem(me_ref[0], GROUP) < REACH
    root = leaf_dev * TILE
    rows = root + TILE
    copies = fetch(
        [
            (group_hbm.at[:, pl.ds(root, TILE), :], roots_v),
            (up_high_hbm, up_high),
            (up_low_hbm, up_low),
        ],
        sems,
    )
    first = jnp.where(low, REACH, 0)
    moves = [
        (group_hbm.at[first + part, pl.ds(0, rows)], half_hbm.at[pl.ds(part * rows, rows)])
        for part in range(REACH)
    ]
    edge_rows = half_hbm.shape[0] - REACH * rows
    moves.append(
        (
            group_hbm.at[jnp.where(low, GROUP - 1, 0), pl.ds(rows, edge_rows)],
            half_hbm.at[pl.ds(REACH * rows, edge_rows)],
        )
    )
    moves = fetch(moves, half_sems)
    for copy in copies:
        copy.wait()
    roots = [roots_v[peer] for peer in range(GROUP)]
    start, tiles = 0, []
    for level in range(1, DEPTH):
        width = 1 << level
        count = GROUP // width
        left = jnp.concatenate(
            [row_of(roots[n * width : (n + 1) * width]) for n in range(count)], axis=0
        )
        size = left.shape[1]
        nodes = dot_halves(left, up_high[start : start + size], up_low[start : start + size], NN)
        start += size
        tiles += [fold(nodes[n * 2 * TILE : (n + 1) * 2 * TILE]) for n in range(count)]
    tiles.append(jnp.zeros((TILE, LANES), F32))
    for peer in range(nodes_out.shape[0]):
        for index, tile in enumerate(tiles):
            nodes_out[peer, index] = tile
    for copy in moves:
        copy.wait()


def down_kernel(me_ref, *refs):
    count = (len(refs) - 3) // 2
    out_ref, y_tree, sems = refs[count], refs[-2], refs[-1]
    held = refs[count + 1 : -2]
    copies = fetch(list(zip(refs[:count], held)), sems)
    (
        group_ref,
        half_ref,
        nodes_ref,
        path_high,
        path_low,
        far_ids_s,
        far_count_s,
        edge_high,
        edge_low,
        leaf_high,
        leaf_low,
        bases_high,
        bases_low,
        near_ref,
        inverse_ref,
    ) = held
    me = me_ref[0]
    leaf_dev, vectors, leaf_size = near_ref.shape
    points_dev = out_ref.shape[1]
    groups = nodes_ref.shape[0]
    slots = far_ids_s.shape[1]
    group = lax.shift_right_logical(me, 3)
    place = me & (GROUP - 1)
    low = place < REACH
    per_leaf = leaf_size // LANES
    start = (leaf_dev + 1) * TILE

    def tile_of(subtree, index):
        other = subtree & (GROUP - 1)
        inside = lax.shift_right_arithmetic(subtree, 3) == group
        row = pl.multiple_of(index * TILE, TILE)
        near_row = jnp.clip(other - jnp.where(low, REACH, 0), 0, REACH - 1) * start
        here = group_ref[other, pl.ds(row, TILE), :]
        there = half_ref[pl.ds(pl.multiple_of(near_row + row, TILE), TILE), :]
        return jnp.where(inside, here, there)

    for copy in copies[:5]:
        copy.wait()
    partners = []
    for level in range(DEPTH):
        node = lax.shift_right_logical(me, level)
        size = (groups * GROUP) >> level
        for offset in OFFSETS:
            other = node + offset
            used = (other >= 0) & (other < size)
            other = jnp.clip(other, 0, size - 1)
            if level == 0:
                tile = tile_of(other, leaf_dev)
            else:
                shift = DEPTH - 1 - level
                first = GROUP - (2 << shift)
                tile = nodes_ref[
                    lax.shift_right_logical(other, shift), first + (other & ((1 << shift) - 1))
                ]
            partners.append(jnp.where(used, tile, 0.0))
    top = lax.shift_right_logical(me, DEPTH)
    for side in range(2):
        blended = jnp.zeros((TILE, LANES), F32)
        for other in range(groups // 2):
            distance = jnp.abs(top - other)
            weight = jnp.where(distance >= 2, 1.0 / jnp.maximum(distance, 1).astype(F32), 0.0)
            blended = blended + weight * nodes_ref[2 * other + side, GROUP - 2]
        partners.append(blended)
    down = dot_halves(row_of(partners), path_high[...], path_low[...], NT)

    for copy in copies[5:9]:
        copy.wait()
    edges = []
    for index, offset in ((0, -1), (1, 1)):
        other = me + offset
        inside = lax.shift_right_arithmetic(other, 3) == group
        here = group_ref[other & (GROUP - 1), start:, :]
        chosen = jnp.where(inside, here, half_ref[REACH * start :, :])
        edges.append(
            jnp.concatenate(
                [chosen[part * vectors : (part + 1) * vectors] for part in range(per_leaf)], axis=1
            )
        )
    edge_parts = [
        dot_halves(edges[index], edge_high[index], edge_low[index], NT) for index in range(2)
    ]

    for copy in copies[9:]:
        copy.wait()
    for leaf in range(leaf_dev):
        picked = []
        for slot in range(slots):
            used = slot < far_count_s[leaf]
            spot = far_ids_s[leaf, slot]
            tile = tile_of(lax.shift_right_logical(spot, 3), spot & (leaf_dev - 1))
            picked.append(jnp.where(used, tile, 0.0))
        left = jnp.concatenate([row_of(picked), down], axis=1)
        leaf_out = dot_halves(left, leaf_high[leaf], leaf_low[leaf], NT)
        y_leaf = near_ref[leaf] + dot_halves(leaf_out, bases_high[leaf], bases_low[leaf], NN)
        if leaf == 0:
            y_leaf = y_leaf + edge_parts[0]
        if leaf == leaf_dev - 1:
            y_leaf = y_leaf + edge_parts[1]
        y_tree[:, leaf * leaf_size : (leaf + 1) * leaf_size] = y_leaf

    y = y_tree[...]
    for tile in range(points_dev // LANES):
        spot = inverse_ref[tile : tile + 1, :]
        out_ref[:, tile * LANES : (tile + 1) * LANES] = lane_gather(
            y, lax.shift_right_logical(spot, 7), spot & (LANES - 1)
        )


def local(
    devices,
    points,
    order,
    bases,
    lift,
    near_ids,
    near_blocks,
    far_ids,
    far_count,
    far_blocks,
    transfer,
    couple,
    links,
    top_couple,
):
    me = lax.axis_index("leaf").astype(jnp.int32).reshape(1)
    vectors, points_dev = points.shape
    leaf_dev, leaf_size, rank = bases.shape
    slots = near_ids.shape[1]
    far_slots = far_ids.shape[1]
    bases_t = jnp.swapaxes(bases, 1, 2)
    tiles = points_dev // LANES
    edge_rows = vectors * (leaf_size // LANES)
    rows = (leaf_dev + 1) * TILE
    groups = devices // GROUP
    order_tiles = order.reshape(tiles, LANES)
    shape = jax.ShapeDtypeStruct

    group_out, tree_x = pl.pallas_call(
        up_kernel,
        out_shape=[
            shape((GROUP, rows + edge_rows, LANES), F32),
            shape((leaf_dev, vectors, leaf_size), F32),
        ],
        in_specs=[SMEM] + [HBM] * 4,
        out_specs=[VMEM] * 2,
        scratch_shapes=[
            pltpu.VMEM(points.shape, F32),
            pltpu.VMEM((tiles, LANES), jnp.int32),
            pltpu.VMEM(bases_t.shape, F32),
            pltpu.VMEM(lift.shape, F32),
            pltpu.SemaphoreType.DMA((4,)),
        ],
        compiler_params=PARAMS,
        name="up",
    )(me, points, order_tiles, bases_t, lift)

    aligned = [[g * GROUP + i for i in range(GROUP)] for g in range(groups)]
    group_in = lax.all_to_all(group_out, "leaf", 0, 0, axis_index_groups=aligned, tiled=True)

    ids_t = near_ids.T
    links_own = links.reshape(links.shape[1:])
    composed_rows = (2 + 4 + 8) * rank
    path_columns = (DEPTH * len(OFFSETS) + 2) * rank
    leaf_columns = (far_slots + 1) * rank
    both = lambda *size: [shape(size, BF16)] * 2
    operands = (
        tree_x,
        order.reshape(1, points_dev),
        ids_t,
        links_own,
        near_blocks,
        bases_t,
        lift,
        far_blocks,
        transfer,
        couple,
        top_couple,
    )
    (
        near_part,
        inverse,
        edge_high,
        edge_low,
        leaf_high,
        leaf_low,
        bases_high,
        bases_low,
        up_high,
        up_low,
        path_high,
        path_low,
    ) = pl.pallas_call(
        side_kernel,
        out_shape=[shape(tree_x.shape, F32), shape((tiles, LANES), jnp.int32)]
        + both(2, leaf_size, leaf_size)
        + both(leaf_dev, rank, leaf_columns)
        + both(leaf_dev, rank, leaf_size)
        + both(composed_rows, rank)
        + both(rank, path_columns),
        in_specs=[SMEM] + [HBM] * len(operands),
        out_specs=[VMEM] * 12,
        scratch_shapes=[
            (pltpu.SMEM if x is ids_t or x is links_own else pltpu.VMEM)(x.shape, x.dtype)
            for x in operands
        ]
        + [pltpu.SemaphoreType.DMA((len(operands) - 1,)), pltpu.SemaphoreType.DMA((leaf_dev,))],
        compiler_params=PARAMS,
        cost_estimate=pl.CostEstimate(
            flops=6 * vectors * near_blocks.size,
            bytes_accessed=4 * near_blocks.size,
            transcendentals=0,
        ),
        name="side",
    )(me, *operands)

    nodes_out, half_out = pl.pallas_call(
        functools.partial(middle_kernel, leaf_dev),
        out_shape=[
            shape((groups, GROUP, TILE, LANES), F32),
            shape((REACH * rows + edge_rows, LANES), F32),
        ],
        in_specs=[SMEM] + [HBM] * 3,
        out_specs=[VMEM, HBM],
        scratch_shapes=[
            pltpu.VMEM((GROUP, TILE, LANES), F32),
            pltpu.VMEM(up_high.shape, BF16),
            pltpu.VMEM(up_low.shape, BF16),
            pltpu.SemaphoreType.DMA((3,)),
            pltpu.SemaphoreType.DMA((REACH + 1,)),
        ],
        compiler_params=PARAMS,
        name="middle",
    )(me, group_in, up_high, up_low)

    pairs = []
    for device in range(devices):
        target = device + GROUP if device % GROUP < REACH else device - GROUP
        if 0 <= target < devices:
            pairs.append((device, target))
    half_in = lax.ppermute(half_out, "leaf", pairs)
    across = [[g * GROUP + i for g in range(groups)] for i in range(GROUP)]
    nodes_in = lax.all_to_all(nodes_out, "leaf", 0, 0, axis_index_groups=across, tiled=True)

    operands = (
        group_in,
        half_in,
        nodes_in,
        path_high,
        path_low,
        far_ids,
        far_count,
        edge_high,
        edge_low,
        leaf_high,
        leaf_low,
        bases_high,
        bases_low,
        near_part,
        inverse,
    )
    return pl.pallas_call(
        down_kernel,
        out_shape=shape((vectors, points_dev), F32),
        in_specs=[SMEM] + [HBM] * len(operands),
        out_specs=VMEM,
        scratch_shapes=[
            (pltpu.SMEM if x is far_ids or x is far_count else pltpu.VMEM)(x.shape, x.dtype)
            for x in operands
        ]
        + [pltpu.VMEM((vectors, points_dev), F32), pltpu.SemaphoreType.DMA((len(operands),))],
        compiler_params=PARAMS,
        name="down",
    )(me, *operands)


def solution(mesh):
    in_specs = (
        P(None, "leaf"),
        P("leaf"),
        P("leaf", None, None),
        P("leaf", None, None),
        P("leaf", None),
        P("leaf", None, None, None),
        P("leaf", None),
        P("leaf"),
        P("leaf", None, None, None),
        P(),
        P(),
        P("leaf", None, None),
        P(),
    )
    return jax.shard_map(
        functools.partial(local, mesh.shape["leaf"]),
        mesh=mesh,
        in_specs=in_specs,
        out_specs=P(None, "leaf"),
        check_vma=False,
    )
```

```python
import functools

import jax
import jax.numpy as jnp
from jax import lax
from jax.experimental import pallas as pl
from jax.experimental.pallas import tpu as pltpu
from jax.sharding import PartitionSpec as P

REACH = 4
DEPTH = 4
OFFSETS = (-3, -2, 2, 3)
GROUP = 2 * REACH
LANES = 128
TILE = 8
VMEM_LIMIT = 64 * 1024 * 1024

NN = (((1,), (0,)), ((), ()))
NT = (((1,), (1,)), ((), ()))

VMEM = pl.BlockSpec(memory_space=pltpu.VMEM)
SMEM = pl.BlockSpec(memory_space=pltpu.SMEM)
HBM = pl.BlockSpec(memory_space=pltpu.HBM)
PARAMS = pltpu.CompilerParams(vmem_limit_bytes=VMEM_LIMIT)
F32 = jnp.float32
BF16 = jnp.bfloat16


def halves(x):
    high = x.astype(BF16)
    low = (x - high.astype(F32)).astype(BF16)
    return high, low


def dot_halves(a, b_high, b_low, dims):
    a_high, a_low = halves(a)
    rows = a.shape[0]
    both = lax.dot_general(
        jnp.concatenate([a_high, a_low], axis=0), b_high, dims, preferred_element_type=F32
    )
    cross = lax.dot_general(a_high, b_low, dims, preferred_element_type=F32)
    return both[:rows] + (both[rows:] + cross)


def dot3(a, b, dims):
    return dot_halves(a, *halves(b), dims)


def fold(x):
    return jnp.concatenate([x[:TILE], x[TILE:]], axis=1)


def beside(p, q):
    rank = p.shape[1] // 2
    left = lax.broadcasted_iota(jnp.int32, p.shape, 1) < rank
    return jnp.concatenate(
        [
            jnp.where(left, p, pltpu.roll(q, rank, 1)),
            jnp.where(left, pltpu.roll(p, rank, 1), q),
        ],
        axis=0,
    )


def row_of(tiles):
    return jnp.concatenate([beside(*tiles[k : k + 2]) for k in range(0, len(tiles), 2)], axis=1)


def lane_gather(x, high, low):
    rows, columns = x.shape
    high = jnp.broadcast_to(high, (rows, LANES))
    low = jnp.broadcast_to(low, (rows, LANES))
    result = jnp.zeros((rows, LANES), x.dtype)
    for source in range(columns // LANES):
        tile = x[:, source * LANES : (source + 1) * LANES]
        moved = jnp.take_along_axis(tile, low, axis=1, mode="promise_in_bounds")
        result = jnp.where(high == source, moved, result)
    return result


def fetch(pairs, sems):
    copies = [
        pltpu.make_async_copy(source, target, sems.at[index])
        for index, (source, target) in enumerate(pairs)
    ]
    for copy in copies:
        copy.start()
    return copies


def up_kernel(
    me_ref,
    points_hbm,
    order_hbm,
    bases_hbm,
    lift_hbm,
    out,
    first_out,
    last_out,
    x_out,
    points_v,
    order_v,
    bases_v,
    lift_v,
    sems,
):
    copies = fetch(
        [(order_hbm, order_v), (points_hbm, points_v), (bases_hbm, bases_v), (lift_hbm, lift_v)], sems
    )
    me = me_ref[0]
    leaf_dev, rank, leaf_size = bases_v.shape
    points_dev = points_v.shape[1]
    copies[0].wait()
    copies[1].wait()
    points = points_v[...]
    per_leaf = leaf_size // LANES
    for t in range(points_dev // LANES):
        spot = order_v[t : t + 1, :] - me * points_dev
        column = t % per_leaf * LANES
        x_out[t // per_leaf, :, column : column + LANES] = lane_gather(
            points, lax.shift_right_logical(spot, 7), spot & (LANES - 1)
        )
    first_out[...] = x_out[0]
    last_out[...] = x_out[leaf_dev - 1]
    copies[2].wait()
    coefs = [dot3(x_out[leaf], bases_v[leaf], NT) for leaf in range(leaf_dev)]
    copies[3].wait()
    weights = lift_v[...].reshape(leaf_dev * rank, rank)
    root = dot3(jnp.concatenate(coefs, axis=1), weights, NN)
    for index, matrix in enumerate(coefs + [root]):
        out[index * TILE : (index + 1) * TILE, :] = fold(matrix)


def side_kernel(
    me_ref,
    x_hbm,
    order_hbm,
    ids_hbm,
    links_hbm,
    blocks_hbm,
    bases_hbm,
    lift_hbm,
    far_hbm,
    transfer_hbm,
    couple_hbm,
    top_hbm,
    near_out,
    inverse_out,
    edge_high,
    edge_low,
    leaf_high,
    leaf_low,
    bases_high,
    bases_low,
    up_high,
    up_low,
    path_high,
    path_low,
    x_ref,
    order_v,
    ids_s,
    links_s,
    blocks_v,
    bases_v,
    lift_v,
    far_v,
    transfer_v,
    couple_v,
    top_v,
    sems,
    block_sems,
):
    me = me_ref[0]
    leaf_dev, slots, leaf_size, _ = blocks_v.shape
    _, rank, _ = bases_v.shape
    small = fetch(
        [
            (ids_hbm, ids_s),
            (links_hbm, links_s),
            (x_hbm, x_ref),
            (order_hbm, order_v),
            (transfer_hbm, transfer_v),
            (couple_hbm, couple_v),
            (top_hbm, top_v),
            (lift_hbm, lift_v),
            (far_hbm, far_v),
            (bases_hbm, bases_v),
        ],
        sems,
    )
    blocks = fetch([(blocks_hbm.at[leaf], blocks_v.at[leaf]) for leaf in range(leaf_dev)], block_sems)
    for copy in small:
        copy.wait()

    points_dev = order_v.shape[1]
    tiles = points_dev // LANES
    spot = order_v[...] - me * points_dev
    times = lax.broadcasted_iota(jnp.int32, (1, points_dev), 1)
    shape = (tiles, points_dev)
    match = lax.broadcasted_iota(jnp.int32, shape, 0) == lax.shift_right_logical(spot, 7)
    digits = [
        jnp.where(match, jnp.broadcast_to(digit.astype(F32), shape), 0.0)
        for digit in (lax.shift_right_logical(times, 4), times & 15)
    ]
    shape = (LANES, points_dev)
    match = lax.broadcasted_iota(jnp.int32, shape, 0) == (spot & (LANES - 1))
    both = lax.dot_general(
        jnp.concatenate(digits, axis=0).astype(BF16),
        jnp.where(match, 1.0, 0.0).astype(BF16),
        NT,
        preferred_element_type=F32,
    )
    inverse_out[...] = (both[:tiles] * 16.0 + both[tiles:]).astype(jnp.int32)

    composed = transfer_v[0].reshape(2 * rank, rank)
    row = 0
    for level in range(1, DEPTH):
        rows = composed.shape[0]
        up_high[row : row + rows], up_low[row : row + rows] = halves(composed)
        row += rows
        if level < DEPTH - 1:
            composed = jnp.concatenate(
                [dot3(composed, transfer_v[level, side], NN) for side in range(2)], axis=0
            )

    path = None
    for level in range(DEPTH):
        weights = []
        for column in range(len(OFFSETS)):
            link = links_s[level, column].astype(F32)
            weights.append(link * couple_v[level, column])
        weights = jnp.concatenate(weights, axis=1)
        step = transfer_v[level, lax.shift_right_logical(me, level) & 1]
        if path is not None:
            weights = dot3(path, weights, NN)
            step = dot3(path, step, NN)
        path = step
        column = level * len(OFFSETS) * rank
        span = slice(column, column + weights.shape[1])
        path_high[:, span], path_low[:, span] = halves(weights)
    top = dot3(path, top_v[...], NN)
    last = jnp.concatenate(
        [dot3(top, transfer_v[DEPTH - 1, side], NT) for side in range(2)], axis=1
    )
    column = DEPTH * len(OFFSETS) * rank
    span = slice(column, column + 2 * rank)
    path_high[:, span], path_low[:, span] = halves(last)

    for leaf in range(leaf_dev):
        row = [far_v[leaf, slot] for slot in range(far_v.shape[1])] + [lift_v[leaf]]
        leaf_high[leaf], leaf_low[leaf] = halves(jnp.concatenate(row, axis=1))
        bases_high[leaf], bases_low[leaf] = halves(bases_v[leaf])

    for copy in blocks:
        copy.wait()

    def near(leaf, carry):
        total = jnp.zeros(near_out.shape[1:], F32)
        for slot in range(slots):
            local = ids_s[slot, leaf] - me * leaf_dev
            here = (local >= 0) & (local < leaf_dev)
            x_leaf = jnp.where(here, x_ref[jnp.clip(local, 0, leaf_dev - 1)], 0.0)
            total = total + dot3(x_leaf, blocks_v[leaf, slot], NT)
        near_out[leaf] = total
        return carry

    lax.fori_loop(0, leaf_dev, near, 0)

    for index, leaf, outside in ((0, 0, -1), (1, leaf_dev - 1, leaf_dev)):
        total = jnp.zeros((leaf_size, leaf_size), F32)
        for slot in range(1, slots):
            remote = ids_s[slot, leaf] - me * leaf_dev == outside
            total = total + jnp.where(remote, blocks_v[leaf, slot], 0.0)
        edge_high[index], edge_low[index] = halves(total)


def down_kernel(leaf_dev, me_ref, all_hbm, *refs):
    count = (len(refs) - 8) // 2
    out_ref = refs[count]
    held = refs[count + 1 : 2 * count + 1]
    window, roots, tops, y_tree, sems, window_sems, root_sem = refs[2 * count + 1 :]
    me = me_ref[0]
    devices = all_hbm.shape[0]
    groups = devices // GROUP
    coef_rows = leaf_dev * TILE
    root_copy = fetch([(all_hbm.at[:, pl.ds(coef_rows, TILE), :], roots)], root_sem)
    copies = fetch(list(zip(refs[:count], held)), sems)
    around = fetch(
        [
            (
                all_hbm.at[jnp.clip(me + index - REACH, 0, devices - 1), pl.ds(0, coef_rows), :],
                window.at[pl.ds(index * coef_rows, coef_rows)],
            )
            for index in range(2 * REACH + 1)
        ],
        window_sems,
    )
    (
        up_high,
        up_low,
        path_high,
        path_low,
        far_ids_s,
        far_count_s,
        below_ref,
        above_ref,
        edge_high,
        edge_low,
        leaf_high,
        leaf_low,
        bases_high,
        bases_low,
        near_ref,
        inverse_ref,
    ) = held
    vectors, leaf_size = below_ref.shape
    points_dev = out_ref.shape[1]
    slots = far_ids_s.shape[1]

    for copy in root_copy + copies[:4]:
        copy.wait()
    columns = []
    start = 0
    for level in range(DEPTH):
        node = lax.shift_right_logical(me, level)
        size = devices >> level
        width = 1 << level
        others = [node + offset for offset in OFFSETS]
        used = [(other >= 0) & (other < size) for other in others]
        others = [jnp.clip(other, 0, size - 1) for other in others]
        if level == 0:
            nodes = [roots[other] for other in others]
        else:
            which = others if level < DEPTH - 1 else range(groups)
            left = jnp.concatenate(
                [row_of([roots[other * width + part] for part in range(width)]) for other in which],
                axis=0,
            )
            rows = left.shape[1]
            result = dot_halves(left, up_high[start : start + rows], up_low[start : start + rows], NN)
            start += rows
            nodes = [fold(result[n * vectors : (n + 1) * vectors]) for n in range(len(which))]
            if level == DEPTH - 1:
                for n in range(groups):
                    tops[n] = nodes[n]
                nodes = [tops[other] for other in others]
        columns += [jnp.where(use, tile, 0.0) for use, tile in zip(used, nodes)]
    top = lax.shift_right_logical(me, DEPTH)
    for side in range(2):
        blended = jnp.zeros((TILE, LANES), F32)
        for other in range(groups // 2):
            distance = jnp.abs(top - other)
            weight = jnp.where(distance >= 2, 1.0 / jnp.maximum(distance, 1).astype(F32), 0.0)
            blended = blended + weight * tops[2 * other + side]
        columns.append(blended)
    down = dot_halves(row_of(columns), path_high[...], path_low[...], NT)

    for copy in copies[4:]:
        copy.wait()
    edge_parts = [
        dot_halves(edge[...], edge_high[index], edge_low[index], NT)
        for index, edge in enumerate((below_ref, above_ref))
    ]
    for copy in around:
        copy.wait()
    spots = (2 * REACH + 1) * leaf_dev
    for leaf in range(leaf_dev):
        picked = []
        for slot in range(slots):
            used = slot < far_count_s[leaf]
            spot = jnp.clip(far_ids_s[leaf, slot] - (me - REACH) * leaf_dev, 0, spots - 1)
            tile = window[pl.ds(pl.multiple_of(spot * TILE, TILE), TILE), :]
            picked.append(jnp.where(used, tile, 0.0))
        left = jnp.concatenate([row_of(picked), down], axis=1)
        leaf_out = dot_halves(left, leaf_high[leaf], leaf_low[leaf], NT)
        y_leaf = near_ref[leaf] + dot_halves(leaf_out, bases_high[leaf], bases_low[leaf], NN)
        if leaf == 0:
            y_leaf = y_leaf + edge_parts[0]
        if leaf == leaf_dev - 1:
            y_leaf = y_leaf + edge_parts[1]
        y_tree[:, leaf * leaf_size : (leaf + 1) * leaf_size] = y_leaf

    y = y_tree[...]
    for tile in range(points_dev // LANES):
        spot = inverse_ref[tile : tile + 1, :]
        out_ref[:, tile * LANES : (tile + 1) * LANES] = lane_gather(
            y, lax.shift_right_logical(spot, 7), spot & (LANES - 1)
        )


def local(
    devices,
    points,
    order,
    bases,
    lift,
    near_ids,
    near_blocks,
    far_ids,
    far_count,
    far_blocks,
    transfer,
    couple,
    links,
    top_couple,
):
    me = lax.axis_index("leaf").astype(jnp.int32).reshape(1)
    vectors, points_dev = points.shape
    leaf_dev, leaf_size, rank = bases.shape
    slots = near_ids.shape[1]
    far_slots = far_ids.shape[1]
    bases_t = jnp.swapaxes(bases, 1, 2)
    tiles = points_dev // LANES
    rows = (leaf_dev + 1) * TILE
    shape = jax.ShapeDtypeStruct

    mine, first_leaf, last_leaf, tree_x = pl.pallas_call(
        up_kernel,
        out_shape=[
            shape((rows, LANES), F32),
            shape((vectors, leaf_size), F32),
            shape((vectors, leaf_size), F32),
            shape((leaf_dev, vectors, leaf_size), F32),
        ],
        in_specs=[SMEM] + [HBM] * 4,
        out_specs=[VMEM] * 4,
        scratch_shapes=[
            pltpu.VMEM(points.shape, F32),
            pltpu.VMEM((tiles, LANES), jnp.int32),
            pltpu.VMEM(bases_t.shape, F32),
            pltpu.VMEM(lift.shape, F32),
            pltpu.SemaphoreType.DMA((4,)),
        ],
        compiler_params=PARAMS,
        name="up",
    )(me, points, order.reshape(tiles, LANES), bases_t, lift)

    gathered = lax.all_gather(mine, "leaf", axis=0, tiled=True).reshape(devices, rows, LANES)
    forward = [(i, i + 1) for i in range(devices - 1)]
    below = lax.ppermute(last_leaf, "leaf", forward)
    above = lax.ppermute(first_leaf, "leaf", [(target, source) for source, target in forward])

    ids_t = near_ids.T
    links_own = links.reshape(links.shape[1:])
    composed_rows = (2 + 4 + 8) * rank
    path_columns = (DEPTH * len(OFFSETS) + 2) * rank
    leaf_columns = (far_slots + 1) * rank
    both = lambda *size: [shape(size, BF16)] * 2
    operands = (
        tree_x,
        order.reshape(1, points_dev),
        ids_t,
        links_own,
        near_blocks,
        bases_t,
        lift,
        far_blocks,
        transfer,
        couple,
        top_couple,
    )
    (
        near_part,
        inverse,
        edge_high,
        edge_low,
        leaf_high,
        leaf_low,
        bases_high,
        bases_low,
        up_high,
        up_low,
        path_high,
        path_low,
    ) = pl.pallas_call(
        side_kernel,
        out_shape=[shape(tree_x.shape, F32), shape((tiles, LANES), jnp.int32)]
        + both(2, leaf_size, leaf_size)
        + both(leaf_dev, rank, leaf_columns)
        + both(leaf_dev, rank, leaf_size)
        + both(composed_rows, rank)
        + both(rank, path_columns),
        in_specs=[SMEM] + [HBM] * len(operands),
        out_specs=[VMEM] * 12,
        scratch_shapes=[
            (pltpu.SMEM if x is ids_t or x is links_own else pltpu.VMEM)(x.shape, x.dtype)
            for x in operands
        ]
        + [pltpu.SemaphoreType.DMA((len(operands) - 1,)), pltpu.SemaphoreType.DMA((leaf_dev,))],
        compiler_params=PARAMS,
        cost_estimate=pl.CostEstimate(
            flops=6 * vectors * near_blocks.size,
            bytes_accessed=4 * near_blocks.size,
            transcendentals=0,
        ),
        name="side",
    )(me, *operands)

    operands = (
        up_high,
        up_low,
        path_high,
        path_low,
        far_ids,
        far_count,
        below,
        above,
        edge_high,
        edge_low,
        leaf_high,
        leaf_low,
        bases_high,
        bases_low,
        near_part,
        inverse,
    )
    return pl.pallas_call(
        functools.partial(down_kernel, leaf_dev),
        out_shape=shape((vectors, points_dev), F32),
        in_specs=[SMEM] + [HBM] * (len(operands) + 1),
        out_specs=VMEM,
        scratch_shapes=[
            (pltpu.SMEM if x is far_ids or x is far_count else pltpu.VMEM)(x.shape, x.dtype)
            for x in operands
        ]
        + [
            pltpu.VMEM(((2 * REACH + 1) * leaf_dev * TILE, LANES), F32),
            pltpu.VMEM((devices, TILE, LANES), F32),
            pltpu.VMEM((devices // GROUP, TILE, LANES), F32),
            pltpu.VMEM((vectors, points_dev), F32),
            pltpu.SemaphoreType.DMA((len(operands),)),
            pltpu.SemaphoreType.DMA((2 * REACH + 1,)),
            pltpu.SemaphoreType.DMA((1,)),
        ],
        compiler_params=PARAMS,
        name="down",
    )(me, gathered, *operands)


def solution(mesh):
    in_specs = (
        P(None, "leaf"),
        P("leaf"),
        P("leaf", None, None),
        P("leaf", None, None),
        P("leaf", None),
        P("leaf", None, None, None),
        P("leaf", None),
        P("leaf"),
        P("leaf", None, None, None),
        P(),
        P(),
        P("leaf", None, None),
        P(),
    )
    return jax.shard_map(
        functools.partial(local, mesh.shape["leaf"]),
        mesh=mesh,
        in_specs=in_specs,
        out_specs=P(None, "leaf"),
        check_vma=False,
    )
```

```python
import functools

import jax
import jax.numpy as jnp
from jax import lax
from jax.experimental import pallas as pl
from jax.experimental.pallas import tpu as pltpu
from jax.sharding import PartitionSpec as P

REACH = 4
DEPTH = 4
OFFSETS = (-3, -2, 2, 3)
GROUP = 2 * REACH
LANES = 128
TILE = 8
VMEM_LIMIT = 64 * 1024 * 1024

NN = (((1,), (0,)), ((), ()))
NT = (((1,), (1,)), ((), ()))

VMEM = pl.BlockSpec(memory_space=pltpu.VMEM)
SMEM = pl.BlockSpec(memory_space=pltpu.SMEM)
HBM = pl.BlockSpec(memory_space=pltpu.HBM)
PARAMS = pltpu.CompilerParams(vmem_limit_bytes=VMEM_LIMIT)
F32 = jnp.float32
BF16 = jnp.bfloat16


def halves(x):
    high = x.astype(BF16)
    low = (x - high.astype(F32)).astype(BF16)
    return high, low


def dot_halves(a, b_high, b_low, dims):
    a_high, a_low = halves(a)
    rows = a.shape[0]
    both = lax.dot_general(
        jnp.concatenate([a_high, a_low], axis=0), b_high, dims, preferred_element_type=F32
    )
    cross = lax.dot_general(a_high, b_low, dims, preferred_element_type=F32)
    return both[:rows] + (both[rows:] + cross)


def dot3(a, b, dims):
    return dot_halves(a, *halves(b), dims)


def fold(x):
    return jnp.concatenate([x[:TILE], x[TILE:]], axis=1)


def beside(p, q):
    rank = p.shape[1] // 2
    left = lax.broadcasted_iota(jnp.int32, p.shape, 1) < rank
    return jnp.concatenate(
        [
            jnp.where(left, p, pltpu.roll(q, rank, 1)),
            jnp.where(left, pltpu.roll(p, rank, 1), q),
        ],
        axis=0,
    )


def row_of(tiles):
    return jnp.concatenate([beside(*tiles[k : k + 2]) for k in range(0, len(tiles), 2)], axis=1)


def lane_gather(x, high, low):
    rows, columns = x.shape
    high = jnp.broadcast_to(high, (rows, LANES))
    low = jnp.broadcast_to(low, (rows, LANES))
    result = jnp.zeros((rows, LANES), x.dtype)
    for source in range(columns // LANES):
        tile = x[:, source * LANES : (source + 1) * LANES]
        moved = jnp.take_along_axis(tile, low, axis=1, mode="promise_in_bounds")
        result = jnp.where(high == source, moved, result)
    return result


def fetch(pairs, sems):
    copies = [
        pltpu.make_async_copy(source, target, sems.at[index])
        for index, (source, target) in enumerate(pairs)
    ]
    for copy in copies:
        copy.start()
    return copies


def up_kernel(
    me_ref, points_hbm, order_hbm, bases_hbm, lift_hbm, out, x_out, points_v, order_v, bases_v, lift_v, sems
):
    copies = fetch(
        [(order_hbm, order_v), (points_hbm, points_v), (bases_hbm, bases_v), (lift_hbm, lift_v)], sems
    )
    me = me_ref[0]
    leaf_dev, rank, leaf_size = bases_v.shape
    vectors, points_dev = points_v.shape
    copies[0].wait()
    copies[1].wait()
    points = points_v[...]
    per_leaf = leaf_size // LANES
    for t in range(points_dev // LANES):
        spot = order_v[t : t + 1, :] - me * points_dev
        column = t % per_leaf * LANES
        x_out[t // per_leaf, :, column : column + LANES] = lane_gather(
            points, lax.shift_right_logical(spot, 7), spot & (LANES - 1)
        )
    copies[2].wait()
    coefs = [dot3(x_out[leaf], bases_v[leaf], NT) for leaf in range(leaf_dev)]
    tiles = [fold(coef) for coef in coefs]
    copies[3].wait()
    weights = lift_v[...].reshape(leaf_dev * rank, rank)
    tiles.append(fold(dot3(jnp.concatenate(coefs, axis=1), weights, NN)))
    for peer in range(GROUP):
        for index, tile in enumerate(tiles):
            out[peer, index * TILE : (index + 1) * TILE, :] = tile
    place = lax.rem(me, GROUP)
    start = len(tiles) * TILE
    for part in range(per_leaf):
        first = x_out[0, :, part * LANES : (part + 1) * LANES]
        last = x_out[leaf_dev - 1, :, part * LANES : (part + 1) * LANES]
        rows = slice(start + part * vectors, start + (part + 1) * vectors)
        for peer in range(GROUP):
            above = lax.rem(place + 1, GROUP) == peer
            out[peer, rows, :] = jnp.where(above, last, first)


def side_kernel(me_ref, *refs):
    inputs, outputs = refs[:11], refs[11:23]
    held, results = refs[23:34], refs[34:46]
    sems, block_sems, out_sems = refs[46:]
    ids_s, links_s, x_ref, order_v, transfer_v, couple_v, top_v, lift_v, far_v, bases_v, blocks_v = held
    (
        inverse_out,
        up_high,
        up_low,
        path_high,
        path_low,
        leaf_high,
        leaf_low,
        bases_high,
        bases_low,
        near_out,
        edge_high,
        edge_low,
    ) = results
    copies = fetch(list(zip(inputs[:-1], held[:-1])), sems)
    leaf_dev, slots, leaf_size, _ = blocks_v.shape
    blocks = fetch([(inputs[-1].at[leaf], blocks_v.at[leaf]) for leaf in range(leaf_dev)], block_sems)
    writes = [
        pltpu.make_async_copy(source, target, out_sems.at[index])
        for index, (source, target) in enumerate(zip(results, outputs))
    ]
    me = me_ref[0]
    _, rank, _ = bases_v.shape

    for copy in copies[:4]:
        copy.wait()
    points_dev = order_v.shape[1]
    tiles = points_dev // LANES
    spot = order_v[...] - me * points_dev
    times = lax.broadcasted_iota(jnp.int32, (1, points_dev), 1)
    shape = (tiles, points_dev)
    match = lax.broadcasted_iota(jnp.int32, shape, 0) == lax.shift_right_logical(spot, 7)
    digits = [
        jnp.where(match, jnp.broadcast_to(digit.astype(F32), shape), 0.0)
        for digit in (lax.shift_right_logical(times, 4), times & 15)
    ]
    shape = (LANES, points_dev)
    match = lax.broadcasted_iota(jnp.int32, shape, 0) == (spot & (LANES - 1))
    both = lax.dot_general(
        jnp.concatenate(digits, axis=0).astype(BF16),
        jnp.where(match, 1.0, 0.0).astype(BF16),
        NT,
        preferred_element_type=F32,
    )
    inverse_out[...] = (both[:tiles] * 16.0 + both[tiles:]).astype(jnp.int32)
    writes[0].start()

    for copy in copies[4:7]:
        copy.wait()
    composed = transfer_v[0].reshape(2 * rank, rank)
    row = 0
    for level in range(1, DEPTH):
        rows = composed.shape[0]
        up_high[row : row + rows], up_low[row : row + rows] = halves(composed)
        row += rows
        if level < DEPTH - 1:
            composed = jnp.concatenate(
                [dot3(composed, transfer_v[level, side], NN) for side in range(2)], axis=0
            )
    writes[1].start()
    writes[2].start()

    path = None
    for level in range(DEPTH):
        weights = []
        for column in range(len(OFFSETS)):
            link = links_s[level, column].astype(F32)
            weights.append(link * couple_v[level, column])
        weights = jnp.concatenate(weights, axis=1)
        step = transfer_v[level, lax.shift_right_logical(me, level) & 1]
        if path is not None:
            weights = dot3(path, weights, NN)
            step = dot3(path, step, NN)
        path = step
        column = level * len(OFFSETS) * rank
        span = slice(column, column + weights.shape[1])
        path_high[:, span], path_low[:, span] = halves(weights)
    top = dot3(path, top_v[...], NN)
    last = jnp.concatenate(
        [dot3(top, transfer_v[DEPTH - 1, side], NT) for side in range(2)], axis=1
    )
    column = DEPTH * len(OFFSETS) * rank
    span = slice(column, column + 2 * rank)
    path_high[:, span], path_low[:, span] = halves(last)
    writes[3].start()
    writes[4].start()

    for copy in copies[7:]:
        copy.wait()
    for leaf in range(leaf_dev):
        row = [far_v[leaf, slot] for slot in range(far_v.shape[1])] + [lift_v[leaf]]
        leaf_high[leaf], leaf_low[leaf] = halves(jnp.concatenate(row, axis=1))
        bases_high[leaf], bases_low[leaf] = halves(bases_v[leaf])
    for write in writes[5:9]:
        write.start()

    for leaf in range(leaf_dev):
        blocks[leaf].wait()
        total = jnp.zeros(near_out.shape[1:], F32)
        for slot in range(slots):
            local = ids_s[slot, leaf] - me * leaf_dev
            here = (local >= 0) & (local < leaf_dev)
            x_leaf = jnp.where(here, x_ref[jnp.clip(local, 0, leaf_dev - 1)], 0.0)
            total = total + dot3(x_leaf, blocks_v[leaf, slot], NT)
        near_out[leaf] = total

    for index, leaf, outside in ((0, 0, -1), (1, leaf_dev - 1, leaf_dev)):
        total = jnp.zeros((leaf_size, leaf_size), F32)
        for slot in range(1, slots):
            remote = ids_s[slot, leaf] - me * leaf_dev == outside
            total = total + jnp.where(remote, blocks_v[leaf, slot], 0.0)
        edge_high[index], edge_low[index] = halves(total)
    for write in writes[9:]:
        write.start()
    for write in writes:
        write.wait()


def half_kernel(rows, me_ref, group_hbm, side_hbm, out, sems):
    del side_hbm
    low = lax.rem(me_ref[0], GROUP) < REACH
    edge_rows = out.shape[0] - REACH * rows
    first = jnp.where(low, REACH, 0)
    moves = [
        (group_hbm.at[first + part, pl.ds(0, rows)], out.at[pl.ds(part * rows, rows)])
        for part in range(REACH)
    ]
    moves.append(
        (
            group_hbm.at[jnp.where(low, GROUP - 1, 0), pl.ds(rows, edge_rows)],
            out.at[pl.ds(REACH * rows, edge_rows)],
        )
    )
    for copy in fetch(moves, sems):
        copy.wait()


def node_kernel(
    leaf_dev, group_hbm, half_hbm, up_high_hbm, up_low_hbm, out, roots_v, up_high, up_low, sems
):
    del half_hbm
    copies = fetch(
        [
            (group_hbm.at[:, pl.ds(leaf_dev * TILE, TILE), :], roots_v),
            (up_high_hbm, up_high),
            (up_low_hbm, up_low),
        ],
        sems,
    )
    for copy in copies:
        copy.wait()
    roots = [roots_v[peer] for peer in range(GROUP)]
    start, tiles = 0, []
    for level in range(1, DEPTH):
        width = 1 << level
        count = GROUP // width
        left = jnp.concatenate(
            [row_of(roots[n * width : (n + 1) * width]) for n in range(count)], axis=0
        )
        size = left.shape[1]
        nodes = dot_halves(left, up_high[start : start + size], up_low[start : start + size], NN)
        start += size
        tiles += [fold(nodes[n * 2 * TILE : (n + 1) * 2 * TILE]) for n in range(count)]
    tiles.append(jnp.zeros((TILE, LANES), F32))
    for peer in range(out.shape[0]):
        for index, tile in enumerate(tiles):
            out[peer, index] = tile


def down_kernel(me_ref, *refs):
    count = (len(refs) - 3) // 2
    out_ref, y_tree, sems = refs[count], refs[-2], refs[-1]
    held = refs[count + 1 : -2]
    copies = fetch(list(zip(refs[:count], held)), sems)
    (
        group_ref,
        half_ref,
        nodes_ref,
        path_high,
        path_low,
        far_ids_s,
        far_count_s,
        edge_high,
        edge_low,
        leaf_high,
        leaf_low,
        bases_high,
        bases_low,
        near_ref,
        inverse_ref,
    ) = held
    me = me_ref[0]
    leaf_dev, vectors, leaf_size = near_ref.shape
    points_dev = out_ref.shape[1]
    groups = nodes_ref.shape[0]
    slots = far_ids_s.shape[1]
    group = lax.shift_right_logical(me, 3)
    place = me & (GROUP - 1)
    low = place < REACH
    per_leaf = leaf_size // LANES
    start = (leaf_dev + 1) * TILE

    def tile_of(subtree, index):
        other = subtree & (GROUP - 1)
        inside = lax.shift_right_arithmetic(subtree, 3) == group
        row = pl.multiple_of(index * TILE, TILE)
        near_row = jnp.clip(other - jnp.where(low, REACH, 0), 0, REACH - 1) * start
        here = group_ref[other, pl.ds(row, TILE), :]
        there = half_ref[pl.ds(pl.multiple_of(near_row + row, TILE), TILE), :]
        return jnp.where(inside, here, there)

    for copy in copies[:5]:
        copy.wait()
    partners = []
    for level in range(DEPTH):
        node = lax.shift_right_logical(me, level)
        size = (groups * GROUP) >> level
        for offset in OFFSETS:
            other = node + offset
            used = (other >= 0) & (other < size)
            other = jnp.clip(other, 0, size - 1)
            if level == 0:
                tile = tile_of(other, leaf_dev)
            else:
                shift = DEPTH - 1 - level
                first = GROUP - (2 << shift)
                tile = nodes_ref[
                    lax.shift_right_logical(other, shift), first + (other & ((1 << shift) - 1))
                ]
            partners.append(jnp.where(used, tile, 0.0))
    top = lax.shift_right_logical(me, DEPTH)
    for side in range(2):
        blended = jnp.zeros((TILE, LANES), F32)
        for other in range(groups // 2):
            distance = jnp.abs(top - other)
            weight = jnp.where(distance >= 2, 1.0 / jnp.maximum(distance, 1).astype(F32), 0.0)
            blended = blended + weight * nodes_ref[2 * other + side, GROUP - 2]
        partners.append(blended)
    down = dot_halves(row_of(partners), path_high[...], path_low[...], NT)

    for copy in copies[5:9]:
        copy.wait()
    edges = []
    for index, offset in ((0, -1), (1, 1)):
        other = me + offset
        inside = lax.shift_right_arithmetic(other, 3) == group
        here = group_ref[other & (GROUP - 1), start:, :]
        chosen = jnp.where(inside, here, half_ref[REACH * start :, :])
        edges.append(
            jnp.concatenate(
                [chosen[part * vectors : (part + 1) * vectors] for part in range(per_leaf)], axis=1
            )
        )
    edge_parts = [
        dot_halves(edges[index], edge_high[index], edge_low[index], NT) for index in range(2)
    ]

    for copy in copies[9:]:
        copy.wait()
    for leaf in range(leaf_dev):
        picked = []
        for slot in range(slots):
            used = slot < far_count_s[leaf]
            spot = far_ids_s[leaf, slot]
            tile = tile_of(lax.shift_right_logical(spot, 3), spot & (leaf_dev - 1))
            picked.append(jnp.where(used, tile, 0.0))
        left = jnp.concatenate([row_of(picked), down], axis=1)
        leaf_out = dot_halves(left, leaf_high[leaf], leaf_low[leaf], NT)
        y_leaf = near_ref[leaf] + dot_halves(leaf_out, bases_high[leaf], bases_low[leaf], NN)
        if leaf == 0:
            y_leaf = y_leaf + edge_parts[0]
        if leaf == leaf_dev - 1:
            y_leaf = y_leaf + edge_parts[1]
        y_tree[:, leaf * leaf_size : (leaf + 1) * leaf_size] = y_leaf

    y = y_tree[...]
    for tile in range(points_dev // LANES):
        spot = inverse_ref[tile : tile + 1, :]
        out_ref[:, tile * LANES : (tile + 1) * LANES] = lane_gather(
            y, lax.shift_right_logical(spot, 7), spot & (LANES - 1)
        )


def local(
    devices,
    points,
    order,
    bases,
    lift,
    near_ids,
    near_blocks,
    far_ids,
    far_count,
    far_blocks,
    transfer,
    couple,
    links,
    top_couple,
):
    me = lax.axis_index("leaf").astype(jnp.int32).reshape(1)
    vectors, points_dev = points.shape
    leaf_dev, leaf_size, rank = bases.shape
    slots = near_ids.shape[1]
    far_slots = far_ids.shape[1]
    bases_t = jnp.swapaxes(bases, 1, 2)
    tiles = points_dev // LANES
    edge_rows = vectors * (leaf_size // LANES)
    rows = (leaf_dev + 1) * TILE
    groups = devices // GROUP
    order_tiles = order.reshape(tiles, LANES)
    shape = jax.ShapeDtypeStruct

    group_out, tree_x = pl.pallas_call(
        up_kernel,
        out_shape=[
            shape((GROUP, rows + edge_rows, LANES), F32),
            shape((leaf_dev, vectors, leaf_size), F32),
        ],
        in_specs=[SMEM] + [HBM] * 4,
        out_specs=[VMEM] * 2,
        scratch_shapes=[
            pltpu.VMEM(points.shape, F32),
            pltpu.VMEM((tiles, LANES), jnp.int32),
            pltpu.VMEM(bases_t.shape, F32),
            pltpu.VMEM(lift.shape, F32),
            pltpu.SemaphoreType.DMA((4,)),
        ],
        compiler_params=PARAMS,
        name="up",
    )(me, points, order_tiles, bases_t, lift)

    aligned = [[g * GROUP + i for i in range(GROUP)] for g in range(groups)]
    group_in = lax.all_to_all(group_out, "leaf", 0, 0, axis_index_groups=aligned, tiled=True)

    ids_t = near_ids.T
    links_own = links.reshape(links.shape[1:])
    composed_rows = (2 + 4 + 8) * rank
    path_columns = (DEPTH * len(OFFSETS) + 2) * rank
    leaf_columns = (far_slots + 1) * rank
    both = lambda *size: [shape(size, BF16)] * 2
    operands = (
        ids_t,
        links_own,
        tree_x,
        order.reshape(1, points_dev),
        transfer,
        couple,
        top_couple,
        lift,
        far_blocks,
        bases_t,
        near_blocks,
    )
    results = (
        [shape((tiles, LANES), jnp.int32)]
        + both(composed_rows, rank)
        + both(rank, path_columns)
        + both(leaf_dev, rank, leaf_columns)
        + both(leaf_dev, rank, leaf_size)
        + [shape(tree_x.shape, F32)]
        + both(2, leaf_size, leaf_size)
    )
    (
        inverse,
        up_high,
        up_low,
        path_high,
        path_low,
        leaf_high,
        leaf_low,
        bases_high,
        bases_low,
        near_part,
        edge_high,
        edge_low,
    ) = pl.pallas_call(
        side_kernel,
        out_shape=results,
        in_specs=[SMEM] + [HBM] * len(operands),
        out_specs=[HBM] * len(results),
        scratch_shapes=[
            (pltpu.SMEM if x is ids_t or x is links_own else pltpu.VMEM)(x.shape, x.dtype)
            for x in operands
        ]
        + [pltpu.VMEM(x.shape, x.dtype) for x in results]
        + [
            pltpu.SemaphoreType.DMA((len(operands) - 1,)),
            pltpu.SemaphoreType.DMA((leaf_dev,)),
            pltpu.SemaphoreType.DMA((len(results),)),
        ],
        compiler_params=PARAMS,
        cost_estimate=pl.CostEstimate(
            flops=6 * vectors * near_blocks.size,
            bytes_accessed=4 * near_blocks.size,
            transcendentals=0,
        ),
        name="side",
    )(me, *operands)

    half_out = pl.pallas_call(
        functools.partial(half_kernel, rows),
        out_shape=shape((REACH * rows + edge_rows, LANES), F32),
        in_specs=[SMEM, HBM, HBM],
        out_specs=VMEM,
        scratch_shapes=[pltpu.SemaphoreType.DMA((REACH + 1,))],
        compiler_params=PARAMS,
        name="half",
    )(me, group_in, inverse)
    nodes_out = pl.pallas_call(
        functools.partial(node_kernel, leaf_dev),
        out_shape=shape((groups, GROUP, TILE, LANES), F32),
        in_specs=[HBM] * 4,
        out_specs=VMEM,
        scratch_shapes=[
            pltpu.VMEM((GROUP, TILE, LANES), F32),
            pltpu.VMEM(up_high.shape, BF16),
            pltpu.VMEM(up_low.shape, BF16),
            pltpu.SemaphoreType.DMA((3,)),
        ],
        compiler_params=PARAMS,
        name="nodes",
    )(group_in, half_out, up_high, up_low)

    pairs = []
    for device in range(devices):
        target = device + GROUP if device % GROUP < REACH else device - GROUP
        if 0 <= target < devices:
            pairs.append((device, target))
    half_in = lax.ppermute(half_out, "leaf", pairs)
    across = [[g * GROUP + i for g in range(groups)] for i in range(GROUP)]
    nodes_in = lax.all_to_all(nodes_out, "leaf", 0, 0, axis_index_groups=across, tiled=True)

    operands = (
        group_in,
        half_in,
        nodes_in,
        path_high,
        path_low,
        far_ids,
        far_count,
        edge_high,
        edge_low,
        leaf_high,
        leaf_low,
        bases_high,
        bases_low,
        near_part,
        inverse,
    )
    return pl.pallas_call(
        down_kernel,
        out_shape=shape((vectors, points_dev), F32),
        in_specs=[SMEM] + [HBM] * len(operands),
        out_specs=VMEM,
        scratch_shapes=[
            (pltpu.SMEM if x is far_ids or x is far_count else pltpu.VMEM)(x.shape, x.dtype)
            for x in operands
        ]
        + [pltpu.VMEM((vectors, points_dev), F32), pltpu.SemaphoreType.DMA((len(operands),))],
        compiler_params=PARAMS,
        name="down",
    )(me, *operands)


def solution(mesh):
    in_specs = (
        P(None, "leaf"),
        P("leaf"),
        P("leaf", None, None),
        P("leaf", None, None),
        P("leaf", None),
        P("leaf", None, None, None),
        P("leaf", None),
        P("leaf"),
        P("leaf", None, None, None),
        P(),
        P(),
        P("leaf", None, None),
        P(),
    )
    return jax.shard_map(
        functools.partial(local, mesh.shape["leaf"]),
        mesh=mesh,
        in_specs=in_specs,
        out_specs=P(None, "leaf"),
        check_vma=False,
    )
```

```python
import functools

import jax
import jax.numpy as jnp
from jax import lax
from jax.experimental import pallas as pl
from jax.experimental.pallas import tpu as pltpu
from jax.sharding import PartitionSpec as P

REACH = 4
DEPTH = 4
OFFSETS = (-3, -2, 2, 3)
GROUP = 2 * REACH
LANES = 128
TILE = 8
NODES = GROUP - 1
VMEM_LIMIT = 64 * 1024 * 1024

NN = (((1,), (0,)), ((), ()))
NT = (((1,), (1,)), ((), ()))

VMEM = pl.BlockSpec(memory_space=pltpu.VMEM)
SMEM = pl.BlockSpec(memory_space=pltpu.SMEM)
HBM = pl.BlockSpec(memory_space=pltpu.HBM)
PARAMS = pltpu.CompilerParams(vmem_limit_bytes=VMEM_LIMIT)
F32 = jnp.float32
BF16 = jnp.bfloat16


def halves(x):
    high = x.astype(BF16)
    low = (x - high.astype(F32)).astype(BF16)
    return high, low


def dot_halves(a, b_high, b_low, dims):
    a_high, a_low = halves(a)
    rows = a.shape[0]
    both = lax.dot_general(
        jnp.concatenate([a_high, a_low], axis=0), b_high, dims, preferred_element_type=F32
    )
    cross = lax.dot_general(a_high, b_low, dims, preferred_element_type=F32)
    return both[:rows] + (both[rows:] + cross)


def dot3(a, b, dims):
    return dot_halves(a, *halves(b), dims)


def fold(x):
    return jnp.concatenate([x[:TILE], x[TILE:]], axis=1)


def beside(p, q):
    rank = p.shape[1] // 2
    left = lax.broadcasted_iota(jnp.int32, p.shape, 1) < rank
    return jnp.concatenate(
        [
            jnp.where(left, p, pltpu.roll(q, rank, 1)),
            jnp.where(left, pltpu.roll(p, rank, 1), q),
        ],
        axis=0,
    )


def row_of(tiles):
    return jnp.concatenate([beside(*tiles[k : k + 2]) for k in range(0, len(tiles), 2)], axis=1)


def lane_gather(x, high, low):
    rows, columns = x.shape
    high = jnp.broadcast_to(high, (rows, LANES))
    low = jnp.broadcast_to(low, (rows, LANES))
    result = jnp.zeros((rows, LANES), x.dtype)
    for source in range(columns // LANES):
        tile = x[:, source * LANES : (source + 1) * LANES]
        moved = jnp.take_along_axis(tile, low, axis=1, mode="promise_in_bounds")
        result = jnp.where(high == source, moved, result)
    return result


def fetch(pairs, sems):
    copies = [
        pltpu.make_async_copy(source, target, sems.at[index])
        for index, (source, target) in enumerate(pairs)
    ]
    for copy in copies:
        copy.start()
    return copies


def up_kernel(
    me_ref, points_hbm, order_hbm, bases_hbm, lift_hbm, out, x_out, points_v, order_v, bases_v, lift_v, sems
):
    copies = fetch(
        [(order_hbm, order_v), (points_hbm, points_v), (bases_hbm, bases_v), (lift_hbm, lift_v)], sems
    )
    me = me_ref[0]
    leaf_dev, rank, leaf_size = bases_v.shape
    vectors, points_dev = points_v.shape
    copies[0].wait()
    copies[1].wait()
    points = points_v[...]
    per_leaf = leaf_size // LANES
    for t in range(points_dev // LANES):
        spot = order_v[t : t + 1, :] - me * points_dev
        column = t % per_leaf * LANES
        x_out[t // per_leaf, :, column : column + LANES] = lane_gather(
            points, lax.shift_right_logical(spot, 7), spot & (LANES - 1)
        )
    copies[2].wait()
    coefs = [dot3(x_out[leaf], bases_v[leaf], NT) for leaf in range(leaf_dev)]
    tiles = [fold(coef) for coef in coefs]
    copies[3].wait()
    weights = lift_v[...].reshape(leaf_dev * rank, rank)
    tiles.append(fold(dot3(jnp.concatenate(coefs, axis=1), weights, NN)))
    for peer in range(GROUP):
        for index, tile in enumerate(tiles):
            out[peer, index * TILE : (index + 1) * TILE, :] = tile
    place = lax.rem(me, GROUP)
    start = len(tiles) * TILE
    for part in range(per_leaf):
        first = x_out[0, :, part * LANES : (part + 1) * LANES]
        last = x_out[leaf_dev - 1, :, part * LANES : (part + 1) * LANES]
        rows = slice(start + part * vectors, start + (part + 1) * vectors)
        for peer in range(GROUP):
            above = lax.rem(place + 1, GROUP) == peer
            out[peer, rows, :] = jnp.where(above, last, first)


def side_kernel(me_ref, *refs):
    inputs, outputs = refs[:11], refs[11:23]
    held, results = refs[23:34], refs[34:46]
    sems, leaf_sems, out_sems, leaf_out_sems = refs[46:]
    ids_s, links_s, transfer_v, couple_v, x_ref, top_v, lift_v, order_v, far_v, bases_v, blocks_v = held
    (
        inverse_out,
        up_high,
        up_low,
        path_high,
        path_low,
        near_out,
        edge_high,
        edge_low,
        leaf_high,
        leaf_low,
        bases_high,
        bases_low,
    ) = results
    leaf_dev, slots, leaf_size, _ = blocks_v.shape
    _, rank, _ = bases_v.shape
    copies = fetch(list(zip(inputs[:8], held[:8])), sems)
    by_leaf = [
        fetch([(x.at[leaf], v.at[leaf]) for x, v in zip(inputs[8:], held[8:])], leaf_sems.at[leaf])
        for leaf in range(leaf_dev)
    ]
    writes = []

    def write(*indices):
        for index in indices:
            writes.extend(
                fetch([(results[index], outputs[index])], out_sems.at[pl.ds(index, 1)])
            )

    me = me_ref[0]
    bits = [lax.shift_right_logical(me, level) & 1 for level in range(DEPTH)]

    def put_up(row, weights):
        span = slice(row, row + weights.shape[0])
        up_high[span], up_low[span] = halves(weights)

    def put_path(column, weights):
        span = slice(column * rank, column * rank + weights.shape[1])
        path_high[:, span], path_low[:, span] = halves(weights)

    def couplings(level):
        return jnp.concatenate(
            [
                links_s[level, column].astype(F32) * couple_v[level, column]
                for column in range(len(OFFSETS))
            ],
            axis=1,
        )

    def inverse():
        points_dev = order_v.shape[1]
        tiles = points_dev // LANES
        spot = order_v[...] - me * points_dev
        times = lax.broadcasted_iota(jnp.int32, (1, points_dev), 1)
        shape = (tiles, points_dev)
        match = lax.broadcasted_iota(jnp.int32, shape, 0) == lax.shift_right_logical(spot, 7)
        digits = [
            jnp.where(match, jnp.broadcast_to(digit.astype(F32), shape), 0.0)
            for digit in (lax.shift_right_logical(times, 4), times & 15)
        ]
        shape = (LANES, points_dev)
        match = lax.broadcasted_iota(jnp.int32, shape, 0) == (spot & (LANES - 1))
        both = lax.dot_general(
            jnp.concatenate(digits, axis=0).astype(BF16),
            jnp.where(match, 1.0, 0.0).astype(BF16),
            NT,
            preferred_element_type=F32,
        )
        inverse_out[...] = (both[:tiles] * 16.0 + both[tiles:]).astype(jnp.int32)

    def edge(index, leaf, outside):
        total = jnp.zeros((leaf_size, leaf_size), F32)
        for slot in range(1, slots):
            remote = ids_s[slot, leaf] - me * leaf_dev == outside
            total = total + jnp.where(remote, blocks_v[leaf, slot], 0.0)
        edge_high[index], edge_low[index] = halves(total)

    def chain():
        up = transfer_v[0].reshape(2 * rank, rank)
        path = transfer_v[0, bits[0]]
        put_up(0, up)
        put_path(0, couplings(0))
        row = up.shape[0]
        for level in range(1, DEPTH):
            yield
            if level < DEPTH - 1:
                up = jnp.concatenate(
                    [dot3(up, transfer_v[level, side], NN) for side in range(2)], axis=0
                )
                put_up(row, up)
                row += up.shape[0]
            put_path(level * len(OFFSETS), dot3(path, couplings(level), NN))
            path = dot3(path, transfer_v[level, bits[level]], NN)
        write(1, 2)
        yield
        top = dot3(path, top_v[...], NN)
        yield
        last = [dot3(top, transfer_v[DEPTH - 1, side], NT) for side in range(2)]
        put_path(DEPTH * len(OFFSETS), jnp.concatenate(last, axis=1))
        write(3, 4)
        yield
        inverse()
        write(0)

    links = chain()
    for copy in copies:
        copy.wait()
    for leaf in range(leaf_dev):
        for copy in by_leaf[leaf]:
            copy.wait()
        total = jnp.zeros(near_out.shape[1:], F32)
        for slot in range(slots):
            local = ids_s[slot, leaf] - me * leaf_dev
            here = (local >= 0) & (local < leaf_dev)
            x_leaf = jnp.where(here, x_ref[jnp.clip(local, 0, leaf_dev - 1)], 0.0)
            total = total + dot3(x_leaf, blocks_v[leaf, slot], NT)
        near_out[leaf] = total
        row = [far_v[leaf, slot] for slot in range(far_v.shape[1])] + [lift_v[leaf]]
        leaf_high[leaf], leaf_low[leaf] = halves(jnp.concatenate(row, axis=1))
        bases_high[leaf], bases_low[leaf] = halves(bases_v[leaf])
        if leaf == 0:
            edge(0, leaf, -1)
        if leaf == leaf_dev - 1:
            edge(1, leaf, leaf_dev)
        next(links, None)
        writes += fetch(
            [(v.at[leaf], x.at[leaf]) for v, x in zip(results[8:], outputs[8:])],
            leaf_out_sems.at[leaf],
        )
    for _ in links:
        pass
    write(5, 6, 7)
    for copy in writes:
        copy.wait()


def middle_kernel(
    leaf_dev,
    me_ref,
    group_hbm,
    up_high_hbm,
    up_low_hbm,
    half_out,
    nodes_out,
    roots_v,
    up_high,
    up_low,
    sems,
    half_sems,
):
    low = lax.rem(me_ref[0], GROUP) < REACH
    copies = fetch(
        [
            (group_hbm.at[:, pl.ds(leaf_dev * TILE, TILE), :], roots_v),
            (up_high_hbm, up_high),
            (up_low_hbm, up_low),
        ],
        sems,
    )
    rows = (leaf_dev + 1) * TILE
    edge_rows = group_hbm.shape[1] - rows
    first = jnp.where(low, REACH, 0)
    moves = [
        (group_hbm.at[first + part, pl.ds(0, rows)], half_out.at[pl.ds(part * rows, rows)])
        for part in range(REACH)
    ]
    moves.append(
        (
            group_hbm.at[jnp.where(low, GROUP - 1, 0), pl.ds(rows, edge_rows)],
            half_out.at[pl.ds(REACH * rows, edge_rows)],
        )
    )
    moves = fetch(moves, half_sems)
    for copy in copies:
        copy.wait()
    roots = [roots_v[peer] for peer in range(GROUP)]
    start, tiles = 0, []
    for level in range(1, DEPTH):
        width = 1 << level
        count = GROUP // width
        left = jnp.concatenate(
            [row_of(roots[n * width : (n + 1) * width]) for n in range(count)], axis=0
        )
        size = left.shape[1]
        nodes = dot_halves(left, up_high[start : start + size], up_low[start : start + size], NN)
        start += size
        tiles += [fold(nodes[n * 2 * TILE : (n + 1) * 2 * TILE]) for n in range(count)]
    row = REACH * rows + edge_rows
    for index, tile in enumerate(tiles):
        half_out[row + index * TILE : row + (index + 1) * TILE, :] = tile
        for peer in range(nodes_out.shape[0]):
            nodes_out[peer, index] = tile
    for copy in moves:
        copy.wait()


def down_kernel(parts, me_ref, *refs):
    node_parts, refs = refs[:parts], refs[parts:]
    count = (len(refs) - 5) // 2
    out_ref = refs[count]
    held = refs[count + 1 : 2 * count + 1]
    nodes_ref, y_tree, sems, node_sems = refs[2 * count + 1 :]
    me = me_ref[0]
    groups = nodes_ref.shape[0]
    group = lax.shift_right_logical(me, 3)
    place = me & (GROUP - 1)
    low = place < REACH
    half_hbm = refs[1]
    if parts > 1:
        near_by, far_by = jnp.where(low, groups - 1, 1), jnp.where(low, 1, groups - 1)
        start = half_hbm.shape[0] - NODES * TILE
        node_copies = fetch(
            [
                (part.at[0], nodes_ref.at[lax.rem(group + by, groups)])
                for part, by in zip(node_parts, (0, far_by, 2))
            ]
            + [
                (
                    half_hbm.at[pl.ds(start + index * TILE, TILE)],
                    nodes_ref.at[lax.rem(group + near_by, groups), index],
                )
                for index in range(NODES)
            ],
            node_sems,
        )
    else:
        node_copies = fetch([(node_parts[0], nodes_ref)], node_sems)
    copies = fetch(list(zip(refs[:count], held)), sems)
    (
        group_ref,
        half_ref,
        path_high,
        path_low,
        far_ids_s,
        far_count_s,
        edge_high,
        edge_low,
        leaf_high,
        leaf_low,
        bases_high,
        bases_low,
        near_ref,
        inverse_ref,
    ) = held
    leaf_dev, vectors, leaf_size = near_ref.shape
    points_dev = out_ref.shape[1]
    slots = far_ids_s.shape[1]
    per_leaf = leaf_size // LANES
    start = (leaf_dev + 1) * TILE
    edge_rows = group_ref.shape[1] - start

    def tile_of(subtree, index):
        other = subtree & (GROUP - 1)
        inside = lax.shift_right_arithmetic(subtree, 3) == group
        row = pl.multiple_of(index * TILE, TILE)
        near_row = jnp.clip(other - jnp.where(low, REACH, 0), 0, REACH - 1) * start
        here = group_ref[other, pl.ds(row, TILE), :]
        there = half_ref[pl.ds(pl.multiple_of(near_row + row, TILE), TILE), :]
        return jnp.where(inside, here, there)

    for copy in node_copies + copies[:4]:
        copy.wait()
    partners = []
    for level in range(DEPTH):
        node = lax.shift_right_logical(me, level)
        size = (groups * GROUP) >> level
        for offset in OFFSETS:
            other = node + offset
            used = (other >= 0) & (other < size)
            other = jnp.clip(other, 0, size - 1)
            if level == 0:
                tile = tile_of(other, leaf_dev)
            else:
                shift = DEPTH - 1 - level
                first = GROUP - (2 << shift)
                tile = nodes_ref[
                    lax.shift_right_logical(other, shift), first + (other & ((1 << shift) - 1))
                ]
            partners.append(jnp.where(used, tile, 0.0))
    top = lax.shift_right_logical(me, DEPTH)
    for side in range(2):
        blended = jnp.zeros((TILE, LANES), F32)
        for other in range(groups // 2):
            distance = jnp.abs(top - other)
            weight = jnp.where(distance >= 2, 1.0 / jnp.maximum(distance, 1).astype(F32), 0.0)
            blended = blended + weight * nodes_ref[2 * other + side, GROUP - 2]
        partners.append(blended)
    down = dot_halves(row_of(partners), path_high[...], path_low[...], NT)

    for copy in copies[4:8]:
        copy.wait()
    edges = []
    for index, offset in ((0, -1), (1, 1)):
        other = me + offset
        inside = lax.shift_right_arithmetic(other, 3) == group
        here = group_ref[other & (GROUP - 1), start:, :]
        chosen = jnp.where(inside, here, half_ref[REACH * start : REACH * start + edge_rows, :])
        edges.append(
            jnp.concatenate(
                [chosen[part * vectors : (part + 1) * vectors] for part in range(per_leaf)], axis=1
            )
        )
    edge_parts = [
        dot_halves(edges[index], edge_high[index], edge_low[index], NT) for index in range(2)
    ]

    for copy in copies[8:]:
        copy.wait()
    for leaf in range(leaf_dev):
        picked = []
        for slot in range(slots):
            used = slot < far_count_s[leaf]
            spot = far_ids_s[leaf, slot]
            tile = tile_of(lax.shift_right_logical(spot, 3), spot & (leaf_dev - 1))
            picked.append(jnp.where(used, tile, 0.0))
        left = jnp.concatenate([row_of(picked), down], axis=1)
        leaf_out = dot_halves(left, leaf_high[leaf], leaf_low[leaf], NT)
        y_leaf = near_ref[leaf] + dot_halves(leaf_out, bases_high[leaf], bases_low[leaf], NN)
        if leaf == 0:
            y_leaf = y_leaf + edge_parts[0]
        if leaf == leaf_dev - 1:
            y_leaf = y_leaf + edge_parts[1]
        y_tree[:, leaf * leaf_size : (leaf + 1) * leaf_size] = y_leaf

    y = y_tree[...]
    for tile in range(points_dev // LANES):
        spot = inverse_ref[tile : tile + 1, :]
        out_ref[:, tile * LANES : (tile + 1) * LANES] = lane_gather(
            y, lax.shift_right_logical(spot, 7), spot & (LANES - 1)
        )


def local(
    devices,
    points,
    order,
    bases,
    lift,
    near_ids,
    near_blocks,
    far_ids,
    far_count,
    far_blocks,
    transfer,
    couple,
    links,
    top_couple,
):
    me = lax.axis_index("leaf").astype(jnp.int32).reshape(1)
    vectors, points_dev = points.shape
    leaf_dev, leaf_size, rank = bases.shape
    slots = near_ids.shape[1]
    far_slots = far_ids.shape[1]
    bases_t = jnp.swapaxes(bases, 1, 2)
    tiles = points_dev // LANES
    edge_rows = vectors * (leaf_size // LANES)
    rows = (leaf_dev + 1) * TILE
    groups = devices // GROUP
    order_tiles = order.reshape(tiles, LANES)
    shape = jax.ShapeDtypeStruct

    group_out, tree_x = pl.pallas_call(
        up_kernel,
        out_shape=[
            shape((GROUP, rows + edge_rows, LANES), F32),
            shape((leaf_dev, vectors, leaf_size), F32),
        ],
        in_specs=[SMEM] + [HBM] * 4,
        out_specs=[VMEM] * 2,
        scratch_shapes=[
            pltpu.VMEM(points.shape, F32),
            pltpu.VMEM((tiles, LANES), jnp.int32),
            pltpu.VMEM(bases_t.shape, F32),
            pltpu.VMEM(lift.shape, F32),
            pltpu.SemaphoreType.DMA((4,)),
        ],
        compiler_params=PARAMS,
        name="up",
    )(me, points, order_tiles, bases_t, lift)

    aligned = [[g * GROUP + i for i in range(GROUP)] for g in range(groups)]
    group_in = lax.all_to_all(group_out, "leaf", 0, 0, axis_index_groups=aligned, tiled=True)

    ids_t = near_ids.T
    links_own = links.reshape(links.shape[1:])
    composed_rows = (2 + 4 + 8) * rank
    path_columns = (DEPTH * len(OFFSETS) + 2) * rank
    leaf_columns = (far_slots + 1) * rank
    both = lambda *size: [shape(size, BF16)] * 2
    operands = (
        ids_t,
        links_own,
        transfer,
        couple,
        tree_x,
        top_couple,
        lift,
        order.reshape(1, points_dev),
        far_blocks,
        bases_t,
        near_blocks,
    )
    results = (
        [shape((tiles, LANES), jnp.int32)]
        + both(composed_rows, rank)
        + both(rank, path_columns)
        + [shape(tree_x.shape, F32)]
        + both(2, leaf_size, leaf_size)
        + both(leaf_dev, rank, leaf_columns)
        + both(leaf_dev, rank, leaf_size)
    )
    (
        inverse,
        up_high,
        up_low,
        path_high,
        path_low,
        near_part,
        edge_high,
        edge_low,
        leaf_high,
        leaf_low,
        bases_high,
        bases_low,
    ) = pl.pallas_call(
        side_kernel,
        out_shape=results,
        in_specs=[SMEM] + [HBM] * len(operands),
        out_specs=[HBM] * len(results),
        scratch_shapes=[
            (pltpu.SMEM if x is ids_t or x is links_own else pltpu.VMEM)(x.shape, x.dtype)
            for x in operands
        ]
        + [pltpu.VMEM(x.shape, x.dtype) for x in results]
        + [
            pltpu.SemaphoreType.DMA((8,)),
            pltpu.SemaphoreType.DMA((leaf_dev, 3)),
            pltpu.SemaphoreType.DMA((8,)),
            pltpu.SemaphoreType.DMA((leaf_dev, 4)),
        ],
        compiler_params=PARAMS,
        cost_estimate=pl.CostEstimate(
            flops=6 * vectors * near_blocks.size,
            bytes_accessed=4 * near_blocks.size,
            transcendentals=0,
        ),
        name="side",
    )(me, *operands)

    by_permute = groups == 4
    half_out, nodes_out = pl.pallas_call(
        functools.partial(middle_kernel, leaf_dev),
        out_shape=[
            shape((REACH * rows + edge_rows + NODES * TILE, LANES), F32),
            shape((1 if by_permute else groups, NODES, TILE, LANES), F32),
        ],
        in_specs=[SMEM] + [HBM] * 3,
        out_specs=[VMEM] * 2,
        scratch_shapes=[
            pltpu.VMEM((GROUP, TILE, LANES), F32),
            pltpu.VMEM(up_high.shape, BF16),
            pltpu.VMEM(up_low.shape, BF16),
            pltpu.SemaphoreType.DMA((3,)),
            pltpu.SemaphoreType.DMA((REACH + 1,)),
        ],
        compiler_params=PARAMS,
        name="middle",
    )(me, group_in, up_high, up_low)

    def shifted(x, low, high):
        pairs = []
        for device in range(devices):
            by = low if device % GROUP < REACH else high
            pairs.append(((device + by * GROUP) % devices, device))
        return lax.ppermute(x, "leaf", pairs)

    half_in = shifted(half_out, -1, 1)
    if by_permute:
        node_parts = (nodes_out, shifted(nodes_out, 1, -1), shifted(nodes_out, 2, 2))
    else:
        across = [[g * GROUP + i for g in range(groups)] for i in range(GROUP)]
        node_parts = (lax.all_to_all(nodes_out, "leaf", 0, 0, axis_index_groups=across, tiled=True),)

    operands = (
        group_in,
        half_in,
        path_high,
        path_low,
        far_ids,
        far_count,
        edge_high,
        edge_low,
        leaf_high,
        leaf_low,
        bases_high,
        bases_low,
        near_part,
        inverse,
    )
    return pl.pallas_call(
        functools.partial(down_kernel, len(node_parts)),
        out_shape=shape((vectors, points_dev), F32),
        in_specs=[SMEM] + [HBM] * (len(node_parts) + len(operands)),
        out_specs=VMEM,
        scratch_shapes=[
            (pltpu.SMEM if x is far_ids or x is far_count else pltpu.VMEM)(x.shape, x.dtype)
            for x in operands
        ]
        + [
            pltpu.VMEM((groups, NODES, TILE, LANES), F32),
            pltpu.VMEM((vectors, points_dev), F32),
            pltpu.SemaphoreType.DMA((len(operands),)),
            pltpu.SemaphoreType.DMA((len(node_parts) + NODES,)),
        ],
        compiler_params=PARAMS,
        name="down",
    )(me, *node_parts, *operands)


def solution(mesh):
    in_specs = (
        P(None, "leaf"),
        P("leaf"),
        P("leaf", None, None),
        P("leaf", None, None),
        P("leaf", None),
        P("leaf", None, None, None),
        P("leaf", None),
        P("leaf"),
        P("leaf", None, None, None),
        P(),
        P(),
        P("leaf", None, None),
        P(),
    )
    return jax.shard_map(
        functools.partial(local, mesh.shape["leaf"]),
        mesh=mesh,
        in_specs=in_specs,
        out_specs=P(None, "leaf"),
        check_vma=False,
    )
```

```python
import functools

import jax
import jax.numpy as jnp
from jax import lax
from jax.experimental import pallas as pl
from jax.experimental.pallas import tpu as pltpu
from jax.sharding import PartitionSpec as P

REACH = 4
DEPTH = 4
OFFSETS = (-3, -2, 2, 3)
GROUP = 2 * REACH
LANES = 128
TILE = 8
NODES = GROUP - 1
VMEM_LIMIT = 64 * 1024 * 1024

NN = (((1,), (0,)), ((), ()))
NT = (((1,), (1,)), ((), ()))

VMEM = pl.BlockSpec(memory_space=pltpu.VMEM)
SMEM = pl.BlockSpec(memory_space=pltpu.SMEM)
HBM = pl.BlockSpec(memory_space=pltpu.HBM)
PARAMS = pltpu.CompilerParams(vmem_limit_bytes=VMEM_LIMIT)
F32 = jnp.float32
BF16 = jnp.bfloat16


def halves(x):
    high = x.astype(BF16)
    low = (x - high.astype(F32)).astype(BF16)
    return high, low


def dot_halves(a, b_high, b_low, dims):
    a_high, a_low = halves(a)
    rows = a.shape[0]
    both = lax.dot_general(
        jnp.concatenate([a_high, a_low], axis=0), b_high, dims, preferred_element_type=F32
    )
    cross = lax.dot_general(a_high, b_low, dims, preferred_element_type=F32)
    return both[:rows] + (both[rows:] + cross)


def pair_dot(a, b, w_high, w_low):
    a_high, a_low = halves(a)
    b_high, b_low = halves(b)
    rows = a.shape[0]
    both = lax.dot_general(
        jnp.concatenate([a_high, b_high, a_low, b_low], axis=0),
        w_high,
        NN,
        preferred_element_type=F32,
    )
    cross = lax.dot_general(
        jnp.concatenate([a_high, b_high], axis=0), w_low, NN, preferred_element_type=F32
    )
    total = both[: 2 * rows] + (both[2 * rows :] + cross)
    return total[:rows], total[rows:]


def dot3(a, b, dims):
    return dot_halves(a, *halves(b), dims)


def fold(x):
    return jnp.concatenate([x[:TILE], x[TILE:]], axis=1)


def beside(p, q):
    rank = p.shape[1] // 2
    left = lax.broadcasted_iota(jnp.int32, p.shape, 1) < rank
    return jnp.concatenate(
        [
            jnp.where(left, p, pltpu.roll(q, rank, 1)),
            jnp.where(left, pltpu.roll(p, rank, 1), q),
        ],
        axis=0,
    )


def row_of(tiles):
    return jnp.concatenate([beside(*tiles[k : k + 2]) for k in range(0, len(tiles), 2)], axis=1)


def lane_gather(x, high, low):
    rows, columns = x.shape
    high = jnp.broadcast_to(high, (rows, LANES))
    low = jnp.broadcast_to(low, (rows, LANES))
    result = jnp.zeros((rows, LANES), x.dtype)
    for source in range(columns // LANES):
        tile = x[:, source * LANES : (source + 1) * LANES]
        moved = jnp.take_along_axis(tile, low, axis=1, mode="promise_in_bounds")
        result = jnp.where(high == source, moved, result)
    return result


def fetch(pairs, sems):
    copies = [
        pltpu.make_async_copy(source, target, sems.at[index])
        for index, (source, target) in enumerate(pairs)
    ]
    for copy in copies:
        copy.start()
    return copies


def up_kernel(
    me_ref, points_hbm, order_hbm, bases_hbm, lift_hbm, out, x_out, points_v, order_v, bases_v, lift_v, sems
):
    copies = fetch(
        [(order_hbm, order_v), (points_hbm, points_v), (bases_hbm, bases_v), (lift_hbm, lift_v)], sems
    )
    me = me_ref[0]
    leaf_dev, rank, leaf_size = bases_v.shape
    vectors, points_dev = points_v.shape
    copies[0].wait()
    copies[1].wait()
    points = points_v[...]
    per_leaf = leaf_size // LANES
    for t in range(points_dev // LANES):
        spot = order_v[t : t + 1, :] - me * points_dev
        column = t % per_leaf * LANES
        x_out[t // per_leaf, :, column : column + LANES] = lane_gather(
            points, lax.shift_right_logical(spot, 7), spot & (LANES - 1)
        )
    copies[2].wait()
    coefs = [dot3(x_out[leaf], bases_v[leaf], NT) for leaf in range(leaf_dev)]
    tiles = [fold(coef) for coef in coefs]
    copies[3].wait()
    weights = lift_v[...].reshape(leaf_dev * rank, rank)
    tiles.append(fold(dot3(jnp.concatenate(coefs, axis=1), weights, NN)))
    for peer in range(GROUP):
        for index, tile in enumerate(tiles):
            out[peer, index * TILE : (index + 1) * TILE, :] = tile
    place = lax.rem(me, GROUP)
    start = len(tiles) * TILE
    for part in range(per_leaf):
        first = x_out[0, :, part * LANES : (part + 1) * LANES]
        last = x_out[leaf_dev - 1, :, part * LANES : (part + 1) * LANES]
        rows = slice(start + part * vectors, start + (part + 1) * vectors)
        for peer in range(GROUP):
            above = lax.rem(place + 1, GROUP) == peer
            out[peer, rows, :] = jnp.where(above, last, first)


def near_kernel(me_ref, *refs):
    inputs, outputs = refs[:4], refs[4:9]
    held, results = refs[9:13], refs[13:18]
    sems, block_sems, out_sems = refs[18:]
    ids_s, x_v, transfer_v, blocks_v = held
    near_out, up_high, up_low, edge_high, edge_low = results
    leaf_dev, slots, leaf_size, _ = blocks_v.shape
    vectors = x_v.shape[1]
    rank = transfer_v.shape[2]
    me = me_ref[0]
    copies = fetch(list(zip(inputs[:3], held[:3])), sems)

    def block(leaf):
        return pltpu.make_async_copy(inputs[3].at[leaf], blocks_v.at[leaf], block_sems.at[leaf])

    for leaf in range(leaf_dev):
        block(leaf).start()
    for copy in copies:
        copy.wait()
    columns = leaf_dev * vectors
    x_high, x_low = halves(x_v[...].reshape(columns, leaf_size).T)
    x_both = jnp.concatenate([x_high, x_low], axis=1)
    owner = lax.broadcasted_iota(jnp.int32, (leaf_size, columns), 1) // vectors

    composed = transfer_v[0].reshape(2 * rank, rank)
    row = 0
    for level in range(1, DEPTH):
        rows = composed.shape[0]
        up_high[row : row + rows], up_low[row : row + rows] = halves(composed)
        row += rows
        if level < DEPTH - 1:
            composed = jnp.concatenate(
                [dot3(composed, transfer_v[level, side], NN) for side in range(2)], axis=0
            )
    writes = fetch([(results[k], outputs[k]) for k in (1, 2)], out_sems)

    def leaf_step(leaf, carry):
        block(leaf).wait()
        total = jnp.zeros((leaf_size, columns), F32)
        for slot in range(slots):
            high, low = halves(blocks_v[leaf, slot])
            wide = lax.dot_general(high, x_both, NN, preferred_element_type=F32)
            cross = lax.dot_general(low, x_high, NN, preferred_element_type=F32)
            product = wide[:, :columns] + (wide[:, columns:] + cross)
            total = total + jnp.where(owner == ids_s[slot, leaf] - me * leaf_dev, product, 0.0)
        parts = total.T
        result = parts[:vectors]
        for other in range(1, leaf_dev):
            result = result + parts[other * vectors : (other + 1) * vectors]
        near_out[leaf] = result
        return carry

    lax.fori_loop(0, leaf_dev, leaf_step, 0)

    for index, leaf, outside in ((0, 0, -1), (1, leaf_dev - 1, leaf_dev)):
        total = jnp.zeros((leaf_size, leaf_size), F32)
        for slot in range(1, slots):
            remote = ids_s[slot, leaf] - me * leaf_dev == outside
            total = total + jnp.where(remote, blocks_v[leaf, slot], 0.0)
        edge_high[index], edge_low[index] = halves(total.T)
    writes += fetch([(results[k], outputs[k]) for k in (0, 3, 4)], out_sems.at[pl.ds(2, 3)])
    for copy in writes:
        copy.wait()


def weight_kernel(me_ref, *refs):
    inputs, outputs = refs[:8], refs[8:15]
    held, results = refs[15:23], refs[23:30]
    sems, out_sems = refs[30:]
    links_s, transfer_v, couple_v, top_v, lift_v, far_v, bases_v, order_v = held
    path_high, path_low, leaf_high, leaf_low, bases_high, bases_low, inverse_out = results
    copies = fetch(list(zip(inputs, held)), sems)
    me = me_ref[0]
    pairs, leaf_rows, _ = leaf_high.shape
    rank = top_v.shape[0]
    slots = far_v.shape[1]
    for copy in copies:
        copy.wait()

    path = None
    blocks = []
    for level in range(DEPTH):
        weights = [
            links_s[level, column].astype(F32) * couple_v[level, column]
            for column in range(len(OFFSETS))
        ]
        weights = jnp.concatenate(weights, axis=1)
        step = transfer_v[level, lax.shift_right_logical(me, level) & 1]
        if path is not None:
            weights = dot3(path, weights, NN)
            step = dot3(path, step, NN)
        path = step
        blocks += [weights[:, k * rank : (k + 1) * rank] for k in range(len(OFFSETS))]
    top = dot3(path, top_v[...], NN)
    blocks += [dot3(top, transfer_v[DEPTH - 1, side], NT) for side in range(2)]
    half = len(blocks) // 2
    for index in range(half):
        span = slice(index * rank, (index + 1) * rank)
        both = jnp.concatenate([blocks[index], blocks[half + index]], axis=0).T
        path_high[span], path_low[span] = halves(both)

    for pair in range(pairs):
        for slot in range(slots + 1):
            two = [
                lift_v[2 * pair + k] if slot == slots else far_v[2 * pair + k, slot]
                for k in range(2)
            ]
            span = slice(slot * rank, (slot + 1) * rank)
            leaf_high[pair, span], leaf_low[pair, span] = halves(jnp.concatenate(two, axis=0).T)
        bases_high[pair], bases_low[pair] = halves(bases_v[pair])

    points_dev = order_v.shape[1]
    tiles = points_dev // LANES
    spot = order_v[...] - me * points_dev
    times = lax.broadcasted_iota(jnp.int32, (1, points_dev), 1)
    shape = (tiles, points_dev)
    match = lax.broadcasted_iota(jnp.int32, shape, 0) == lax.shift_right_logical(spot, 7)
    digits = [
        jnp.where(match, jnp.broadcast_to(digit.astype(F32), shape), 0.0)
        for digit in (lax.shift_right_logical(times, 4), times & 15)
    ]
    shape = (LANES, points_dev)
    match = lax.broadcasted_iota(jnp.int32, shape, 0) == (spot & (LANES - 1))
    both = lax.dot_general(
        jnp.concatenate(digits, axis=0).astype(BF16),
        jnp.where(match, 1.0, 0.0).astype(BF16),
        NT,
        preferred_element_type=F32,
    )
    inverse_out[...] = (both[:tiles] * 16.0 + both[tiles:]).astype(jnp.int32)
    for copy in fetch(list(zip(results, outputs)), out_sems):
        copy.wait()


def middle_kernel(
    leaf_dev,
    me_ref,
    group_hbm,
    up_high_hbm,
    up_low_hbm,
    half_out,
    nodes_out,
    roots_v,
    up_high,
    up_low,
    sems,
    half_sems,
):
    low = lax.rem(me_ref[0], GROUP) < REACH
    copies = fetch(
        [
            (group_hbm.at[:, pl.ds(leaf_dev * TILE, TILE), :], roots_v),
            (up_high_hbm, up_high),
            (up_low_hbm, up_low),
        ],
        sems,
    )
    rows = (leaf_dev + 1) * TILE
    edge_rows = group_hbm.shape[1] - rows
    first = jnp.where(low, REACH, 0)
    moves = [
        (group_hbm.at[first + part, pl.ds(0, rows)], half_out.at[pl.ds(part * rows, rows)])
        for part in range(REACH)
    ]
    moves.append(
        (
            group_hbm.at[jnp.where(low, GROUP - 1, 0), pl.ds(rows, edge_rows)],
            half_out.at[pl.ds(REACH * rows, edge_rows)],
        )
    )
    moves = fetch(moves, half_sems)
    for copy in copies:
        copy.wait()
    roots = [roots_v[peer] for peer in range(GROUP)]
    start, tiles = 0, []
    for level in range(1, DEPTH):
        width = 1 << level
        count = GROUP // width
        left = jnp.concatenate(
            [row_of(roots[n * width : (n + 1) * width]) for n in range(count)], axis=0
        )
        size = left.shape[1]
        nodes = dot_halves(left, up_high[start : start + size], up_low[start : start + size], NN)
        start += size
        tiles += [fold(nodes[n * 2 * TILE : (n + 1) * 2 * TILE]) for n in range(count)]
    row = REACH * rows + edge_rows
    for index, tile in enumerate(tiles):
        half_out[row + index * TILE : row + (index + 1) * TILE, :] = tile
        for peer in range(nodes_out.shape[0]):
            nodes_out[peer, index] = tile
    for copy in moves:
        copy.wait()


def down_kernel(parts, me_ref, *refs):
    node_parts, refs = refs[:parts], refs[parts:]
    count = (len(refs) - 5) // 2
    out_ref = refs[count]
    held = refs[count + 1 : 2 * count + 1]
    nodes_ref, y_tree, sems, node_sems = refs[2 * count + 1 :]
    me = me_ref[0]
    groups = nodes_ref.shape[0]
    group = lax.shift_right_logical(me, 3)
    place = me & (GROUP - 1)
    low = place < REACH
    half_hbm = refs[1]
    if parts > 1:
        near_by, far_by = jnp.where(low, groups - 1, 1), jnp.where(low, 1, groups - 1)
        start = half_hbm.shape[0] - NODES * TILE
        node_copies = fetch(
            [
                (part.at[0], nodes_ref.at[lax.rem(group + by, groups)])
                for part, by in zip(node_parts, (0, far_by, 2))
            ]
            + [
                (
                    half_hbm.at[pl.ds(start + index * TILE, TILE)],
                    nodes_ref.at[lax.rem(group + near_by, groups), index],
                )
                for index in range(NODES)
            ],
            node_sems,
        )
    else:
        node_copies = fetch([(node_parts[0], nodes_ref)], node_sems)
    copies = fetch(list(zip(refs[:count], held)), sems)
    (
        group_ref,
        half_ref,
        path_high,
        path_low,
        far_ids_s,
        far_count_s,
        edge_high,
        edge_low,
        leaf_high,
        leaf_low,
        bases_high,
        bases_low,
        near_ref,
        inverse_ref,
    ) = held
    leaf_dev, vectors, leaf_size = near_ref.shape
    points_dev = out_ref.shape[1]
    slots = far_ids_s.shape[1]
    per_leaf = leaf_size // LANES
    rank = bases_high.shape[1] // 2
    start = (leaf_dev + 1) * TILE
    edge_rows = group_ref.shape[1] - start

    def tile_of(subtree, index):
        other = subtree & (GROUP - 1)
        inside = lax.shift_right_arithmetic(subtree, 3) == group
        row = pl.multiple_of(index * TILE, TILE)
        near_row = jnp.clip(other - jnp.where(low, REACH, 0), 0, REACH - 1) * start
        here = group_ref[other, pl.ds(row, TILE), :]
        there = half_ref[pl.ds(pl.multiple_of(near_row + row, TILE), TILE), :]
        return jnp.where(inside, here, there)

    for copy in node_copies + copies[:4]:
        copy.wait()
    partners = []
    for level in range(DEPTH):
        node = lax.shift_right_logical(me, level)
        size = (groups * GROUP) >> level
        for offset in OFFSETS:
            other = node + offset
            used = (other >= 0) & (other < size)
            other = jnp.clip(other, 0, size - 1)
            if level == 0:
                tile = tile_of(other, leaf_dev)
            else:
                shift = DEPTH - 1 - level
                first = GROUP - (2 << shift)
                tile = nodes_ref[
                    lax.shift_right_logical(other, shift), first + (other & ((1 << shift) - 1))
                ]
            partners.append(jnp.where(used, tile, 0.0))
    top = lax.shift_right_logical(me, DEPTH)
    for side in range(2):
        blended = jnp.zeros((TILE, LANES), F32)
        for other in range(groups // 2):
            distance = jnp.abs(top - other)
            weight = jnp.where(distance >= 2, 1.0 / jnp.maximum(distance, 1).astype(F32), 0.0)
            blended = blended + weight * nodes_ref[2 * other + side, GROUP - 2]
        partners.append(blended)
    half = len(partners) // 2
    row = row_of(partners)
    first, second = pair_dot(
        row[:, : half * rank], row[:, half * rank :], path_high[...], path_low[...]
    )
    down = first[:, :rank] + second[:, rank:]

    for copy in copies[4:8]:
        copy.wait()
    edges = []
    for index, offset in ((0, -1), (1, 1)):
        other = me + offset
        inside = lax.shift_right_arithmetic(other, 3) == group
        here = group_ref[other & (GROUP - 1), start:, :]
        chosen = jnp.where(inside, here, half_ref[REACH * start : REACH * start + edge_rows, :])
        edges.append(
            jnp.concatenate(
                [chosen[part * vectors : (part + 1) * vectors] for part in range(per_leaf)], axis=1
            )
        )
    edge_parts = [
        dot_halves(edges[index], edge_high[index], edge_low[index], NN) for index in range(2)
    ]

    for copy in copies[8:]:
        copy.wait()
    left_half = lax.broadcasted_iota(jnp.int32, (vectors, 2 * rank), 1) < rank
    for pair in range(leaf_dev // 2):
        rows = []
        for leaf in (2 * pair, 2 * pair + 1):
            picked = []
            for slot in range(slots):
                used = slot < far_count_s[leaf]
                spot = far_ids_s[leaf, slot]
                tile = tile_of(lax.shift_right_logical(spot, 3), spot & (leaf_dev - 1))
                picked.append(jnp.where(used, tile, 0.0))
            rows.append(jnp.concatenate([row_of(picked), down], axis=1))
        first, second = pair_dot(*rows, leaf_high[pair], leaf_low[pair])
        first = jnp.where(left_half, first, 0.0)
        second = jnp.where(left_half, 0.0, second)
        parts = pair_dot(first, second, bases_high[pair], bases_low[pair])
        for leaf, part in zip((2 * pair, 2 * pair + 1), parts):
            y_leaf = near_ref[leaf] + part
            if leaf == 0:
                y_leaf = y_leaf + edge_parts[0]
            if leaf == leaf_dev - 1:
                y_leaf = y_leaf + edge_parts[1]
            y_tree[:, leaf * leaf_size : (leaf + 1) * leaf_size] = y_leaf

    y = y_tree[...]
    for tile in range(points_dev // LANES):
        spot = inverse_ref[tile : tile + 1, :]
        out_ref[:, tile * LANES : (tile + 1) * LANES] = lane_gather(
            y, lax.shift_right_logical(spot, 7), spot & (LANES - 1)
        )


def local(
    devices,
    points,
    order,
    bases,
    lift,
    near_ids,
    near_blocks,
    far_ids,
    far_count,
    far_blocks,
    transfer,
    couple,
    links,
    top_couple,
):
    me = lax.axis_index("leaf").astype(jnp.int32).reshape(1)
    vectors, points_dev = points.shape
    leaf_dev, leaf_size, rank = bases.shape
    slots = near_ids.shape[1]
    far_slots = far_ids.shape[1]
    bases_t = jnp.swapaxes(bases, 1, 2)
    tiles = points_dev // LANES
    edge_rows = vectors * (leaf_size // LANES)
    rows = (leaf_dev + 1) * TILE
    groups = devices // GROUP
    order_tiles = order.reshape(tiles, LANES)
    shape = jax.ShapeDtypeStruct

    group_out, tree_x = pl.pallas_call(
        up_kernel,
        out_shape=[
            shape((GROUP, rows + edge_rows, LANES), F32),
            shape((leaf_dev, vectors, leaf_size), F32),
        ],
        in_specs=[SMEM] + [HBM] * 4,
        out_specs=[VMEM] * 2,
        scratch_shapes=[
            pltpu.VMEM(points.shape, F32),
            pltpu.VMEM((tiles, LANES), jnp.int32),
            pltpu.VMEM(bases_t.shape, F32),
            pltpu.VMEM(lift.shape, F32),
            pltpu.SemaphoreType.DMA((4,)),
        ],
        compiler_params=PARAMS,
        name="up",
    )(me, points, order_tiles, bases_t, lift)

    aligned = [[g * GROUP + i for i in range(GROUP)] for g in range(groups)]
    group_in = lax.all_to_all(group_out, "leaf", 0, 0, axis_index_groups=aligned, tiled=True)

    ids_t = near_ids.T
    both = lambda *size: [shape(size, BF16)] * 2

    def call(kernel, operands, results, scalar, sems, cost, name):
        return pl.pallas_call(
            kernel,
            out_shape=results,
            in_specs=[SMEM] + [HBM] * len(operands),
            out_specs=[HBM] * len(results),
            scratch_shapes=[
                (pltpu.SMEM if x is scalar else pltpu.VMEM)(x.shape, x.dtype) for x in operands
            ]
            + [pltpu.VMEM(x.shape, x.dtype) for x in results]
            + [pltpu.SemaphoreType.DMA((count,)) for count in sems],
            compiler_params=PARAMS,
            cost_estimate=pl.CostEstimate(flops=cost * 250, bytes_accessed=cost, transcendentals=0),
            name=name,
        )(me, *operands)

    near_part, up_high, up_low, edge_high, edge_low = call(
        near_kernel,
        (ids_t, tree_x, transfer, near_blocks),
        [shape(tree_x.shape, F32)] + both(14 * rank, rank) + both(2, leaf_size, leaf_size),
        ids_t,
        (3, leaf_dev, 5),
        12_000_000,
        "near",
    )
    links_own = links.reshape(links.shape[1:])
    path_rows = (DEPTH * len(OFFSETS) + 2) // 2 * rank
    path_high, path_low, leaf_high, leaf_low, bases_high, bases_low, inverse = call(
        weight_kernel,
        (
            links_own,
            transfer,
            couple,
            top_couple,
            lift,
            far_blocks,
            bases_t.reshape(leaf_dev // 2, 2 * rank, leaf_size),
            order.reshape(1, points_dev),
        ),
        both(path_rows, 2 * rank)
        + both(leaf_dev // 2, (far_slots + 1) * rank, 2 * rank)
        + both(leaf_dev // 2, 2 * rank, leaf_size)
        + [shape((tiles, LANES), jnp.int32)],
        links_own,
        (8, 7),
        12_000_000,
        "weights",
    )

    by_permute = groups == 4
    half_out, nodes_out = pl.pallas_call(
        functools.partial(middle_kernel, leaf_dev),
        out_shape=[
            shape((REACH * rows + edge_rows + NODES * TILE, LANES), F32),
            shape((1 if by_permute else groups, NODES, TILE, LANES), F32),
        ],
        in_specs=[SMEM] + [HBM] * 3,
        out_specs=[VMEM] * 2,
        scratch_shapes=[
            pltpu.VMEM((GROUP, TILE, LANES), F32),
            pltpu.VMEM(up_high.shape, BF16),
            pltpu.VMEM(up_low.shape, BF16),
            pltpu.SemaphoreType.DMA((3,)),
            pltpu.SemaphoreType.DMA((REACH + 1,)),
        ],
        compiler_params=PARAMS,
        name="middle",
    )(me, group_in, up_high, up_low)

    def shifted(x, low, high):
        pairs = []
        for device in range(devices):
            by = low if device % GROUP < REACH else high
            pairs.append(((device + by * GROUP) % devices, device))
        return lax.ppermute(x, "leaf", pairs)

    half_in = shifted(half_out, -1, 1)
    if by_permute:
        node_parts = (nodes_out, shifted(nodes_out, 1, -1), shifted(nodes_out, 2, 2))
    else:
        across = [[g * GROUP + i for g in range(groups)] for i in range(GROUP)]
        node_parts = (lax.all_to_all(nodes_out, "leaf", 0, 0, axis_index_groups=across, tiled=True),)

    operands = (
        group_in,
        half_in,
        path_high,
        path_low,
        far_ids,
        far_count,
        edge_high,
        edge_low,
        leaf_high,
        leaf_low,
        bases_high,
        bases_low,
        near_part,
        inverse,
    )
    return pl.pallas_call(
        functools.partial(down_kernel, len(node_parts)),
        out_shape=shape((vectors, points_dev), F32),
        in_specs=[SMEM] + [HBM] * (len(node_parts) + len(operands)),
        out_specs=VMEM,
        scratch_shapes=[
            (pltpu.SMEM if x is far_ids or x is far_count else pltpu.VMEM)(x.shape, x.dtype)
            for x in operands
        ]
        + [
            pltpu.VMEM((groups, NODES, TILE, LANES), F32),
            pltpu.VMEM((vectors, points_dev), F32),
            pltpu.SemaphoreType.DMA((len(operands),)),
            pltpu.SemaphoreType.DMA((len(node_parts) + NODES,)),
        ],
        compiler_params=PARAMS,
        name="down",
    )(me, *node_parts, *operands)


def solution(mesh):
    in_specs = (
        P(None, "leaf"),
        P("leaf"),
        P("leaf", None, None),
        P("leaf", None, None),
        P("leaf", None),
        P("leaf", None, None, None),
        P("leaf", None),
        P("leaf"),
        P("leaf", None, None, None),
        P(),
        P(),
        P("leaf", None, None),
        P(),
    )
    return jax.shard_map(
        functools.partial(local, mesh.shape["leaf"]),
        mesh=mesh,
        in_specs=in_specs,
        out_specs=P(None, "leaf"),
        check_vma=False,
    )
```

```python
import functools

import jax
import jax.numpy as jnp
from jax import lax
from jax.experimental import pallas as pl
from jax.experimental.pallas import tpu as pltpu
from jax.sharding import PartitionSpec as P

REACH = 4
DEPTH = 4
OFFSETS = (-3, -2, 2, 3)
GROUP = 2 * REACH
LANES = 128
TILE = 8
NODES = GROUP - 1
VMEM_LIMIT = 64 * 1024 * 1024

NN = (((1,), (0,)), ((), ()))
NT = (((1,), (1,)), ((), ()))

VMEM = pl.BlockSpec(memory_space=pltpu.VMEM)
SMEM = pl.BlockSpec(memory_space=pltpu.SMEM)
HBM = pl.BlockSpec(memory_space=pltpu.HBM)
PARAMS = pltpu.CompilerParams(vmem_limit_bytes=VMEM_LIMIT)
F32 = jnp.float32
BF16 = jnp.bfloat16


def halves(x):
    high = x.astype(BF16)
    low = (x - high.astype(F32)).astype(BF16)
    return high, low


def dot_halves(a, b_high, b_low, dims):
    a_high, a_low = halves(a)
    rows = a.shape[0]
    both = lax.dot_general(
        jnp.concatenate([a_high, a_low], axis=0), b_high, dims, preferred_element_type=F32
    )
    cross = lax.dot_general(a_high, b_low, dims, preferred_element_type=F32)
    return both[:rows] + (both[rows:] + cross)


def pair_dot(a, b, w_high, w_low):
    a_high, a_low = halves(a)
    b_high, b_low = halves(b)
    rows = a.shape[0]
    both = lax.dot_general(
        jnp.concatenate([a_high, b_high, a_low, b_low], axis=0),
        w_high,
        NN,
        preferred_element_type=F32,
    )
    cross = lax.dot_general(
        jnp.concatenate([a_high, b_high], axis=0), w_low, NN, preferred_element_type=F32
    )
    total = both[: 2 * rows] + (both[2 * rows :] + cross)
    return total[:rows], total[rows:]


def dot3(a, b, dims):
    return dot_halves(a, *halves(b), dims)


def fold(x):
    return jnp.concatenate([x[:TILE], x[TILE:]], axis=1)


def beside(p, q):
    rank = p.shape[1] // 2
    left = lax.broadcasted_iota(jnp.int32, p.shape, 1) < rank
    return jnp.concatenate(
        [
            jnp.where(left, p, pltpu.roll(q, rank, 1)),
            jnp.where(left, pltpu.roll(p, rank, 1), q),
        ],
        axis=0,
    )


def row_of(tiles):
    return jnp.concatenate([beside(*tiles[k : k + 2]) for k in range(0, len(tiles), 2)], axis=1)


def lane_gather(x, high, low):
    rows, columns = x.shape
    high = jnp.broadcast_to(high, (rows, LANES))
    low = jnp.broadcast_to(low, (rows, LANES))
    result = jnp.zeros((rows, LANES), x.dtype)
    for source in range(columns // LANES):
        tile = x[:, source * LANES : (source + 1) * LANES]
        moved = jnp.take_along_axis(tile, low, axis=1, mode="promise_in_bounds")
        result = jnp.where(high == source, moved, result)
    return result


def fetch(pairs, sems):
    copies = [
        pltpu.make_async_copy(source, target, sems.at[index])
        for index, (source, target) in enumerate(pairs)
    ]
    for copy in copies:
        copy.start()
    return copies


def up_kernel(
    me_ref,
    points_hbm,
    order_hbm,
    bases_hbm,
    lift_hbm,
    out,
    x_out,
    first_out,
    last_out,
    points_v,
    order_v,
    bases_v,
    lift_v,
    sems,
):
    copies = fetch(
        [(order_hbm, order_v), (points_hbm, points_v), (bases_hbm, bases_v), (lift_hbm, lift_v)], sems
    )
    me = me_ref[0]
    leaf_dev, rank, leaf_size = bases_v.shape
    vectors, points_dev = points_v.shape
    copies[0].wait()
    copies[1].wait()
    points = points_v[...]
    per_leaf = leaf_size // LANES
    for t in range(points_dev // LANES):
        spot = order_v[t : t + 1, :] - me * points_dev
        column = t % per_leaf * LANES
        x_out[t // per_leaf, :, column : column + LANES] = lane_gather(
            points, lax.shift_right_logical(spot, 7), spot & (LANES - 1)
        )
    copies[2].wait()
    coefs = [dot3(x_out[leaf], bases_v[leaf], NT) for leaf in range(leaf_dev)]
    tiles = [fold(coef) for coef in coefs]
    copies[3].wait()
    weights = lift_v[...].reshape(leaf_dev * rank, rank)
    tiles.append(fold(dot3(jnp.concatenate(coefs, axis=1), weights, NN)))
    for peer in range(GROUP):
        for index, tile in enumerate(tiles):
            out[peer, index * TILE : (index + 1) * TILE, :] = tile
    first_out[...] = x_out[0]
    last_out[...] = x_out[leaf_dev - 1]


def near_kernel(me_ref, *refs):
    inputs, outputs = refs[:4], refs[4:9]
    held, results = refs[9:13], refs[13:18]
    product_v, total_v, sems, block_sems, out_sems = refs[18:]
    ids_s, x_v, transfer_v, blocks_v = held
    near_out, up_high, up_low, edge_high, edge_low = results
    leaf_dev, slots, leaf_size, _ = blocks_v.shape
    vectors = x_v.shape[1]
    rank = transfer_v.shape[2]
    me = me_ref[0]
    copies = fetch(list(zip(inputs[:3], held[:3])), sems)

    def block(leaf):
        return pltpu.make_async_copy(inputs[3].at[leaf], blocks_v.at[leaf], block_sems.at[leaf])

    for leaf in range(leaf_dev):
        block(leaf).start()
    for copy in copies:
        copy.wait()
    columns = leaf_dev * vectors
    x_both = jnp.concatenate(halves(x_v[...].reshape(columns, leaf_size).T), axis=1)
    chunk = 64
    owner = lax.broadcasted_iota(jnp.int32, (chunk, columns), 1) // vectors

    composed = transfer_v[0].reshape(2 * rank, rank)
    row = 0
    for level in range(1, DEPTH):
        rows = composed.shape[0]
        up_high[row : row + rows], up_low[row : row + rows] = halves(composed)
        row += rows
        if level < DEPTH - 1:
            composed = jnp.concatenate(
                [dot3(composed, transfer_v[level, side], NN) for side in range(2)], axis=0
            )
    writes = fetch([(results[k], outputs[k]) for k in (1, 2)], out_sems)

    def leaf_step(leaf, carry):
        block(leaf).wait()
        left = []
        for slot in range(slots):
            left += halves(blocks_v[leaf, slot])
        product_v[...] = lax.dot_general(
            jnp.concatenate(left, axis=0), x_both, NN, preferred_element_type=F32
        )
        local = [ids_s[slot, leaf] - me * leaf_dev for slot in range(slots)]
        for start in range(0, leaf_size, chunk):
            total = jnp.zeros((chunk, columns), F32)
            for slot in range(slots):
                high = 2 * slot * leaf_size + start
                low = high + leaf_size
                wide = product_v[high : high + chunk] + product_v[low : low + chunk]
                product = wide[:, :columns] + wide[:, columns:]
                total = total + jnp.where(owner == local[slot], product, 0.0)
            total_v[start : start + chunk] = total
        parts = total_v[...].T
        result = parts[:vectors]
        for other in range(1, leaf_dev):
            result = result + parts[other * vectors : (other + 1) * vectors]
        near_out[leaf] = result
        return carry

    lax.fori_loop(0, leaf_dev, leaf_step, 0)

    for index, leaf, outside in ((0, 0, -1), (1, leaf_dev - 1, leaf_dev)):
        total = jnp.zeros((leaf_size, leaf_size), F32)
        for slot in range(1, slots):
            remote = ids_s[slot, leaf] - me * leaf_dev == outside
            total = total + jnp.where(remote, blocks_v[leaf, slot], 0.0)
        edge_high[index], edge_low[index] = halves(total.T)
    writes += fetch([(results[k], outputs[k]) for k in (0, 3, 4)], out_sems.at[pl.ds(2, 3)])
    for copy in writes:
        copy.wait()


def weight_kernel(me_ref, *refs):
    inputs, outputs = refs[:8], refs[8:15]
    held, results = refs[15:23], refs[23:30]
    sems, out_sems = refs[30:]
    links_s, transfer_v, couple_v, top_v, lift_v, far_v, bases_v, order_v = held
    path_high, path_low, leaf_high, leaf_low, bases_high, bases_low, inverse_out = results
    copies = fetch(list(zip(inputs, held)), sems)
    me = me_ref[0]
    pairs, leaf_rows, _ = leaf_high.shape
    rank = top_v.shape[0]
    slots = far_v.shape[1]
    for copy in copies[:4]:
        copy.wait()

    path = None
    blocks = []
    for level in range(DEPTH):
        weights = [
            links_s[level, column].astype(F32) * couple_v[level, column]
            for column in range(len(OFFSETS))
        ]
        weights = jnp.concatenate(weights, axis=1)
        step = transfer_v[level, lax.shift_right_logical(me, level) & 1]
        if path is not None:
            weights = dot3(path, weights, NN)
            step = dot3(path, step, NN)
        path = step
        blocks += [weights[:, k * rank : (k + 1) * rank] for k in range(len(OFFSETS))]
    top = dot3(path, top_v[...], NN)
    blocks += [dot3(top, transfer_v[DEPTH - 1, side], NT) for side in range(2)]
    half = len(blocks) // 2
    for index in range(half):
        span = slice(index * rank, (index + 1) * rank)
        both = jnp.concatenate([blocks[index], blocks[half + index]], axis=0).T
        path_high[span], path_low[span] = halves(both)

    writes = fetch([(results[k], outputs[k]) for k in range(2)], out_sems)
    for copy in copies[4:]:
        copy.wait()

    for pair in range(pairs):
        for slot in range(slots + 1):
            two = [
                lift_v[2 * pair + k] if slot == slots else far_v[2 * pair + k, slot]
                for k in range(2)
            ]
            span = slice(slot * rank, (slot + 1) * rank)
            leaf_high[pair, span], leaf_low[pair, span] = halves(jnp.concatenate(two, axis=0).T)
        bases_high[pair], bases_low[pair] = halves(bases_v[pair])

    writes += fetch([(results[k], outputs[k]) for k in range(2, 6)], out_sems.at[pl.ds(2, 4)])

    points_dev = order_v.shape[1]
    tiles = points_dev // LANES
    spot = order_v[...] - me * points_dev
    times = lax.broadcasted_iota(jnp.int32, (1, points_dev), 1)
    shape = (tiles, points_dev)
    match = lax.broadcasted_iota(jnp.int32, shape, 0) == lax.shift_right_logical(spot, 7)
    digits = [
        jnp.where(match, jnp.broadcast_to(digit.astype(F32), shape), 0.0)
        for digit in (lax.shift_right_logical(times, 4), times & 15)
    ]
    shape = (LANES, points_dev)
    match = lax.broadcasted_iota(jnp.int32, shape, 0) == (spot & (LANES - 1))
    both = lax.dot_general(
        jnp.concatenate(digits, axis=0).astype(BF16),
        jnp.where(match, 1.0, 0.0).astype(BF16),
        NT,
        preferred_element_type=F32,
    )
    inverse_out[...] = (both[:tiles] * 16.0 + both[tiles:]).astype(jnp.int32)
    writes += fetch([(inverse_out, outputs[6])], out_sems.at[pl.ds(6, 1)])
    for copy in writes:
        copy.wait()


def middle_kernel(
    leaf_dev,
    me_ref,
    group_hbm,
    up_high_hbm,
    up_low_hbm,
    below_hbm,
    above_hbm,
    half_out,
    nodes_out,
    roots_v,
    up_high,
    up_low,
    sems,
    half_sems,
):
    del below_hbm, above_hbm
    low = lax.rem(me_ref[0], GROUP) < REACH
    copies = fetch(
        [
            (group_hbm.at[:, pl.ds(leaf_dev * TILE, TILE), :], roots_v),
            (up_high_hbm, up_high),
            (up_low_hbm, up_low),
        ],
        sems,
    )
    rows = (leaf_dev + 1) * TILE
    first = jnp.where(low, REACH, 0)
    moves = [
        (group_hbm.at[first + part, pl.ds(0, rows)], half_out.at[pl.ds(part * rows, rows)])
        for part in range(REACH)
    ]
    moves = fetch(moves, half_sems)
    for copy in copies:
        copy.wait()
    roots = [roots_v[peer] for peer in range(GROUP)]
    start, tiles = 0, []
    for level in range(1, DEPTH):
        width = 1 << level
        count = GROUP // width
        left = jnp.concatenate(
            [row_of(roots[n * width : (n + 1) * width]) for n in range(count)], axis=0
        )
        size = left.shape[1]
        nodes = dot_halves(left, up_high[start : start + size], up_low[start : start + size], NN)
        start += size
        tiles += [fold(nodes[n * 2 * TILE : (n + 1) * 2 * TILE]) for n in range(count)]
    row = REACH * rows
    for index, tile in enumerate(tiles):
        half_out[row + index * TILE : row + (index + 1) * TILE, :] = tile
        for peer in range(nodes_out.shape[0]):
            nodes_out[peer, index] = tile
    for copy in moves:
        copy.wait()


def down_kernel(parts, me_ref, *refs):
    node_parts, refs = refs[:parts], refs[parts:]
    count = (len(refs) - 5) // 2
    out_ref = refs[count]
    held = refs[count + 1 : 2 * count + 1]
    nodes_ref, y_tree, sems, node_sems = refs[2 * count + 1 :]
    me = me_ref[0]
    groups = nodes_ref.shape[0]
    group = lax.shift_right_logical(me, 3)
    place = me & (GROUP - 1)
    low = place < REACH
    half_hbm = refs[1]
    if parts > 1:
        near_by, far_by = jnp.where(low, groups - 1, 1), jnp.where(low, 1, groups - 1)
        start = half_hbm.shape[0] - NODES * TILE
        node_copies = fetch(
            [
                (part.at[0], nodes_ref.at[lax.rem(group + by, groups)])
                for part, by in zip(node_parts, (0, far_by, 2))
            ]
            + [
                (
                    half_hbm.at[pl.ds(start + index * TILE, TILE)],
                    nodes_ref.at[lax.rem(group + near_by, groups), index],
                )
                for index in range(NODES)
            ],
            node_sems,
        )
    else:
        node_copies = fetch([(node_parts[0], nodes_ref)], node_sems)
    copies = fetch(list(zip(refs[:count], held)), sems)
    (
        group_ref,
        half_ref,
        path_high,
        path_low,
        far_ids_s,
        far_count_s,
        below_ref,
        above_ref,
        edge_high,
        edge_low,
        leaf_high,
        leaf_low,
        bases_high,
        bases_low,
        near_ref,
        inverse_ref,
    ) = held
    leaf_dev, vectors, leaf_size = near_ref.shape
    points_dev = out_ref.shape[1]
    slots = far_ids_s.shape[1]
    rank = bases_high.shape[1] // 2
    start = (leaf_dev + 1) * TILE

    def tile_of(subtree, index):
        other = subtree & (GROUP - 1)
        inside = lax.shift_right_arithmetic(subtree, 3) == group
        row = pl.multiple_of(index * TILE, TILE)
        near_row = jnp.clip(other - jnp.where(low, REACH, 0), 0, REACH - 1) * start
        here = group_ref[other, pl.ds(row, TILE), :]
        there = half_ref[pl.ds(pl.multiple_of(near_row + row, TILE), TILE), :]
        return jnp.where(inside, here, there)

    for copy in node_copies + copies[:4]:
        copy.wait()
    partners = []
    for level in range(DEPTH):
        node = lax.shift_right_logical(me, level)
        size = (groups * GROUP) >> level
        for offset in OFFSETS:
            other = node + offset
            used = (other >= 0) & (other < size)
            other = jnp.clip(other, 0, size - 1)
            if level == 0:
                tile = tile_of(other, leaf_dev)
            else:
                shift = DEPTH - 1 - level
                first = GROUP - (2 << shift)
                tile = nodes_ref[
                    lax.shift_right_logical(other, shift), first + (other & ((1 << shift) - 1))
                ]
            partners.append(jnp.where(used, tile, 0.0))
    top = lax.shift_right_logical(me, DEPTH)
    for side in range(2):
        blended = jnp.zeros((TILE, LANES), F32)
        for other in range(groups // 2):
            distance = jnp.abs(top - other)
            weight = jnp.where(distance >= 2, 1.0 / jnp.maximum(distance, 1).astype(F32), 0.0)
            blended = blended + weight * nodes_ref[2 * other + side, GROUP - 2]
        partners.append(blended)
    half = len(partners) // 2
    row = row_of(partners)
    first, second = pair_dot(
        row[:, : half * rank], row[:, half * rank :], path_high[...], path_low[...]
    )
    down = first[:, :rank] + second[:, rank:]

    for copy in copies[4:10]:
        copy.wait()
    edge_parts = [
        dot_halves(edge[...], edge_high[index], edge_low[index], NN)
        for index, edge in enumerate((below_ref, above_ref))
    ]

    for copy in copies[10:]:
        copy.wait()
    left_half = lax.broadcasted_iota(jnp.int32, (vectors, 2 * rank), 1) < rank
    for pair in range(leaf_dev // 2):
        rows = []
        for leaf in (2 * pair, 2 * pair + 1):
            picked = []
            for slot in range(slots):
                used = slot < far_count_s[leaf]
                spot = far_ids_s[leaf, slot]
                tile = tile_of(lax.shift_right_logical(spot, 3), spot & (leaf_dev - 1))
                picked.append(jnp.where(used, tile, 0.0))
            rows.append(jnp.concatenate([row_of(picked), down], axis=1))
        first, second = pair_dot(*rows, leaf_high[pair], leaf_low[pair])
        first = jnp.where(left_half, first, 0.0)
        second = jnp.where(left_half, 0.0, second)
        parts = pair_dot(first, second, bases_high[pair], bases_low[pair])
        for leaf, part in zip((2 * pair, 2 * pair + 1), parts):
            y_leaf = near_ref[leaf] + part
            if leaf == 0:
                y_leaf = y_leaf + edge_parts[0]
            if leaf == leaf_dev - 1:
                y_leaf = y_leaf + edge_parts[1]
            y_tree[:, leaf * leaf_size : (leaf + 1) * leaf_size] = y_leaf

    y = y_tree[...]
    for tile in range(points_dev // LANES):
        spot = inverse_ref[tile : tile + 1, :]
        out_ref[:, tile * LANES : (tile + 1) * LANES] = lane_gather(
            y, lax.shift_right_logical(spot, 7), spot & (LANES - 1)
        )


def local(
    devices,
    points,
    order,
    bases,
    lift,
    near_ids,
    near_blocks,
    far_ids,
    far_count,
    far_blocks,
    transfer,
    couple,
    links,
    top_couple,
):
    me = lax.axis_index("leaf").astype(jnp.int32).reshape(1)
    vectors, points_dev = points.shape
    leaf_dev, leaf_size, rank = bases.shape
    slots = near_ids.shape[1]
    far_slots = far_ids.shape[1]
    bases_t = jnp.swapaxes(bases, 1, 2)
    tiles = points_dev // LANES
    rows = (leaf_dev + 1) * TILE
    groups = devices // GROUP
    order_tiles = order.reshape(tiles, LANES)
    shape = jax.ShapeDtypeStruct

    group_out, tree_x, first_leaf, last_leaf = pl.pallas_call(
        up_kernel,
        out_shape=[
            shape((GROUP, rows, LANES), F32),
            shape((leaf_dev, vectors, leaf_size), F32),
            shape((vectors, leaf_size), F32),
            shape((vectors, leaf_size), F32),
        ],
        in_specs=[SMEM] + [HBM] * 4,
        out_specs=[VMEM] * 4,
        scratch_shapes=[
            pltpu.VMEM(points.shape, F32),
            pltpu.VMEM((tiles, LANES), jnp.int32),
            pltpu.VMEM(bases_t.shape, F32),
            pltpu.VMEM(lift.shape, F32),
            pltpu.SemaphoreType.DMA((4,)),
        ],
        compiler_params=PARAMS,
        name="up",
    )(me, points, order_tiles, bases_t, lift)

    aligned = [[g * GROUP + i for i in range(GROUP)] for g in range(groups)]
    group_in = lax.all_to_all(group_out, "leaf", 0, 0, axis_index_groups=aligned, tiled=True)
    forward = [(i, i + 1) for i in range(devices - 1)]
    below = lax.ppermute(last_leaf, "leaf", forward)
    above = lax.ppermute(first_leaf, "leaf", [(target, source) for source, target in forward])

    ids_t = near_ids.T
    both = lambda *size: [shape(size, BF16)] * 2

    def call(kernel, operands, results, scalar, scratch, sems, cost, name):
        return pl.pallas_call(
            kernel,
            out_shape=results,
            in_specs=[SMEM] + [HBM] * len(operands),
            out_specs=[HBM] * len(results),
            scratch_shapes=[
                (pltpu.SMEM if x is scalar else pltpu.VMEM)(x.shape, x.dtype) for x in operands
            ]
            + [pltpu.VMEM(x.shape, x.dtype) for x in results]
            + [pltpu.VMEM(size, F32) for size in scratch]
            + [pltpu.SemaphoreType.DMA((count,)) for count in sems],
            compiler_params=PARAMS,
            cost_estimate=pl.CostEstimate(flops=cost * 250, bytes_accessed=cost, transcendentals=0),
            name=name,
        )(me, *operands)

    near_part, up_high, up_low, edge_high, edge_low = call(
        near_kernel,
        (ids_t, tree_x, transfer, near_blocks),
        [shape(tree_x.shape, F32)] + both(14 * rank, rank) + both(2, leaf_size, leaf_size),
        ids_t,
        ((2 * slots * leaf_size, 2 * leaf_dev * vectors), (leaf_size, leaf_dev * vectors)),
        (3, leaf_dev, 5),
        12_000_000,
        "near",
    )
    links_own = links.reshape(links.shape[1:])
    path_rows = (DEPTH * len(OFFSETS) + 2) // 2 * rank
    path_high, path_low, leaf_high, leaf_low, bases_high, bases_low, inverse = call(
        weight_kernel,
        (
            links_own,
            transfer,
            couple,
            top_couple,
            lift,
            far_blocks,
            bases_t.reshape(leaf_dev // 2, 2 * rank, leaf_size),
            order.reshape(1, points_dev),
        ),
        both(path_rows, 2 * rank)
        + both(leaf_dev // 2, (far_slots + 1) * rank, 2 * rank)
        + both(leaf_dev // 2, 2 * rank, leaf_size)
        + [shape((tiles, LANES), jnp.int32)],
        links_own,
        (),
        (8, 7),
        12_000_000,
        "weights",
    )

    by_permute = groups == 4
    half_out, nodes_out = pl.pallas_call(
        functools.partial(middle_kernel, leaf_dev),
        out_shape=[
            shape((REACH * rows + NODES * TILE, LANES), F32),
            shape((1 if by_permute else groups, NODES, TILE, LANES), F32),
        ],
        in_specs=[SMEM] + [HBM] * 5,
        out_specs=[VMEM] * 2,
        scratch_shapes=[
            pltpu.VMEM((GROUP, TILE, LANES), F32),
            pltpu.VMEM(up_high.shape, BF16),
            pltpu.VMEM(up_low.shape, BF16),
            pltpu.SemaphoreType.DMA((3,)),
            pltpu.SemaphoreType.DMA((REACH,)),
        ],
        compiler_params=PARAMS,
        name="middle",
    )(me, group_in, up_high, up_low, below, above)

    def shifted(x, low, high):
        pairs = []
        for device in range(devices):
            by = low if device % GROUP < REACH else high
            pairs.append(((device + by * GROUP) % devices, device))
        return lax.ppermute(x, "leaf", pairs)

    half_in = shifted(half_out, -1, 1)
    if by_permute:
        node_parts = (nodes_out, shifted(nodes_out, 1, -1), shifted(nodes_out, 2, 2))
    else:
        across = [[g * GROUP + i for g in range(groups)] for i in range(GROUP)]
        node_parts = (lax.all_to_all(nodes_out, "leaf", 0, 0, axis_index_groups=across, tiled=True),)

    operands = (
        group_in,
        half_in,
        path_high,
        path_low,
        far_ids,
        far_count,
        below,
        above,
        edge_high,
        edge_low,
        leaf_high,
        leaf_low,
        bases_high,
        bases_low,
        near_part,
        inverse,
    )
    return pl.pallas_call(
        functools.partial(down_kernel, len(node_parts)),
        out_shape=shape((vectors, points_dev), F32),
        in_specs=[SMEM] + [HBM] * (len(node_parts) + len(operands)),
        out_specs=VMEM,
        scratch_shapes=[
            (pltpu.SMEM if x is far_ids or x is far_count else pltpu.VMEM)(x.shape, x.dtype)
            for x in operands
        ]
        + [
            pltpu.VMEM((groups, NODES, TILE, LANES), F32),
            pltpu.VMEM((vectors, points_dev), F32),
            pltpu.SemaphoreType.DMA((len(operands),)),
            pltpu.SemaphoreType.DMA((len(node_parts) + NODES,)),
        ],
        compiler_params=PARAMS,
        name="down",
    )(me, *node_parts, *operands)


def solution(mesh):
    in_specs = (
        P(None, "leaf"),
        P("leaf"),
        P("leaf", None, None),
        P("leaf", None, None),
        P("leaf", None),
        P("leaf", None, None, None),
        P("leaf", None),
        P("leaf"),
        P("leaf", None, None, None),
        P(),
        P(),
        P("leaf", None, None),
        P(),
    )
    return jax.shard_map(
        functools.partial(local, mesh.shape["leaf"]),
        mesh=mesh,
        in_specs=in_specs,
        out_specs=P(None, "leaf"),
        check_vma=False,
    )
```

```python
import functools

import jax
import jax.numpy as jnp
from jax import lax
from jax.experimental import pallas as pl
from jax.experimental.pallas import tpu as pltpu
from jax.sharding import PartitionSpec as P

REACH = 4
DEPTH = 4
OFFSETS = (-3, -2, 2, 3)
GROUP = 2 * REACH
LANES = 128
TILE = 8
NODES = GROUP - 1
VMEM_LIMIT = 64 * 1024 * 1024

NN = (((1,), (0,)), ((), ()))
NT = (((1,), (1,)), ((), ()))

VMEM = pl.BlockSpec(memory_space=pltpu.VMEM)
SMEM = pl.BlockSpec(memory_space=pltpu.SMEM)
HBM = pl.BlockSpec(memory_space=pltpu.HBM)
PARAMS = pltpu.CompilerParams(vmem_limit_bytes=VMEM_LIMIT)
F32 = jnp.float32
BF16 = jnp.bfloat16


def halves(x):
    high = x.astype(BF16)
    low = (x - high.astype(F32)).astype(BF16)
    return high, low


def dot_halves(a, b_high, b_low, dims):
    a_high, a_low = halves(a)
    rows = a.shape[0]
    both = lax.dot_general(
        jnp.concatenate([a_high, a_low], axis=0), b_high, dims, preferred_element_type=F32
    )
    cross = lax.dot_general(a_high, b_low, dims, preferred_element_type=F32)
    return both[:rows] + (both[rows:] + cross)


def pair_dot(a, b, w_high, w_low):
    a_high, a_low = halves(a)
    b_high, b_low = halves(b)
    rows = a.shape[0]
    both = lax.dot_general(
        jnp.concatenate([a_high, b_high, a_low, b_low], axis=0),
        w_high,
        NN,
        preferred_element_type=F32,
    )
    cross = lax.dot_general(
        jnp.concatenate([a_high, b_high], axis=0), w_low, NN, preferred_element_type=F32
    )
    total = both[: 2 * rows] + (both[2 * rows :] + cross)
    return total[:rows], total[rows:]


def dot3(a, b, dims):
    return dot_halves(a, *halves(b), dims)


def fold(x):
    return jnp.concatenate([x[:TILE], x[TILE:]], axis=1)


def beside(p, q):
    rank = p.shape[1] // 2
    left = lax.broadcasted_iota(jnp.int32, p.shape, 1) < rank
    return jnp.concatenate(
        [
            jnp.where(left, p, pltpu.roll(q, rank, 1)),
            jnp.where(left, pltpu.roll(p, rank, 1), q),
        ],
        axis=0,
    )


def row_of(tiles):
    return jnp.concatenate([beside(*tiles[k : k + 2]) for k in range(0, len(tiles), 2)], axis=1)


def lane_gather(x, high, low):
    rows, columns = x.shape
    high = jnp.broadcast_to(high, (rows, LANES))
    low = jnp.broadcast_to(low, (rows, LANES))
    result = jnp.zeros((rows, LANES), x.dtype)
    for source in range(columns // LANES):
        tile = x[:, source * LANES : (source + 1) * LANES]
        moved = jnp.take_along_axis(tile, low, axis=1, mode="promise_in_bounds")
        result = jnp.where(high == source, moved, result)
    return result


def fetch(pairs, sems):
    copies = [
        pltpu.make_async_copy(source, target, sems.at[index])
        for index, (source, target) in enumerate(pairs)
    ]
    for copy in copies:
        copy.start()
    return copies


def up_kernel(
    me_ref, points_hbm, order_hbm, bases_hbm, lift_hbm, out, x_out, points_v, order_v, bases_v, lift_v, sems
):
    copies = fetch(
        [(order_hbm, order_v), (points_hbm, points_v), (bases_hbm, bases_v), (lift_hbm, lift_v)], sems
    )
    me = me_ref[0]
    leaf_dev, rank, leaf_size = bases_v.shape
    vectors, points_dev = points_v.shape
    copies[0].wait()
    copies[1].wait()
    points = points_v[...]
    per_leaf = leaf_size // LANES
    for t in range(points_dev // LANES):
        spot = order_v[t : t + 1, :] - me * points_dev
        column = t % per_leaf * LANES
        x_out[t // per_leaf, :, column : column + LANES] = lane_gather(
            points, lax.shift_right_logical(spot, 7), spot & (LANES - 1)
        )
    copies[2].wait()
    coefs = [dot3(x_out[leaf], bases_v[leaf], NT) for leaf in range(leaf_dev)]
    tiles = [fold(coef) for coef in coefs]
    copies[3].wait()
    weights = lift_v[...].reshape(leaf_dev * rank, rank)
    tiles.append(fold(dot3(jnp.concatenate(coefs, axis=1), weights, NN)))
    for peer in range(GROUP):
        for index, tile in enumerate(tiles):
            out[peer, index * TILE : (index + 1) * TILE, :] = tile
    place = lax.rem(me, GROUP)
    start = len(tiles) * TILE
    for part in range(per_leaf):
        first = x_out[0, :, part * LANES : (part + 1) * LANES]
        last = x_out[leaf_dev - 1, :, part * LANES : (part + 1) * LANES]
        rows = slice(start + part * vectors, start + (part + 1) * vectors)
        for peer in range(GROUP):
            above = lax.rem(place + 1, GROUP) == peer
            out[peer, rows, :] = jnp.where(above, last, first)


def near_kernel(me_ref, *refs):
    inputs, outputs = refs[:4], refs[4:9]
    held, results = refs[9:13], refs[13:18]
    product_v, total_v, sems, block_sems, out_sems = refs[18:]
    ids_s, x_v, transfer_v, blocks_v = held
    near_out, up_high, up_low, edge_high, edge_low = results
    leaf_dev, slots, leaf_size, _ = blocks_v.shape
    vectors = x_v.shape[1]
    rank = transfer_v.shape[2]
    me = me_ref[0]
    copies = fetch(list(zip(inputs[:3], held[:3])), sems)

    def block(leaf):
        return pltpu.make_async_copy(inputs[3].at[leaf], blocks_v.at[leaf], block_sems.at[leaf])

    for leaf in (0, leaf_dev - 1, *range(1, leaf_dev - 1)):
        block(leaf).start()
    for copy in copies:
        copy.wait()
    columns = leaf_dev * vectors
    x_both = jnp.concatenate(halves(x_v[...].reshape(columns, leaf_size).T), axis=1)
    chunk = 64
    owner = lax.broadcasted_iota(jnp.int32, (chunk, columns), 1) // vectors

    x_both = jnp.concatenate([x_both, x_both], axis=0)
    writes = []

    def write(index):
        writes.extend(fetch([(results[index], outputs[index])], out_sems.at[pl.ds(index, 1)]))

    def node_weights():
        composed = transfer_v[0].reshape(2 * rank, rank)
        row = 0
        for level in range(1, DEPTH):
            rows = composed.shape[0]
            up_high[row : row + rows], up_low[row : row + rows] = halves(composed)
            row += rows
            if level < DEPTH - 1:
                yield
                composed = jnp.concatenate(
                    [dot3(composed, transfer_v[level, side], NN) for side in range(2)], axis=0
                )
        write(1)
        write(2)

    def edge(index, leaf, outside):
        total = jnp.zeros((leaf_size, leaf_size), F32)
        for slot in range(1, slots):
            remote = ids_s[slot, leaf] - me * leaf_dev == outside
            total = total + jnp.where(remote, blocks_v[leaf, slot], 0.0)
        edge_high[index], edge_low[index] = halves(total.T)

    def near(leaf):
        left = jnp.concatenate(
            [jnp.concatenate(halves(blocks_v[leaf, slot]), axis=1) for slot in range(slots)], axis=0
        )
        product_v[...] = lax.dot_general(left, x_both, NN, preferred_element_type=F32)
        local = [ids_s[slot, leaf] - me * leaf_dev for slot in range(slots)]
        for start in range(0, leaf_size, chunk):
            total = jnp.zeros((chunk, columns), F32)
            for slot in range(slots):
                first = slot * leaf_size + start
                wide = product_v[first : first + chunk]
                product = wide[:, :columns] + wide[:, columns:]
                total = total + jnp.where(owner == local[slot], product, 0.0)
            total_v[start : start + chunk] = total
        parts = total_v[...].T
        result = parts[:vectors]
        for other in range(1, leaf_dev):
            result = result + parts[other * vectors : (other + 1) * vectors]
        near_out[leaf] = result

    links = node_weights()
    next(links)
    block(0).wait()
    near(0)
    edge(0, 0, -1)
    next(links)
    block(leaf_dev - 1).wait()
    near(leaf_dev - 1)
    edge(1, leaf_dev - 1, leaf_dev)
    next(links, None)
    write(3)
    write(4)

    def leaf_step(leaf, carry):
        block(leaf).wait()
        near(leaf)
        return carry

    lax.fori_loop(1, leaf_dev - 1, leaf_step, 0)
    write(0)
    for copy in writes:
        copy.wait()


def weight_kernel(me_ref, *refs):
    inputs, outputs = refs[:8], refs[8:17]
    held, results = refs[8 + 9 : 8 + 9 + 8], refs[25:34]
    sems, pair_sems, out_sems = refs[34:]
    links_s, transfer_v, couple_v, top_v, order_v, lift_v, far_v, bases_v = held
    path_high, path_low, leaf_high, leaf_low, lift_high, lift_low = results[:6]
    bases_high, bases_low, inverse_out = results[6:]
    copies = fetch(list(zip(inputs[:6], held[:6])), sems)
    me = me_ref[0]
    pairs, leaf_rows, _ = leaf_high.shape
    rank = top_v.shape[0]
    slots = far_v.shape[1]
    pair_copies = [
        fetch(
            [
                (inputs[6].at[pl.ds(2 * pair, 2)], far_v.at[pl.ds(2 * pair, 2)]),
                (inputs[7].at[pair], bases_v.at[pair]),
            ],
            pair_sems.at[pair],
        )
        for pair in range(pairs)
    ]
    writes = []

    def write(*indices):
        for index in indices:
            writes.extend(fetch([(results[index], outputs[index])], out_sems.at[pl.ds(index, 1)]))

    def couplings(level):
        weights = [
            links_s[level, column].astype(F32) * couple_v[level, column]
            for column in range(len(OFFSETS))
        ]
        return jnp.concatenate(weights, axis=1)

    def chain():
        bits = [lax.shift_right_logical(me, level) & 1 for level in range(DEPTH)]
        path = transfer_v[0, bits[0]]
        blocks = [couplings(0)]
        for level in range(1, DEPTH):
            blocks.append(dot3(path, couplings(level), NN))
            path = dot3(path, transfer_v[level, bits[level]], NN)
            yield
        top = dot3(path, top_v[...], NN)
        yield
        blocks = [x[:, k * rank : (k + 1) * rank] for x in blocks for k in range(len(OFFSETS))]
        blocks += [dot3(top, transfer_v[DEPTH - 1, side], NT) for side in range(2)]
        half = len(blocks) // 2
        for index in range(half):
            span = slice(index * rank, (index + 1) * rank)
            both = jnp.concatenate([blocks[index], blocks[half + index]], axis=0).T
            path_high[span], path_low[span] = halves(both)

    def inverse():
        points_dev = order_v.shape[1]
        tiles = points_dev // LANES
        spot = order_v[...] - me * points_dev
        times = lax.broadcasted_iota(jnp.int32, (1, points_dev), 1)
        shape = (tiles, points_dev)
        match = lax.broadcasted_iota(jnp.int32, shape, 0) == lax.shift_right_logical(spot, 7)
        digits = [
            jnp.where(match, jnp.broadcast_to(digit.astype(F32), shape), 0.0)
            for digit in (lax.shift_right_logical(times, 4), times & 15)
        ]
        shape = (LANES, points_dev)
        match = lax.broadcasted_iota(jnp.int32, shape, 0) == (spot & (LANES - 1))
        both = lax.dot_general(
            jnp.concatenate(digits, axis=0).astype(BF16),
            jnp.where(match, 1.0, 0.0).astype(BF16),
            NT,
            preferred_element_type=F32,
        )
        inverse_out[...] = (both[:tiles] * 16.0 + both[tiles:]).astype(jnp.int32)

    for copy in copies:
        copy.wait()
    links = chain()
    next(links)
    inverse()
    for pair in range(pairs):
        for copy in pair_copies[pair]:
            copy.wait()
        next(links, None)
        two = range(2 * pair, 2 * pair + 2)
        for slot in range(slots):
            span = slice(slot * rank, (slot + 1) * rank)
            both = jnp.concatenate([far_v[leaf, slot] for leaf in two], axis=0).T
            leaf_high[pair, span], leaf_low[pair, span] = halves(both)
        span = slice(pair * 2 * rank, (pair + 1) * 2 * rank)
        both = jnp.concatenate([lift_v[leaf] for leaf in two], axis=0).T
        lift_high[:, span], lift_low[:, span] = halves(both)
        bases_high[pair], bases_low[pair] = halves(bases_v[pair])
    for _ in links:
        pass
    write(*range(9))
    for copy in writes:
        copy.wait()


def middle_kernel(
    leaf_dev,
    me_ref,
    group_hbm,
    up_high_hbm,
    up_low_hbm,
    half_out,
    nodes_out,
    far_out,
    last_out,
    roots_v,
    up_high,
    up_low,
    sems,
    half_sems,
):
    low = lax.rem(me_ref[0], GROUP) < REACH
    copies = fetch(
        [
            (group_hbm.at[:, pl.ds(leaf_dev * TILE, TILE), :], roots_v),
            (up_high_hbm, up_high),
            (up_low_hbm, up_low),
        ],
        sems,
    )
    rows = (leaf_dev + 1) * TILE
    edge_rows = group_hbm.shape[1] - rows
    first = jnp.where(low, REACH, 0)
    moves = [
        (group_hbm.at[first + part, pl.ds(0, rows)], half_out.at[pl.ds(part * rows, rows)])
        for part in range(REACH)
    ]
    moves.append(
        (
            group_hbm.at[jnp.where(low, GROUP - 1, 0), pl.ds(rows, edge_rows)],
            half_out.at[pl.ds(REACH * rows, edge_rows)],
        )
    )
    moves = fetch(moves, half_sems)
    for copy in copies:
        copy.wait()
    roots = [roots_v[peer] for peer in range(GROUP)]
    start, tiles = 0, []
    for level in range(1, DEPTH):
        width = 1 << level
        count = GROUP // width
        left = jnp.concatenate(
            [row_of(roots[n * width : (n + 1) * width]) for n in range(count)], axis=0
        )
        size = left.shape[1]
        nodes = dot_halves(left, up_high[start : start + size], up_low[start : start + size], NN)
        start += size
        tiles += [fold(nodes[n * 2 * TILE : (n + 1) * 2 * TILE]) for n in range(count)]
    row = REACH * rows + edge_rows
    for index, tile in enumerate(tiles):
        half_out[row + index * TILE : row + (index + 1) * TILE, :] = tile
        for peer in range(nodes_out.shape[0]):
            nodes_out[peer, index] = tile
    for index in range(3):
        far_out[index] = tiles[NODES - 3 + index]
    last_out[0] = tiles[-1]
    for copy in moves:
        copy.wait()


def down_kernel(parts, me_ref, *refs):
    node_parts, refs = refs[:parts], refs[parts:]
    count = (len(refs) - 6) // 2
    out_ref = refs[count]
    held = refs[count + 1 : 2 * count + 1]
    nodes_ref, end_v, y_tree, sems, node_sems = refs[2 * count + 1 :]
    me = me_ref[0]
    groups = nodes_ref.shape[0]
    group = lax.shift_right_logical(me, 3)
    place = me & (GROUP - 1)
    low = place < REACH
    if parts > 1:
        near_by, far_by = jnp.where(low, groups - 1, 1), jnp.where(low, 1, groups - 1)
        across = lax.rem(group + 2, groups)
        near_group = lax.rem(group + near_by, groups)
        ends = group == jnp.where(low, 0, groups - 1)
        node_copies = fetch(
            [
                (node_parts[0].at[0], nodes_ref.at[group]),
                (node_parts[1].at[0], nodes_ref.at[lax.rem(group + far_by, groups)]),
                (node_parts[2], nodes_ref.at[across, pl.ds(NODES - 3, 3)]),
                (node_parts[3], end_v),
            ],
            node_sems,
        )
    else:
        node_copies = fetch([(node_parts[0], nodes_ref)], node_sems)
    copies = fetch(list(zip(refs[:count], held)), sems)
    (
        group_ref,
        half_ref,
        far_ids_s,
        far_count_s,
        path_high,
        path_low,
        leaf_high,
        leaf_low,
        lift_high,
        lift_low,
        edge_high,
        edge_low,
        bases_high,
        bases_low,
        near_ref,
        inverse_ref,
    ) = held
    leaf_dev, vectors, leaf_size = near_ref.shape
    points_dev = out_ref.shape[1]
    slots = far_ids_s.shape[1]
    per_leaf = leaf_size // LANES
    rank = bases_high.shape[1] // 2
    start = (leaf_dev + 1) * TILE
    edge_rows = group_ref.shape[1] - start

    def tile_of(subtree, index):
        other = subtree & (GROUP - 1)
        inside = lax.shift_right_arithmetic(subtree, 3) == group
        row = pl.multiple_of(index * TILE, TILE)
        near_row = jnp.clip(other - jnp.where(low, REACH, 0), 0, REACH - 1) * start
        here = group_ref[other, pl.ds(row, TILE), :]
        there = half_ref[pl.ds(pl.multiple_of(near_row + row, TILE), TILE), :]
        return jnp.where(inside, here, there)

    for copy in node_copies + copies[:6]:
        copy.wait()
    if parts > 1:
        for index in range(NODES):
            row = half_ref.shape[0] - (NODES - index) * TILE
            tile = half_ref[row : row + TILE, :]
            if index == NODES - 1:
                tile = jnp.where(ends, end_v[0], tile)
            nodes_ref[near_group, index] = tile
    partners = []
    for level in range(DEPTH):
        node = lax.shift_right_logical(me, level)
        size = (groups * GROUP) >> level
        for offset in OFFSETS:
            other = node + offset
            used = (other >= 0) & (other < size)
            other = jnp.clip(other, 0, size - 1)
            if level == 0:
                tile = tile_of(other, leaf_dev)
            else:
                shift = DEPTH - 1 - level
                first = GROUP - (2 << shift)
                tile = nodes_ref[
                    lax.shift_right_logical(other, shift), first + (other & ((1 << shift) - 1))
                ]
            partners.append(jnp.where(used, tile, 0.0))
    top = lax.shift_right_logical(me, DEPTH)
    for side in range(2):
        blended = jnp.zeros((TILE, LANES), F32)
        for other in range(groups // 2):
            distance = jnp.abs(top - other)
            weight = jnp.where(distance >= 2, 1.0 / jnp.maximum(distance, 1).astype(F32), 0.0)
            blended = blended + weight * nodes_ref[2 * other + side, GROUP - 2]
        partners.append(blended)
    half = len(partners) // 2
    row = row_of(partners)
    first, second = pair_dot(
        row[:, : half * rank], row[:, half * rank :], path_high[...], path_low[...]
    )
    down = first[:, :rank] + second[:, rank:]

    rows = []
    for leaf in range(leaf_dev):
        picked = []
        for slot in range(slots):
            used = slot < far_count_s[leaf]
            spot = far_ids_s[leaf, slot]
            tile = tile_of(lax.shift_right_logical(spot, 3), spot & (leaf_dev - 1))
            picked.append(jnp.where(used, tile, 0.0))
        rows.append(row_of(picked))
    edges = []
    for offset in (-1, 1):
        other = me + offset
        inside = lax.shift_right_arithmetic(other, 3) == group
        here = group_ref[other & (GROUP - 1), start:, :]
        chosen = jnp.where(inside, here, half_ref[REACH * start : REACH * start + edge_rows, :])
        edges.append(
            jnp.concatenate(
                [chosen[part * vectors : (part + 1) * vectors] for part in range(per_leaf)], axis=1
            )
        )

    for copy in copies[6:]:
        copy.wait()
    edge_parts = [
        dot_halves(edges[index], edge_high[index], edge_low[index], NN) for index in range(2)
    ]
    lifted = dot_halves(down, lift_high[...], lift_low[...], NN)
    left_half = lax.broadcasted_iota(jnp.int32, (vectors, 2 * rank), 1) < rank
    for pair in range(leaf_dev // 2):
        two = (2 * pair, 2 * pair + 1)
        first, second = pair_dot(rows[two[0]], rows[two[1]], leaf_high[pair], leaf_low[pair])
        lift = lifted[:, two[0] * rank : (two[1] + 1) * rank]
        first = jnp.where(left_half, first + lift, 0.0)
        second = jnp.where(left_half, 0.0, second + lift)
        products = pair_dot(first, second, bases_high[pair], bases_low[pair])
        for leaf, product in zip(two, products):
            y_leaf = near_ref[leaf] + product
            if leaf == 0:
                y_leaf = y_leaf + edge_parts[0]
            if leaf == leaf_dev - 1:
                y_leaf = y_leaf + edge_parts[1]
            y_tree[:, leaf * leaf_size : (leaf + 1) * leaf_size] = y_leaf

    y = y_tree[...]
    for tile in range(points_dev // LANES):
        spot = inverse_ref[tile : tile + 1, :]
        out_ref[:, tile * LANES : (tile + 1) * LANES] = lane_gather(
            y, lax.shift_right_logical(spot, 7), spot & (LANES - 1)
        )


def local(
    devices,
    points,
    order,
    bases,
    lift,
    near_ids,
    near_blocks,
    far_ids,
    far_count,
    far_blocks,
    transfer,
    couple,
    links,
    top_couple,
):
    me = lax.axis_index("leaf").astype(jnp.int32).reshape(1)
    vectors, points_dev = points.shape
    leaf_dev, leaf_size, rank = bases.shape
    slots = near_ids.shape[1]
    far_slots = far_ids.shape[1]
    bases_t = jnp.swapaxes(bases, 1, 2)
    tiles = points_dev // LANES
    edge_rows = vectors * (leaf_size // LANES)
    rows = (leaf_dev + 1) * TILE
    groups = devices // GROUP
    order_tiles = order.reshape(tiles, LANES)
    shape = jax.ShapeDtypeStruct

    group_out, tree_x = pl.pallas_call(
        up_kernel,
        out_shape=[
            shape((GROUP, rows + edge_rows, LANES), F32),
            shape((leaf_dev, vectors, leaf_size), F32),
        ],
        in_specs=[SMEM] + [HBM] * 4,
        out_specs=[VMEM] * 2,
        scratch_shapes=[
            pltpu.VMEM(points.shape, F32),
            pltpu.VMEM((tiles, LANES), jnp.int32),
            pltpu.VMEM(bases_t.shape, F32),
            pltpu.VMEM(lift.shape, F32),
            pltpu.SemaphoreType.DMA((4,)),
        ],
        compiler_params=PARAMS,
        name="up",
    )(me, points, order_tiles, bases_t, lift)

    aligned = [[g * GROUP + i for i in range(GROUP)] for g in range(groups)]
    group_in = lax.all_to_all(group_out, "leaf", 0, 0, axis_index_groups=aligned, tiled=True)

    ids_t = near_ids.T
    both = lambda *size: [shape(size, BF16)] * 2

    def call(kernel, operands, results, scalar, scratch, sems, cost, name):
        return pl.pallas_call(
            kernel,
            out_shape=results,
            in_specs=[SMEM] + [HBM] * len(operands),
            out_specs=[HBM] * len(results),
            scratch_shapes=[
                (pltpu.SMEM if x is scalar else pltpu.VMEM)(x.shape, x.dtype) for x in operands
            ]
            + [pltpu.VMEM(x.shape, x.dtype) for x in results]
            + [pltpu.VMEM(size, F32) for size in scratch]
            + [pltpu.SemaphoreType.DMA(size) for size in sems],
            compiler_params=PARAMS,
            cost_estimate=pl.CostEstimate(flops=cost * 250, bytes_accessed=cost, transcendentals=0),
            name=name,
        )(me, *operands)

    near_part, up_high, up_low, edge_high, edge_low = call(
        near_kernel,
        (ids_t, tree_x, transfer, near_blocks),
        [shape(tree_x.shape, F32)] + both(14 * rank, rank) + both(2, leaf_size, leaf_size),
        ids_t,
        ((slots * leaf_size, 2 * leaf_dev * vectors), (leaf_size, leaf_dev * vectors)),
        ((3,), (leaf_dev,), (5,)),
        12_000_000,
        "near",
    )
    links_own = links.reshape(links.shape[1:])
    path_rows = (DEPTH * len(OFFSETS) + 2) // 2 * rank
    (
        path_high,
        path_low,
        leaf_high,
        leaf_low,
        lift_high,
        lift_low,
        bases_high,
        bases_low,
        inverse,
    ) = call(
        weight_kernel,
        (
            links_own,
            transfer,
            couple,
            top_couple,
            order.reshape(1, points_dev),
            lift,
            far_blocks,
            bases_t.reshape(leaf_dev // 2, 2 * rank, leaf_size),
        ),
        both(path_rows, 2 * rank)
        + both(leaf_dev // 2, far_slots * rank, 2 * rank)
        + both(rank, leaf_dev * rank)
        + both(leaf_dev // 2, 2 * rank, leaf_size)
        + [shape((tiles, LANES), jnp.int32)],
        links_own,
        (),
        ((6,), (leaf_dev // 2, 2), (9,)),
        1000,
        "weights",
    )

    by_permute = groups == 4
    half_out, nodes_out, far_nodes, last_node = pl.pallas_call(
        functools.partial(middle_kernel, leaf_dev),
        out_shape=[
            shape((REACH * rows + edge_rows + NODES * TILE, LANES), F32),
            shape((1 if by_permute else groups, NODES, TILE, LANES), F32),
            shape((3, TILE, LANES), F32),
            shape((1, TILE, LANES), F32),
        ],
        in_specs=[SMEM] + [HBM] * 3,
        out_specs=[VMEM] * 4,
        scratch_shapes=[
            pltpu.VMEM((GROUP, TILE, LANES), F32),
            pltpu.VMEM(up_high.shape, BF16),
            pltpu.VMEM(up_low.shape, BF16),
            pltpu.SemaphoreType.DMA((3,)),
            pltpu.SemaphoreType.DMA((REACH + 1,)),
        ],
        compiler_params=PARAMS,
        name="middle",
    )(me, group_in, up_high, up_low)

    def shifted(x, low, high, wrap):
        pairs = []
        for device in range(devices):
            by = low if device % GROUP < REACH else high
            source = device + by * GROUP
            outside = not 0 <= source < devices
            if outside == (wrap == "only") or wrap == "too":
                pairs.append((source % devices, device))
        return lax.ppermute(x, "leaf", pairs)

    half_in = shifted(half_out, -1, 1, "not")
    if by_permute:
        node_parts = (
            nodes_out,
            shifted(nodes_out, 1, -1, "too"),
            shifted(far_nodes, 2, 2, "too"),
            shifted(last_node, -1, 1, "only"),
        )
    else:
        across = [[g * GROUP + i for g in range(groups)] for i in range(GROUP)]
        node_parts = (lax.all_to_all(nodes_out, "leaf", 0, 0, axis_index_groups=across, tiled=True),)

    operands = (
        group_in,
        half_in,
        far_ids,
        far_count,
        path_high,
        path_low,
        leaf_high,
        leaf_low,
        lift_high,
        lift_low,
        edge_high,
        edge_low,
        bases_high,
        bases_low,
        near_part,
        inverse,
    )
    return pl.pallas_call(
        functools.partial(down_kernel, len(node_parts)),
        out_shape=shape((vectors, points_dev), F32),
        in_specs=[SMEM] + [HBM] * (len(node_parts) + len(operands)),
        out_specs=VMEM,
        scratch_shapes=[
            (pltpu.SMEM if x is far_ids or x is far_count else pltpu.VMEM)(x.shape, x.dtype)
            for x in operands
        ]
        + [
            pltpu.VMEM((groups, NODES, TILE, LANES), F32),
            pltpu.VMEM((1, TILE, LANES), F32),
            pltpu.VMEM((vectors, points_dev), F32),
            pltpu.SemaphoreType.DMA((len(operands),)),
            pltpu.SemaphoreType.DMA((4,)),
        ],
        compiler_params=PARAMS,
        name="down",
    )(me, *node_parts, *operands)


def solution(mesh):
    in_specs = (
        P(None, "leaf"),
        P("leaf"),
        P("leaf", None, None),
        P("leaf", None, None),
        P("leaf", None),
        P("leaf", None, None, None),
        P("leaf", None),
        P("leaf"),
        P("leaf", None, None, None),
        P(),
        P(),
        P("leaf", None, None),
        P(),
    )
    return jax.shard_map(
        functools.partial(local, mesh.shape["leaf"]),
        mesh=mesh,
        in_specs=in_specs,
        out_specs=P(None, "leaf"),
        check_vma=False,
    )
```

```python
import functools

import jax
import jax.numpy as jnp
from jax import lax
from jax.experimental import pallas as pl
from jax.experimental.pallas import tpu as pltpu
from jax.sharding import PartitionSpec as P

REACH = 4
DEPTH = 4
OFFSETS = (-3, -2, 2, 3)
GROUP = 2 * REACH
LANES = 128
TILE = 8
NODES = GROUP - 1
VMEM_LIMIT = 64 * 1024 * 1024

NN = (((1,), (0,)), ((), ()))
NT = (((1,), (1,)), ((), ()))

VMEM = pl.BlockSpec(memory_space=pltpu.VMEM)
SMEM = pl.BlockSpec(memory_space=pltpu.SMEM)
HBM = pl.BlockSpec(memory_space=pltpu.HBM)
PARAMS = pltpu.CompilerParams(vmem_limit_bytes=VMEM_LIMIT)
F32 = jnp.float32
BF16 = jnp.bfloat16


def halves(x):
    high = x.astype(BF16)
    low = (x - high.astype(F32)).astype(BF16)
    return high, low


def dot_halves(a, b_high, b_low, dims):
    a_high, a_low = halves(a)
    rows = a.shape[0]
    both = lax.dot_general(
        jnp.concatenate([a_high, a_low], axis=0), b_high, dims, preferred_element_type=F32
    )
    cross = lax.dot_general(a_high, b_low, dims, preferred_element_type=F32)
    return both[:rows] + (both[rows:] + cross)


def pair_dot(a, b, w_high, w_low):
    a_high, a_low = halves(a)
    b_high, b_low = halves(b)
    rows = a.shape[0]
    both = lax.dot_general(
        jnp.concatenate([a_high, b_high, a_low, b_low], axis=0),
        w_high,
        NN,
        preferred_element_type=F32,
    )
    cross = lax.dot_general(
        jnp.concatenate([a_high, b_high], axis=0), w_low, NN, preferred_element_type=F32
    )
    total = both[: 2 * rows] + (both[2 * rows :] + cross)
    return total[:rows], total[rows:]


def dot3(a, b, dims):
    return dot_halves(a, *halves(b), dims)


def fold(x):
    return jnp.concatenate([x[:TILE], x[TILE:]], axis=1)


def beside(p, q):
    rank = p.shape[1] // 2
    left = lax.broadcasted_iota(jnp.int32, p.shape, 1) < rank
    return jnp.concatenate(
        [
            jnp.where(left, p, pltpu.roll(q, rank, 1)),
            jnp.where(left, pltpu.roll(p, rank, 1), q),
        ],
        axis=0,
    )


def row_of(tiles):
    return jnp.concatenate([beside(*tiles[k : k + 2]) for k in range(0, len(tiles), 2)], axis=1)


def lane_gather(x_ref, high, low):
    rows, columns = x_ref.shape[-2:]
    high = jnp.broadcast_to(high, (rows, LANES))
    low = jnp.broadcast_to(low, (rows, LANES))
    result = jnp.zeros((rows, LANES), x_ref.dtype)
    for source in range(x_ref.size // (rows * LANES)):
        leaf, part = divmod(source * LANES, columns)
        span = slice(part, part + LANES)
        tile = x_ref[:, span] if len(x_ref.shape) == 2 else x_ref[leaf, :, span]
        moved = jnp.take_along_axis(tile, low, axis=1, mode="promise_in_bounds")
        result = jnp.where(high == source, moved, result)
    return result


def fetch(pairs, sems):
    copies = [
        pltpu.make_async_copy(source, target, sems.at[index])
        for index, (source, target) in enumerate(pairs)
    ]
    for copy in copies:
        copy.start()
    return copies


def up_kernel(
    me_ref, points_hbm, order_hbm, bases_hbm, lift_hbm, out, x_out, points_v, order_v, bases_v, lift_v, sems
):
    copies = fetch(
        [(order_hbm, order_v), (points_hbm, points_v), (bases_hbm, bases_v), (lift_hbm, lift_v)], sems
    )
    me = me_ref[0]
    leaf_dev, rank, leaf_size = bases_v.shape
    vectors, points_dev = points_v.shape
    copies[0].wait()
    copies[1].wait()
    per_leaf = leaf_size // LANES
    copies[2].wait()
    copies[3].wait()

    def leaf_step(leaf, root):
        parts = []
        for part in range(per_leaf):
            spot = order_v[pl.ds(leaf * per_leaf + part, 1), :] - me * points_dev
            parts.append(
                lane_gather(points_v, lax.shift_right_logical(spot, 7), spot & (LANES - 1))
            )
        x_leaf = jnp.concatenate(parts, axis=1)
        x_out[leaf] = x_leaf
        coef = dot3(x_leaf, bases_v[leaf], NT)
        tile = fold(coef)
        for peer in range(GROUP):
            out[peer, pl.ds(pl.multiple_of(leaf * TILE, TILE), TILE), :] = tile
        return root + dot3(coef, lift_v[leaf], NN)

    root = lax.fori_loop(0, leaf_dev, leaf_step, jnp.zeros((vectors, rank), F32))
    start = leaf_dev * TILE
    for peer in range(GROUP):
        out[peer, start : start + TILE, :] = fold(root)
    start += TILE
    place = lax.rem(me, GROUP)
    for part in range(per_leaf):
        first = x_out[0, :, part * LANES : (part + 1) * LANES]
        last = x_out[leaf_dev - 1, :, part * LANES : (part + 1) * LANES]
        rows = slice(start + part * vectors, start + (part + 1) * vectors)
        for peer in range(GROUP):
            above = lax.rem(place + 1, GROUP) == peer
            out[peer, rows, :] = jnp.where(above, last, first)


def near_kernel(me_ref, *refs):
    inputs, outputs = refs[:4], refs[4:9]
    held, results = refs[9:13], refs[13:18]
    product_v, total_v, sems, block_sems, out_sems = refs[18:]
    ids_s, x_v, transfer_v, blocks_v = held
    near_out, up_high, up_low, edge_high, edge_low = results
    leaf_dev, slots, leaf_size, _ = blocks_v.shape
    vectors = x_v.shape[1]
    rank = transfer_v.shape[2]
    me = me_ref[0]
    copies = fetch(list(zip(inputs[:3], held[:3])), sems)

    def block(leaf):
        return pltpu.make_async_copy(inputs[3].at[leaf], blocks_v.at[leaf], block_sems.at[leaf])

    for leaf in range(leaf_dev):
        block(leaf).start()
    for copy in copies:
        copy.wait()
    columns = leaf_dev * vectors
    x_both = jnp.concatenate(halves(x_v[...].reshape(columns, leaf_size).T), axis=1)
    chunk = 64
    owner = lax.broadcasted_iota(jnp.int32, (chunk, columns), 1) // vectors

    x_both = jnp.concatenate([x_both, x_both], axis=0)
    writes = []

    def write(index):
        writes.extend(fetch([(results[index], outputs[index])], out_sems.at[pl.ds(index, 1)]))

    def node_weights():
        composed = transfer_v[0].reshape(2 * rank, rank)
        row = 0
        for level in range(1, DEPTH):
            rows = composed.shape[0]
            up_high[row : row + rows], up_low[row : row + rows] = halves(composed)
            row += rows
            if level < DEPTH - 1:
                yield
                composed = jnp.concatenate(
                    [dot3(composed, transfer_v[level, side], NN) for side in range(2)], axis=0
                )
        write(1)
        write(2)

    def edge(index, leaf, outside):
        total = jnp.zeros((leaf_size, leaf_size), F32)
        for slot in range(1, slots):
            remote = ids_s[slot, leaf] - me * leaf_dev == outside
            total = total + jnp.where(remote, blocks_v[leaf, slot], 0.0)
        edge_high[index], edge_low[index] = halves(total.T)

    def near(leaf):
        left = jnp.concatenate(
            [jnp.concatenate(halves(blocks_v[leaf, slot]), axis=1) for slot in range(slots)], axis=0
        )
        product_v[...] = lax.dot_general(left, x_both, NN, preferred_element_type=F32)
        local = [ids_s[slot, leaf] - me * leaf_dev for slot in range(slots)]
        for start in range(0, leaf_size, chunk):
            total = jnp.zeros((chunk, columns), F32)
            for slot in range(slots):
                first = slot * leaf_size + start
                wide = product_v[first : first + chunk]
                product = wide[:, :columns] + wide[:, columns:]
                total = total + jnp.where(owner == local[slot], product, 0.0)
            total_v[start : start + chunk] = total
        parts = total_v[...].T
        result = parts[:vectors]
        for other in range(1, leaf_dev):
            result = result + parts[other * vectors : (other + 1) * vectors]
        near_out[leaf] = result

    for _ in node_weights():
        pass

    def leaf_step(leaf, carry):
        block(leaf).wait()
        near(leaf)
        return carry

    lax.fori_loop(0, leaf_dev, leaf_step, 0)

    def edge_step(index, carry):
        edge(index, index * (leaf_dev - 1), index * (leaf_dev + 1) - 1)
        return carry

    lax.fori_loop(0, 2, edge_step, 0)
    for index in (0, 3, 4):
        write(index)
    for copy in writes:
        copy.wait()


def weight_kernel(me_ref, *refs):
    inputs, outputs = refs[:8], refs[8:17]
    held, results = refs[8 + 9 : 8 + 9 + 8], refs[25:34]
    sems, pair_sems, out_sems = refs[34:]
    links_s, transfer_v, couple_v, top_v, order_v, lift_v, far_v, bases_v = held
    path_high, path_low, leaf_high, leaf_low, lift_high, lift_low = results[:6]
    bases_high, bases_low, inverse_out = results[6:]
    copies = fetch(list(zip(inputs[:6], held[:6])), sems)
    me = me_ref[0]
    pairs, leaf_rows, _ = leaf_high.shape
    rank = top_v.shape[0]
    slots = far_v.shape[1]
    pair_copies = fetch(list(zip(inputs[6:], held[6:])), pair_sems)
    writes = []

    def write(*indices):
        for index in indices:
            writes.extend(fetch([(results[index], outputs[index])], out_sems.at[pl.ds(index, 1)]))

    def couplings(level):
        weights = [
            links_s[level, column].astype(F32) * couple_v[level, column]
            for column in range(len(OFFSETS))
        ]
        return jnp.concatenate(weights, axis=1)

    def chain():
        bits = [lax.shift_right_logical(me, level) & 1 for level in range(DEPTH)]
        path = transfer_v[0, bits[0]]
        blocks = [couplings(0)]
        for level in range(1, DEPTH):
            blocks.append(dot3(path, couplings(level), NN))
            path = dot3(path, transfer_v[level, bits[level]], NN)
            yield
        top = dot3(path, top_v[...], NN)
        yield
        blocks = [x[:, k * rank : (k + 1) * rank] for x in blocks for k in range(len(OFFSETS))]
        blocks += [dot3(top, transfer_v[DEPTH - 1, side], NT) for side in range(2)]
        half = len(blocks) // 2
        for index in range(half):
            span = slice(index * rank, (index + 1) * rank)
            both = jnp.concatenate([blocks[index], blocks[half + index]], axis=0).T
            path_high[span], path_low[span] = halves(both)

    def inverse():
        points_dev = order_v.shape[1]
        tiles = points_dev // LANES
        spot = order_v[...] - me * points_dev
        times = lax.broadcasted_iota(jnp.int32, (1, points_dev), 1)
        shape = (tiles, points_dev)
        match = lax.broadcasted_iota(jnp.int32, shape, 0) == lax.shift_right_logical(spot, 7)
        digits = [
            jnp.where(match, jnp.broadcast_to(digit.astype(F32), shape), 0.0)
            for digit in (lax.shift_right_logical(times, 4), times & 15)
        ]
        shape = (LANES, points_dev)
        match = lax.broadcasted_iota(jnp.int32, shape, 0) == (spot & (LANES - 1))
        both = lax.dot_general(
            jnp.concatenate(digits, axis=0).astype(BF16),
            jnp.where(match, 1.0, 0.0).astype(BF16),
            NT,
            preferred_element_type=F32,
        )
        inverse_out[...] = (both[:tiles] * 16.0 + both[tiles:]).astype(jnp.int32)

    for copy in copies:
        copy.wait()
    for _ in chain():
        pass
    inverse()
    for copy in pair_copies:
        copy.wait()

    def pair_step(pair, carry):
        for slot in range(slots):
            span = slice(slot * rank, (slot + 1) * rank)
            both = jnp.concatenate([far_v[2 * pair, slot], far_v[2 * pair + 1, slot]], axis=0).T
            leaf_high[pair, span], leaf_low[pair, span] = halves(both)
        both = jnp.concatenate([lift_v[2 * pair], lift_v[2 * pair + 1]], axis=0).T
        lift_high[pair], lift_low[pair] = halves(both)
        bases_high[pair], bases_low[pair] = halves(bases_v[pair])
        return carry

    lax.fori_loop(0, pairs, pair_step, 0)
    write(*range(9))
    for copy in writes:
        copy.wait()


def middle_kernel(
    leaf_dev,
    me_ref,
    group_hbm,
    up_high_hbm,
    up_low_hbm,
    half_out,
    nodes_out,
    far_out,
    roots_v,
    up_high,
    up_low,
    sems,
    half_sems,
):
    low = lax.rem(me_ref[0], GROUP) < REACH
    copies = fetch(
        [
            (group_hbm.at[:, pl.ds(leaf_dev * TILE, TILE), :], roots_v),
            (up_high_hbm, up_high),
            (up_low_hbm, up_low),
        ],
        sems,
    )
    rows = (leaf_dev + 1) * TILE
    edge_rows = group_hbm.shape[1] - rows
    first = jnp.where(low, REACH, 0)
    moves = [
        (group_hbm.at[first + part, pl.ds(0, rows)], half_out.at[pl.ds(part * rows, rows)])
        for part in range(REACH)
    ]
    moves.append(
        (
            group_hbm.at[jnp.where(low, GROUP - 1, 0), pl.ds(rows, edge_rows)],
            half_out.at[pl.ds(REACH * rows, edge_rows)],
        )
    )
    moves = fetch(moves, half_sems)
    for copy in copies:
        copy.wait()
    roots = [roots_v[peer] for peer in range(GROUP)]
    start, tiles = 0, []
    for level in range(1, DEPTH):
        width = 1 << level
        count = GROUP // width
        left = jnp.concatenate(
            [row_of(roots[n * width : (n + 1) * width]) for n in range(count)], axis=0
        )
        size = left.shape[1]
        nodes = dot_halves(left, up_high[start : start + size], up_low[start : start + size], NN)
        start += size
        tiles += [fold(nodes[n * 2 * TILE : (n + 1) * 2 * TILE]) for n in range(count)]
    row = REACH * rows + edge_rows
    for index, tile in enumerate(tiles):
        half_out[row + index * TILE : row + (index + 1) * TILE, :] = tile
        for peer in range(nodes_out.shape[0]):
            nodes_out[peer, index] = tile
    for index in range(3):
        far_out[index] = tiles[NODES - 3 + index]
    for copy in moves:
        copy.wait()


def down_kernel(parts, me_ref, *refs):
    node_parts, refs = refs[:parts], refs[parts:]
    count = (len(refs) - 5) // 2
    out_ref = refs[count]
    held = refs[count + 1 : 2 * count + 1]
    nodes_ref, y_tree, sems, node_sems = refs[2 * count + 1 :]
    me = me_ref[0]
    groups = nodes_ref.shape[0]
    group = lax.shift_right_logical(me, 3)
    place = me & (GROUP - 1)
    low = place < REACH
    if parts > 1:
        near_by, far_by = jnp.where(low, groups - 1, 1), jnp.where(low, 1, groups - 1)
        across = lax.rem(group + 2, groups)
        near_group = lax.rem(group + near_by, groups)
        node_copies = fetch(
            [
                (node_parts[0].at[0], nodes_ref.at[group]),
                (node_parts[1].at[0], nodes_ref.at[lax.rem(group + far_by, groups)]),
                (node_parts[2], nodes_ref.at[across, pl.ds(NODES - 3, 3)]),
            ],
            node_sems,
        )
    else:
        node_copies = fetch([(node_parts[0], nodes_ref)], node_sems)
    copies = fetch(list(zip(refs[:count], held)), sems)
    (
        group_ref,
        half_ref,
        far_ids_s,
        far_count_s,
        path_high,
        path_low,
        leaf_high,
        leaf_low,
        lift_high,
        lift_low,
        edge_high,
        edge_low,
        bases_high,
        bases_low,
        near_ref,
        inverse_ref,
    ) = held
    leaf_dev, vectors, leaf_size = near_ref.shape
    points_dev = out_ref.shape[1]
    slots = far_ids_s.shape[1]
    per_leaf = leaf_size // LANES
    rank = bases_high.shape[1] // 2
    start = (leaf_dev + 1) * TILE
    edge_rows = group_ref.shape[1] - start

    def tile_of(subtree, index):
        other = subtree & (GROUP - 1)
        inside = lax.shift_right_arithmetic(subtree, 3) == group
        row = pl.multiple_of(index * TILE, TILE)
        near_row = jnp.clip(other - jnp.where(low, REACH, 0), 0, REACH - 1) * start
        here = group_ref[other, pl.ds(row, TILE), :]
        there = half_ref[pl.ds(pl.multiple_of(near_row + row, TILE), TILE), :]
        return jnp.where(inside, here, there)

    for copy in node_copies + copies[:6]:
        copy.wait()
    if parts > 1:
        for index in range(NODES):
            row = half_ref.shape[0] - (NODES - index) * TILE
            tile = half_ref[row : row + TILE, :]
            nodes_ref[near_group, index] = tile
    partners = []
    for level in range(DEPTH):
        node = lax.shift_right_logical(me, level)
        size = (groups * GROUP) >> level
        for offset in OFFSETS:
            other = node + offset
            used = (other >= 0) & (other < size)
            other = jnp.clip(other, 0, size - 1)
            if level == 0:
                tile = tile_of(other, leaf_dev)
            else:
                shift = DEPTH - 1 - level
                first = GROUP - (2 << shift)
                tile = nodes_ref[
                    lax.shift_right_logical(other, shift), first + (other & ((1 << shift) - 1))
                ]
            partners.append(jnp.where(used, tile, 0.0))
    top = lax.shift_right_logical(me, DEPTH)
    for side in range(2):
        blended = jnp.zeros((TILE, LANES), F32)
        for other in range(groups // 2):
            distance = jnp.abs(top - other)
            weight = jnp.where(distance >= 2, 1.0 / jnp.maximum(distance, 1).astype(F32), 0.0)
            blended = blended + weight * nodes_ref[2 * other + side, GROUP - 2]
        partners.append(blended)
    half = len(partners) // 2
    row = row_of(partners)
    first, second = pair_dot(
        row[:, : half * rank], row[:, half * rank :], path_high[...], path_low[...]
    )
    down = first[:, :rank] + second[:, rank:]

    edges = []
    for offset in (-1, 1):
        other = me + offset
        inside = lax.shift_right_arithmetic(other, 3) == group
        here = group_ref[other & (GROUP - 1), start:, :]
        chosen = jnp.where(inside, here, half_ref[REACH * start : REACH * start + edge_rows, :])
        edges.append(
            jnp.concatenate(
                [chosen[part * vectors : (part + 1) * vectors] for part in range(per_leaf)], axis=1
            )
        )

    for copy in copies[6:]:
        copy.wait()
    edge_parts = [
        dot_halves(edges[index], edge_high[index], edge_low[index], NN) for index in range(2)
    ]
    left_half = lax.broadcasted_iota(jnp.int32, (vectors, 2 * rank), 1) < rank

    def far_of(leaf):
        picked = []
        for slot in range(slots):
            used = slot < far_count_s[leaf]
            spot = far_ids_s[leaf, slot]
            tile = tile_of(lax.shift_right_logical(spot, 3), spot & (leaf_dev - 1))
            picked.append(jnp.where(used, tile, 0.0))
        return row_of(picked)

    def pair_step(pair, carry):
        two = (2 * pair, 2 * pair + 1)
        first, second = pair_dot(far_of(two[0]), far_of(two[1]), leaf_high[pair], leaf_low[pair])
        lifted = dot_halves(down, lift_high[pair], lift_low[pair], NN)
        first = jnp.where(left_half, first + lifted, 0.0)
        second = jnp.where(left_half, 0.0, second + lifted)
        products = pair_dot(first, second, bases_high[pair], bases_low[pair])
        for leaf, product in zip(two, products):
            y_tree[leaf] = near_ref[leaf] + product
        return carry

    lax.fori_loop(0, leaf_dev // 2, pair_step, 0)
    y_tree[0] = y_tree[0] + edge_parts[0]
    y_tree[leaf_dev - 1] = y_tree[leaf_dev - 1] + edge_parts[1]

    def tile_step(tile, carry):
        spot = inverse_ref[pl.ds(tile, 1), :]
        out_ref[:, pl.ds(pl.multiple_of(tile * LANES, LANES), LANES)] = lane_gather(
            y_tree, lax.shift_right_logical(spot, 7), spot & (LANES - 1)
        )
        return carry

    lax.fori_loop(0, points_dev // LANES, tile_step, 0)


def local(
    devices,
    points,
    order,
    bases,
    lift,
    near_ids,
    near_blocks,
    far_ids,
    far_count,
    far_blocks,
    transfer,
    couple,
    links,
    top_couple,
):
    me = lax.axis_index("leaf").astype(jnp.int32).reshape(1)
    vectors, points_dev = points.shape
    leaf_dev, leaf_size, rank = bases.shape
    slots = near_ids.shape[1]
    far_slots = far_ids.shape[1]
    bases_t = jnp.swapaxes(bases, 1, 2)
    tiles = points_dev // LANES
    edge_rows = vectors * (leaf_size // LANES)
    rows = (leaf_dev + 1) * TILE
    groups = devices // GROUP
    order_tiles = order.reshape(tiles, LANES)
    shape = jax.ShapeDtypeStruct

    group_out, tree_x = pl.pallas_call(
        up_kernel,
        out_shape=[
            shape((GROUP, rows + edge_rows, LANES), F32),
            shape((leaf_dev, vectors, leaf_size), F32),
        ],
        in_specs=[SMEM] + [HBM] * 4,
        out_specs=[VMEM] * 2,
        scratch_shapes=[
            pltpu.VMEM(points.shape, F32),
            pltpu.VMEM((tiles, LANES), jnp.int32),
            pltpu.VMEM(bases_t.shape, F32),
            pltpu.VMEM(lift.shape, F32),
            pltpu.SemaphoreType.DMA((4,)),
        ],
        compiler_params=PARAMS,
        name="up",
    )(me, points, order_tiles, bases_t, lift)

    aligned = [[g * GROUP + i for i in range(GROUP)] for g in range(groups)]
    group_in = lax.all_to_all(group_out, "leaf", 0, 0, axis_index_groups=aligned, tiled=True)

    ids_t = near_ids.T
    both = lambda *size: [shape(size, BF16)] * 2

    def call(kernel, operands, results, scalar, scratch, sems, cost, name):
        return pl.pallas_call(
            kernel,
            out_shape=results,
            in_specs=[SMEM] + [HBM] * len(operands),
            out_specs=[HBM] * len(results),
            scratch_shapes=[
                (pltpu.SMEM if x is scalar else pltpu.VMEM)(x.shape, x.dtype) for x in operands
            ]
            + [pltpu.VMEM(x.shape, x.dtype) for x in results]
            + [pltpu.VMEM(size, F32) for size in scratch]
            + [pltpu.SemaphoreType.DMA(size) for size in sems],
            compiler_params=PARAMS,
            cost_estimate=pl.CostEstimate(flops=cost * 250, bytes_accessed=cost, transcendentals=0),
            name=name,
        )(me, *operands)

    near_part, up_high, up_low, edge_high, edge_low = call(
        near_kernel,
        (ids_t, tree_x, transfer, near_blocks),
        [shape(tree_x.shape, F32)] + both(14 * rank, rank) + both(2, leaf_size, leaf_size),
        ids_t,
        ((slots * leaf_size, 2 * leaf_dev * vectors), (leaf_size, leaf_dev * vectors)),
        ((3,), (leaf_dev,), (5,)),
        12_000_000,
        "near",
    )
    links_own = links.reshape(links.shape[1:])
    path_rows = (DEPTH * len(OFFSETS) + 2) // 2 * rank
    (
        path_high,
        path_low,
        leaf_high,
        leaf_low,
        lift_high,
        lift_low,
        bases_high,
        bases_low,
        inverse,
    ) = call(
        weight_kernel,
        (
            links_own,
            transfer,
            couple,
            top_couple,
            order.reshape(1, points_dev),
            lift,
            far_blocks,
            bases_t.reshape(leaf_dev // 2, 2 * rank, leaf_size),
        ),
        both(path_rows, 2 * rank)
        + both(leaf_dev // 2, far_slots * rank, 2 * rank)
        + both(leaf_dev // 2, rank, 2 * rank)
        + both(leaf_dev // 2, 2 * rank, leaf_size)
        + [shape((tiles, LANES), jnp.int32)],
        links_own,
        (),
        ((6,), (2,), (9,)),
        12_000_000,
        "weights",
    )

    by_permute = groups == 4
    half_out, nodes_out, far_nodes = pl.pallas_call(
        functools.partial(middle_kernel, leaf_dev),
        out_shape=[
            shape((REACH * rows + edge_rows + NODES * TILE, LANES), F32),
            shape((1 if by_permute else groups, NODES, TILE, LANES), F32),
            shape((3, TILE, LANES), F32),
        ],
        in_specs=[SMEM] + [HBM] * 3,
        out_specs=[VMEM] * 3,
        scratch_shapes=[
            pltpu.VMEM((GROUP, TILE, LANES), F32),
            pltpu.VMEM(up_high.shape, BF16),
            pltpu.VMEM(up_low.shape, BF16),
            pltpu.SemaphoreType.DMA((3,)),
            pltpu.SemaphoreType.DMA((REACH + 1,)),
        ],
        compiler_params=PARAMS,
        name="middle",
    )(me, group_in, up_high, up_low)

    def shifted(x, low, high):
        pairs = []
        for device in range(devices):
            by = low if device % GROUP < REACH else high
            pairs.append(((device + by * GROUP) % devices, device))
        return lax.ppermute(x, "leaf", pairs)

    half_in = shifted(half_out, -1, 1)
    if by_permute:
        node_parts = (nodes_out, shifted(nodes_out, 1, -1), shifted(far_nodes, 2, 2))
    else:
        across = [[g * GROUP + i for g in range(groups)] for i in range(GROUP)]
        node_parts = (lax.all_to_all(nodes_out, "leaf", 0, 0, axis_index_groups=across, tiled=True),)

    operands = (
        group_in,
        half_in,
        far_ids,
        far_count,
        path_high,
        path_low,
        leaf_high,
        leaf_low,
        lift_high,
        lift_low,
        edge_high,
        edge_low,
        bases_high,
        bases_low,
        near_part,
        inverse,
    )
    return pl.pallas_call(
        functools.partial(down_kernel, len(node_parts)),
        out_shape=shape((vectors, points_dev), F32),
        in_specs=[SMEM] + [HBM] * (len(node_parts) + len(operands)),
        out_specs=VMEM,
        scratch_shapes=[
            (pltpu.SMEM if x is far_ids or x is far_count else pltpu.VMEM)(x.shape, x.dtype)
            for x in operands
        ]
        + [
            pltpu.VMEM((groups, NODES, TILE, LANES), F32),
            pltpu.VMEM(tree_x.shape, F32),
            pltpu.SemaphoreType.DMA((len(operands),)),
            pltpu.SemaphoreType.DMA((3,)),
        ],
        compiler_params=PARAMS,
        name="down",
    )(me, *node_parts, *operands)


def solution(mesh):
    in_specs = (
        P(None, "leaf"),
        P("leaf"),
        P("leaf", None, None),
        P("leaf", None, None),
        P("leaf", None),
        P("leaf", None, None, None),
        P("leaf", None),
        P("leaf"),
        P("leaf", None, None, None),
        P(),
        P(),
        P("leaf", None, None),
        P(),
    )
    return jax.shard_map(
        functools.partial(local, mesh.shape["leaf"]),
        mesh=mesh,
        in_specs=in_specs,
        out_specs=P(None, "leaf"),
        check_vma=False,
    )
```

```python
import functools

import jax
import jax.numpy as jnp
from jax import lax
from jax.experimental import pallas as pl
from jax.experimental.pallas import tpu as pltpu
from jax.sharding import PartitionSpec as P

REACH = 4
DEPTH = 4
OFFSETS = (-3, -2, 2, 3)
GROUP = 2 * REACH
LANES = 128
TILE = 8
NODES = GROUP - 1
VMEM_LIMIT = 64 * 1024 * 1024

NN = (((1,), (0,)), ((), ()))
NT = (((1,), (1,)), ((), ()))

VMEM = pl.BlockSpec(memory_space=pltpu.VMEM)
SMEM = pl.BlockSpec(memory_space=pltpu.SMEM)
HBM = pl.BlockSpec(memory_space=pltpu.HBM)
PARAMS = pltpu.CompilerParams(vmem_limit_bytes=VMEM_LIMIT)
F32 = jnp.float32
BF16 = jnp.bfloat16


def halves(x):
    high = x.astype(BF16)
    low = (x - high.astype(F32)).astype(BF16)
    return high, low


def dot_halves(a, b_high, b_low, dims):
    a_high, a_low = halves(a)
    rows = a.shape[0]
    both = lax.dot_general(
        jnp.concatenate([a_high, a_low], axis=0), b_high, dims, preferred_element_type=F32
    )
    cross = lax.dot_general(a_high, b_low, dims, preferred_element_type=F32)
    return both[:rows] + (both[rows:] + cross)


def pair_dot(a, b, w_high, w_low):
    a_high, a_low = halves(a)
    b_high, b_low = halves(b)
    rows = a.shape[0]
    both = lax.dot_general(
        jnp.concatenate([a_high, b_high, a_low, b_low], axis=0),
        w_high,
        NN,
        preferred_element_type=F32,
    )
    cross = lax.dot_general(
        jnp.concatenate([a_high, b_high], axis=0), w_low, NN, preferred_element_type=F32
    )
    total = both[: 2 * rows] + (both[2 * rows :] + cross)
    return total[:rows], total[rows:]


def dot3(a, b, dims):
    return dot_halves(a, *halves(b), dims)


def fold(x):
    return jnp.concatenate([x[:TILE], x[TILE:]], axis=1)


def beside(p, q):
    rank = p.shape[1] // 2
    left = lax.broadcasted_iota(jnp.int32, p.shape, 1) < rank
    return jnp.concatenate(
        [
            jnp.where(left, p, pltpu.roll(q, rank, 1)),
            jnp.where(left, pltpu.roll(p, rank, 1), q),
        ],
        axis=0,
    )


def row_of(tiles):
    return jnp.concatenate([beside(*tiles[k : k + 2]) for k in range(0, len(tiles), 2)], axis=1)


def lane_gather(x, high, low):
    rows, columns = x.shape
    high = jnp.broadcast_to(high, (rows, LANES))
    low = jnp.broadcast_to(low, (rows, LANES))
    result = jnp.zeros((rows, LANES), x.dtype)
    for source in range(columns // LANES):
        tile = x[:, source * LANES : (source + 1) * LANES]
        moved = jnp.take_along_axis(tile, low, axis=1, mode="promise_in_bounds")
        result = jnp.where(high == source, moved, result)
    return result


def fetch(pairs, sems):
    copies = [
        pltpu.make_async_copy(source, target, sems.at[index])
        for index, (source, target) in enumerate(pairs)
    ]
    for copy in copies:
        copy.start()
    return copies


def up_kernel(
    me_ref, points_hbm, order_hbm, bases_hbm, lift_hbm, out, x_out, points_v, order_v, bases_v, lift_v, sems
):
    copies = fetch(
        [(order_hbm, order_v), (points_hbm, points_v), (bases_hbm, bases_v), (lift_hbm, lift_v)], sems
    )
    me = me_ref[0]
    leaf_dev, rank, leaf_size = bases_v.shape
    vectors, points_dev = points_v.shape
    copies[0].wait()
    copies[1].wait()
    points = points_v[...]
    per_leaf = leaf_size // LANES
    for t in range(points_dev // LANES):
        spot = order_v[t : t + 1, :] - me * points_dev
        column = t % per_leaf * LANES
        x_out[t // per_leaf, :, column : column + LANES] = lane_gather(
            points, lax.shift_right_logical(spot, 7), spot & (LANES - 1)
        )
    copies[2].wait()
    coefs = [dot3(x_out[leaf], bases_v[leaf], NT) for leaf in range(leaf_dev)]
    tiles = [fold(coef) for coef in coefs]
    copies[3].wait()
    weights = lift_v[...].reshape(leaf_dev * rank, rank)
    tiles.append(fold(dot3(jnp.concatenate(coefs, axis=1), weights, NN)))
    for peer in range(GROUP):
        for index, tile in enumerate(tiles):
            out[peer, index * TILE : (index + 1) * TILE, :] = tile
    place = lax.rem(me, GROUP)
    start = len(tiles) * TILE
    for part in range(per_leaf):
        first = x_out[0, :, part * LANES : (part + 1) * LANES]
        last = x_out[leaf_dev - 1, :, part * LANES : (part + 1) * LANES]
        rows = slice(start + part * vectors, start + (part + 1) * vectors)
        for peer in range(GROUP):
            above = lax.rem(place + 1, GROUP) == peer
            out[peer, rows, :] = jnp.where(above, last, first)


def side_kernel(me_ref, *refs):
    inputs, outputs = refs[:11], refs[11:25]
    held, results = refs[25:36], refs[36:50]
    sems, block_sems, out_sems = refs[50:]
    ids_s, links_s, transfer_v, couple_v, x_v, top_v, lift_v, order_v, far_v, bases_v, blocks_v = held
    (
        up_high,
        up_low,
        path_high,
        path_low,
        inverse_out,
        leaf_high,
        leaf_low,
        lift_high,
        lift_low,
        bases_high,
        bases_low,
        edge_high,
        edge_low,
        near_out,
    ) = results
    leaf_dev, slots, leaf_size, _ = blocks_v.shape
    rank = top_v.shape[0]
    pairs = leaf_dev // 2
    me = me_ref[0]
    first = fetch(list(zip(inputs[:8], held[:8])), sems)

    def block(pair):
        two = pl.ds(2 * pair, 2)
        return fetch([(inputs[10].at[two], blocks_v.at[two])], block_sems.at[pl.ds(pair, 1)])

    blocks = block(0)
    second = fetch(list(zip(inputs[8:10], held[8:10])), sems.at[pl.ds(8, 2)])
    for pair in range(1, pairs):
        blocks += block(pair)
    writes = []

    def write(*indices):
        for index in indices:
            writes.extend(fetch([(results[index], outputs[index])], out_sems.at[pl.ds(index, 1)]))

    def couplings(level):
        weights = [
            links_s[level, column].astype(F32) * couple_v[level, column]
            for column in range(len(OFFSETS))
        ]
        return jnp.concatenate(weights, axis=1)

    def chain():
        bits = [lax.shift_right_logical(me, level) & 1 for level in range(DEPTH)]
        up = transfer_v[0].reshape(2 * rank, rank)
        path = transfer_v[0, bits[0]]
        parts = [couplings(0)]
        row = 0
        for level in range(1, DEPTH):
            rows = up.shape[0]
            up_high[row : row + rows], up_low[row : row + rows] = halves(up)
            row += rows
            if level < DEPTH - 1:
                up = jnp.concatenate(
                    [dot3(up, transfer_v[level, side], NN) for side in range(2)], axis=0
                )
            parts.append(dot3(path, couplings(level), NN))
            path = dot3(path, transfer_v[level, bits[level]], NN)
            if level < DEPTH - 1:
                yield
        write(0, 1)
        top = dot3(path, top_v[...], NN)
        yield
        parts = [x[:, k * rank : (k + 1) * rank] for x in parts for k in range(len(OFFSETS))]
        parts += [dot3(top, transfer_v[DEPTH - 1, side], NT) for side in range(2)]
        half = len(parts) // 2
        for index in range(half):
            span = slice(index * rank, (index + 1) * rank)
            both = jnp.concatenate([parts[index], parts[half + index]], axis=0).T
            path_high[span], path_low[span] = halves(both)
        write(2, 3)

    def inverse():
        points_dev = order_v.shape[1]
        tiles = points_dev // LANES
        spot = order_v[...] - me * points_dev
        times = lax.broadcasted_iota(jnp.int32, (1, points_dev), 1)
        shape = (tiles, points_dev)
        match = lax.broadcasted_iota(jnp.int32, shape, 0) == lax.shift_right_logical(spot, 7)
        digits = [
            jnp.where(match, jnp.broadcast_to(digit.astype(F32), shape), 0.0)
            for digit in (lax.shift_right_logical(times, 4), times & 15)
        ]
        shape = (LANES, points_dev)
        match = lax.broadcasted_iota(jnp.int32, shape, 0) == (spot & (LANES - 1))
        both = lax.dot_general(
            jnp.concatenate(digits, axis=0).astype(BF16),
            jnp.where(match, 1.0, 0.0).astype(BF16),
            NT,
            preferred_element_type=F32,
        )
        inverse_out[...] = (both[:tiles] * 16.0 + both[tiles:]).astype(jnp.int32)
        write(4)

    def transposes(pair):
        two = range(2 * pair, 2 * pair + 2)
        for slot in range(far_v.shape[1]):
            span = slice(slot * rank, (slot + 1) * rank)
            both = jnp.concatenate([far_v[leaf, slot] for leaf in two], axis=0).T
            leaf_high[pair, span], leaf_low[pair, span] = halves(both)
        both = jnp.concatenate([lift_v[leaf] for leaf in two], axis=0).T
        lift_high[pair], lift_low[pair] = halves(both)
        bases_high[pair], bases_low[pair] = halves(bases_v[pair])

    def near(leaf):
        total = jnp.zeros(near_out.shape[1:], F32)
        for slot in range(slots):
            local = ids_s[slot, leaf] - me * leaf_dev
            here = (local >= 0) & (local < leaf_dev)
            x_leaf = jnp.where(here, x_v[jnp.clip(local, 0, leaf_dev - 1)], 0.0)
            total = total + dot3(x_leaf, blocks_v[leaf, slot], NT)
        near_out[leaf] = total

    def edge(index, leaf, outside):
        total = jnp.zeros((leaf_size, leaf_size), F32)
        for slot in range(1, slots):
            remote = ids_s[slot, leaf] - me * leaf_dev == outside
            total = total + jnp.where(remote, blocks_v[leaf, slot], 0.0)
        edge_high[index], edge_low[index] = halves(total.T)

    for copy in first:
        copy.wait()
    links = chain()
    next(links)
    for pair in range(pairs):
        blocks[pair].wait()
        if pair == 0:
            for copy in second:
                copy.wait()
        near(2 * pair)
        near(2 * pair + 1)
        transposes(pair)
        next(links, None)
        if pair == 0:
            edge(0, 0, -1)
        if pair == 1:
            inverse()
        if pair == pairs - 1:
            edge(1, leaf_dev - 1, leaf_dev)
    for _ in links:
        pass
    write(*range(5, 14))
    for copy in writes:
        copy.wait()


def middle_kernel(
    leaf_dev,
    me_ref,
    group_hbm,
    up_high_hbm,
    up_low_hbm,
    half_out,
    nodes_out,
    far_out,
    roots_v,
    up_high,
    up_low,
    sems,
    half_sems,
):
    low = lax.rem(me_ref[0], GROUP) < REACH
    copies = fetch(
        [
            (group_hbm.at[:, pl.ds(leaf_dev * TILE, TILE), :], roots_v),
            (up_high_hbm, up_high),
            (up_low_hbm, up_low),
        ],
        sems,
    )
    rows = (leaf_dev + 1) * TILE
    edge_rows = group_hbm.shape[1] - rows
    first = jnp.where(low, REACH, 0)
    moves = [
        (group_hbm.at[first + part, pl.ds(0, rows)], half_out.at[pl.ds(part * rows, rows)])
        for part in range(REACH)
    ]
    moves.append(
        (
            group_hbm.at[jnp.where(low, GROUP - 1, 0), pl.ds(rows, edge_rows)],
            half_out.at[pl.ds(REACH * rows, edge_rows)],
        )
    )
    moves = fetch(moves, half_sems)
    for copy in copies:
        copy.wait()
    roots = [roots_v[peer] for peer in range(GROUP)]
    start, tiles = 0, []
    for level in range(1, DEPTH):
        width = 1 << level
        count = GROUP // width
        left = jnp.concatenate(
            [row_of(roots[n * width : (n + 1) * width]) for n in range(count)], axis=0
        )
        size = left.shape[1]
        nodes = dot_halves(left, up_high[start : start + size], up_low[start : start + size], NN)
        start += size
        tiles += [fold(nodes[n * 2 * TILE : (n + 1) * 2 * TILE]) for n in range(count)]
    row = REACH * rows + edge_rows
    for index, tile in enumerate(tiles):
        half_out[row + index * TILE : row + (index + 1) * TILE, :] = tile
        for peer in range(nodes_out.shape[0]):
            nodes_out[peer, index] = tile
    for index in range(3):
        far_out[index] = tiles[NODES - 3 + index]
    for copy in moves:
        copy.wait()


def down_kernel(parts, me_ref, *refs):
    node_parts, refs = refs[:parts], refs[parts:]
    count = (len(refs) - 5) // 2
    out_ref = refs[count]
    held = refs[count + 1 : 2 * count + 1]
    nodes_ref, y_tree, sems, node_sems = refs[2 * count + 1 :]
    me = me_ref[0]
    groups = nodes_ref.shape[0]
    group = lax.shift_right_logical(me, 3)
    place = me & (GROUP - 1)
    low = place < REACH
    if parts > 1:
        near_by, far_by = jnp.where(low, groups - 1, 1), jnp.where(low, 1, groups - 1)
        across = lax.rem(group + 2, groups)
        near_group = lax.rem(group + near_by, groups)
        node_copies = fetch(
            [
                (node_parts[0].at[0], nodes_ref.at[group]),
                (node_parts[1].at[0], nodes_ref.at[lax.rem(group + far_by, groups)]),
                (node_parts[2], nodes_ref.at[across, pl.ds(NODES - 3, 3)]),
            ],
            node_sems,
        )
    else:
        node_copies = fetch([(node_parts[0], nodes_ref)], node_sems)
    copies = fetch(list(zip(refs[:count], held)), sems)
    (
        group_ref,
        half_ref,
        far_ids_s,
        far_count_s,
        path_high,
        path_low,
        leaf_high,
        leaf_low,
        lift_high,
        lift_low,
        edge_high,
        edge_low,
        bases_high,
        bases_low,
        near_ref,
        inverse_ref,
    ) = held
    leaf_dev, vectors, leaf_size = near_ref.shape
    points_dev = out_ref.shape[1]
    slots = far_ids_s.shape[1]
    per_leaf = leaf_size // LANES
    rank = bases_high.shape[1] // 2
    start = (leaf_dev + 1) * TILE
    edge_rows = group_ref.shape[1] - start

    def tile_of(subtree, index):
        other = subtree & (GROUP - 1)
        inside = lax.shift_right_arithmetic(subtree, 3) == group
        row = pl.multiple_of(index * TILE, TILE)
        near_row = jnp.clip(other - jnp.where(low, REACH, 0), 0, REACH - 1) * start
        here = group_ref[other, pl.ds(row, TILE), :]
        there = half_ref[pl.ds(pl.multiple_of(near_row + row, TILE), TILE), :]
        return jnp.where(inside, here, there)

    for copy in node_copies + copies[:6]:
        copy.wait()
    if parts > 1:
        for index in range(NODES):
            row = half_ref.shape[0] - (NODES - index) * TILE
            tile = half_ref[row : row + TILE, :]
            nodes_ref[near_group, index] = tile
    partners = []
    for level in range(DEPTH):
        node = lax.shift_right_logical(me, level)
        size = (groups * GROUP) >> level
        for offset in OFFSETS:
            other = node + offset
            used = (other >= 0) & (other < size)
            other = jnp.clip(other, 0, size - 1)
            if level == 0:
                tile = tile_of(other, leaf_dev)
            else:
                shift = DEPTH - 1 - level
                first = GROUP - (2 << shift)
                tile = nodes_ref[
                    lax.shift_right_logical(other, shift), first + (other & ((1 << shift) - 1))
                ]
            partners.append(jnp.where(used, tile, 0.0))
    top = lax.shift_right_logical(me, DEPTH)
    for side in range(2):
        blended = jnp.zeros((TILE, LANES), F32)
        for other in range(groups // 2):
            distance = jnp.abs(top - other)
            weight = jnp.where(distance >= 2, 1.0 / jnp.maximum(distance, 1).astype(F32), 0.0)
            blended = blended + weight * nodes_ref[2 * other + side, GROUP - 2]
        partners.append(blended)
    half = len(partners) // 2
    row = row_of(partners)
    first, second = pair_dot(
        row[:, : half * rank], row[:, half * rank :], path_high[...], path_low[...]
    )
    down = first[:, :rank] + second[:, rank:]

    rows = []
    for leaf in range(leaf_dev):
        picked = []
        for slot in range(slots):
            used = slot < far_count_s[leaf]
            spot = far_ids_s[leaf, slot]
            tile = tile_of(lax.shift_right_logical(spot, 3), spot & (leaf_dev - 1))
            picked.append(jnp.where(used, tile, 0.0))
        rows.append(row_of(picked))
    edges = []
    for offset in (-1, 1):
        other = me + offset
        inside = lax.shift_right_arithmetic(other, 3) == group
        here = group_ref[other & (GROUP - 1), start:, :]
        chosen = jnp.where(inside, here, half_ref[REACH * start : REACH * start + edge_rows, :])
        edges.append(
            jnp.concatenate(
                [chosen[part * vectors : (part + 1) * vectors] for part in range(per_leaf)], axis=1
            )
        )

    for copy in copies[6:]:
        copy.wait()
    edge_parts = [
        dot_halves(edges[index], edge_high[index], edge_low[index], NN) for index in range(2)
    ]
    left_half = lax.broadcasted_iota(jnp.int32, (vectors, 2 * rank), 1) < rank
    for pair in range(leaf_dev // 2):
        two = (2 * pair, 2 * pair + 1)
        first, second = pair_dot(rows[two[0]], rows[two[1]], leaf_high[pair], leaf_low[pair])
        lift = dot_halves(down, lift_high[pair], lift_low[pair], NN)
        first = jnp.where(left_half, first + lift, 0.0)
        second = jnp.where(left_half, 0.0, second + lift)
        products = pair_dot(first, second, bases_high[pair], bases_low[pair])
        for leaf, product in zip(two, products):
            y_leaf = near_ref[leaf] + product
            if leaf == 0:
                y_leaf = y_leaf + edge_parts[0]
            if leaf == leaf_dev - 1:
                y_leaf = y_leaf + edge_parts[1]
            y_tree[:, leaf * leaf_size : (leaf + 1) * leaf_size] = y_leaf

    y = y_tree[...]
    for tile in range(points_dev // LANES):
        spot = inverse_ref[tile : tile + 1, :]
        out_ref[:, tile * LANES : (tile + 1) * LANES] = lane_gather(
            y, lax.shift_right_logical(spot, 7), spot & (LANES - 1)
        )


def local(
    devices,
    points,
    order,
    bases,
    lift,
    near_ids,
    near_blocks,
    far_ids,
    far_count,
    far_blocks,
    transfer,
    couple,
    links,
    top_couple,
):
    me = lax.axis_index("leaf").astype(jnp.int32).reshape(1)
    vectors, points_dev = points.shape
    leaf_dev, leaf_size, rank = bases.shape
    slots = near_ids.shape[1]
    far_slots = far_ids.shape[1]
    bases_t = jnp.swapaxes(bases, 1, 2)
    tiles = points_dev // LANES
    edge_rows = vectors * (leaf_size // LANES)
    rows = (leaf_dev + 1) * TILE
    groups = devices // GROUP
    order_tiles = order.reshape(tiles, LANES)
    shape = jax.ShapeDtypeStruct

    group_out, tree_x = pl.pallas_call(
        up_kernel,
        out_shape=[
            shape((GROUP, rows + edge_rows, LANES), F32),
            shape((leaf_dev, vectors, leaf_size), F32),
        ],
        in_specs=[SMEM] + [HBM] * 4,
        out_specs=[VMEM] * 2,
        scratch_shapes=[
            pltpu.VMEM(points.shape, F32),
            pltpu.VMEM((tiles, LANES), jnp.int32),
            pltpu.VMEM(bases_t.shape, F32),
            pltpu.VMEM(lift.shape, F32),
            pltpu.SemaphoreType.DMA((4,)),
        ],
        compiler_params=PARAMS,
        name="up",
    )(me, points, order_tiles, bases_t, lift)

    aligned = [[g * GROUP + i for i in range(GROUP)] for g in range(groups)]
    group_in = lax.all_to_all(group_out, "leaf", 0, 0, axis_index_groups=aligned, tiled=True)

    ids_t = near_ids.T
    both = lambda *size: [shape(size, BF16)] * 2

    links_own = links.reshape(links.shape[1:])
    path_rows = (DEPTH * len(OFFSETS) + 2) // 2 * rank
    operands = (
        ids_t,
        links_own,
        transfer,
        couple,
        tree_x,
        top_couple,
        lift,
        order.reshape(1, points_dev),
        far_blocks,
        bases_t.reshape(leaf_dev // 2, 2 * rank, leaf_size),
        near_blocks,
    )
    results = (
        both(14 * rank, rank)
        + both(path_rows, 2 * rank)
        + [shape((tiles, LANES), jnp.int32)]
        + both(leaf_dev // 2, far_slots * rank, 2 * rank)
        + both(leaf_dev // 2, rank, 2 * rank)
        + both(leaf_dev // 2, 2 * rank, leaf_size)
        + both(2, leaf_size, leaf_size)
        + [shape(tree_x.shape, F32)]
    )
    (
        up_high,
        up_low,
        path_high,
        path_low,
        inverse,
        leaf_high,
        leaf_low,
        lift_high,
        lift_low,
        bases_high,
        bases_low,
        edge_high,
        edge_low,
        near_part,
    ) = pl.pallas_call(
        side_kernel,
        out_shape=results,
        in_specs=[SMEM] + [HBM] * len(operands),
        out_specs=[HBM] * len(results),
        scratch_shapes=[
            (pltpu.SMEM if x is ids_t or x is links_own else pltpu.VMEM)(x.shape, x.dtype)
            for x in operands
        ]
        + [pltpu.VMEM(x.shape, x.dtype) for x in results]
        + [
            pltpu.SemaphoreType.DMA((10,)),
            pltpu.SemaphoreType.DMA((leaf_dev // 2,)),
            pltpu.SemaphoreType.DMA((len(results),)),
        ],
        compiler_params=PARAMS,
        cost_estimate=pl.CostEstimate(
            flops=250 * 12_000_000, bytes_accessed=12_000_000, transcendentals=0
        ),
        name="side",
    )(me, *operands)

    by_permute = groups == 4
    half_out, nodes_out, far_nodes = pl.pallas_call(
        functools.partial(middle_kernel, leaf_dev),
        out_shape=[
            shape((REACH * rows + edge_rows + NODES * TILE, LANES), F32),
            shape((1 if by_permute else groups, NODES, TILE, LANES), F32),
            shape((3, TILE, LANES), F32),
        ],
        in_specs=[SMEM] + [HBM] * 3,
        out_specs=[VMEM] * 3,
        scratch_shapes=[
            pltpu.VMEM((GROUP, TILE, LANES), F32),
            pltpu.VMEM(up_high.shape, BF16),
            pltpu.VMEM(up_low.shape, BF16),
            pltpu.SemaphoreType.DMA((3,)),
            pltpu.SemaphoreType.DMA((REACH + 1,)),
        ],
        compiler_params=PARAMS,
        name="middle",
    )(me, group_in, up_high, up_low)

    def shifted(x, low, high):
        pairs = []
        for device in range(devices):
            by = low if device % GROUP < REACH else high
            pairs.append(((device + by * GROUP) % devices, device))
        return lax.ppermute(x, "leaf", pairs)

    half_in = shifted(half_out, -1, 1)
    if by_permute:
        node_parts = (nodes_out, shifted(nodes_out, 1, -1), shifted(far_nodes, 2, 2))
    else:
        across = [[g * GROUP + i for g in range(groups)] for i in range(GROUP)]
        node_parts = (lax.all_to_all(nodes_out, "leaf", 0, 0, axis_index_groups=across, tiled=True),)

    operands = (
        group_in,
        half_in,
        far_ids,
        far_count,
        path_high,
        path_low,
        leaf_high,
        leaf_low,
        lift_high,
        lift_low,
        edge_high,
        edge_low,
        bases_high,
        bases_low,
        near_part,
        inverse,
    )
    return pl.pallas_call(
        functools.partial(down_kernel, len(node_parts)),
        out_shape=shape((vectors, points_dev), F32),
        in_specs=[SMEM] + [HBM] * (len(node_parts) + len(operands)),
        out_specs=VMEM,
        scratch_shapes=[
            (pltpu.SMEM if x is far_ids or x is far_count else pltpu.VMEM)(x.shape, x.dtype)
            for x in operands
        ]
        + [
            pltpu.VMEM((groups, NODES, TILE, LANES), F32),
            pltpu.VMEM((vectors, points_dev), F32),
            pltpu.SemaphoreType.DMA((len(operands),)),
            pltpu.SemaphoreType.DMA((3,)),
        ],
        compiler_params=PARAMS,
        name="down",
    )(me, *node_parts, *operands)


def solution(mesh):
    in_specs = (
        P(None, "leaf"),
        P("leaf"),
        P("leaf", None, None),
        P("leaf", None, None),
        P("leaf", None),
        P("leaf", None, None, None),
        P("leaf", None),
        P("leaf"),
        P("leaf", None, None, None),
        P(),
        P(),
        P("leaf", None, None),
        P(),
    )
    return jax.shard_map(
        functools.partial(local, mesh.shape["leaf"]),
        mesh=mesh,
        in_specs=in_specs,
        out_specs=P(None, "leaf"),
        check_vma=False,
    )
```

```python
import functools

import jax
import jax.numpy as jnp
from jax import lax
from jax.experimental import pallas as pl
from jax.experimental.pallas import tpu as pltpu
from jax.sharding import PartitionSpec as P

REACH = 4
DEPTH = 4
OFFSETS = (-3, -2, 2, 3)
GROUP = 2 * REACH
LANES = 128
TILE = 8
NODES = GROUP - 1
VMEM_LIMIT = 64 * 1024 * 1024

NN = (((1,), (0,)), ((), ()))
NT = (((1,), (1,)), ((), ()))

VMEM = pl.BlockSpec(memory_space=pltpu.VMEM)
SMEM = pl.BlockSpec(memory_space=pltpu.SMEM)
HBM = pl.BlockSpec(memory_space=pltpu.HBM)
PARAMS = pltpu.CompilerParams(vmem_limit_bytes=VMEM_LIMIT)
F32 = jnp.float32
BF16 = jnp.bfloat16


def halves(x):
    high = x.astype(BF16)
    low = (x - high.astype(F32)).astype(BF16)
    return high, low


def dot_halves(a, b_high, b_low, dims):
    a_high, a_low = halves(a)
    rows = a.shape[0]
    both = lax.dot_general(
        jnp.concatenate([a_high, a_low], axis=0), b_high, dims, preferred_element_type=F32
    )
    cross = lax.dot_general(a_high, b_low, dims, preferred_element_type=F32)
    return both[:rows] + (both[rows:] + cross)


def pair_dot(a, b, w_high, w_low):
    a_high, a_low = halves(a)
    b_high, b_low = halves(b)
    rows = a.shape[0]
    both = lax.dot_general(
        jnp.concatenate([a_high, b_high, a_low, b_low], axis=0),
        w_high,
        NN,
        preferred_element_type=F32,
    )
    cross = lax.dot_general(
        jnp.concatenate([a_high, b_high], axis=0), w_low, NN, preferred_element_type=F32
    )
    total = both[: 2 * rows] + (both[2 * rows :] + cross)
    return total[:rows], total[rows:]


def dot3(a, b, dims):
    return dot_halves(a, *halves(b), dims)


def fold(x):
    return jnp.concatenate([x[:TILE], x[TILE:]], axis=1)


def beside(p, q):
    rank = p.shape[1] // 2
    left = lax.broadcasted_iota(jnp.int32, p.shape, 1) < rank
    return jnp.concatenate(
        [
            jnp.where(left, p, pltpu.roll(q, rank, 1)),
            jnp.where(left, pltpu.roll(p, rank, 1), q),
        ],
        axis=0,
    )


def row_of(tiles):
    return jnp.concatenate([beside(*tiles[k : k + 2]) for k in range(0, len(tiles), 2)], axis=1)


def lane_gather(x, high, low):
    rows, columns = x.shape
    high = jnp.broadcast_to(high, (rows, LANES))
    low = jnp.broadcast_to(low, (rows, LANES))
    result = jnp.zeros((rows, LANES), x.dtype)
    for source in range(columns // LANES):
        tile = x[:, source * LANES : (source + 1) * LANES]
        moved = jnp.take_along_axis(tile, low, axis=1, mode="promise_in_bounds")
        result = jnp.where(high == source, moved, result)
    return result


def fetch(pairs, sems):
    copies = [
        pltpu.make_async_copy(source, target, sems.at[index])
        for index, (source, target) in enumerate(pairs)
    ]
    for copy in copies:
        copy.start()
    return copies


def up_kernel(
    me_ref, points_hbm, order_hbm, bases_hbm, lift_hbm, out, x_out, points_v, order_v, bases_v, lift_v, sems
):
    copies = fetch(
        [(order_hbm, order_v), (points_hbm, points_v), (bases_hbm, bases_v), (lift_hbm, lift_v)], sems
    )
    me = me_ref[0]
    leaf_dev, rank, leaf_size = bases_v.shape
    vectors, points_dev = points_v.shape
    copies[0].wait()
    copies[1].wait()
    points = points_v[...]
    per_leaf = leaf_size // LANES
    for t in range(points_dev // LANES):
        spot = order_v[t : t + 1, :] - me * points_dev
        column = t % per_leaf * LANES
        x_out[t // per_leaf, :, column : column + LANES] = lane_gather(
            points, lax.shift_right_logical(spot, 7), spot & (LANES - 1)
        )
    copies[2].wait()
    coefs = [dot3(x_out[leaf], bases_v[leaf], NT) for leaf in range(leaf_dev)]
    tiles = [fold(coef) for coef in coefs]
    copies[3].wait()
    weights = lift_v[...].reshape(leaf_dev * rank, rank)
    tiles.append(fold(dot3(jnp.concatenate(coefs, axis=1), weights, NN)))
    for peer in range(GROUP):
        for index, tile in enumerate(tiles):
            out[peer, index * TILE : (index + 1) * TILE, :] = tile
    place = lax.rem(me, GROUP)
    start = len(tiles) * TILE
    for part in range(per_leaf):
        first = x_out[0, :, part * LANES : (part + 1) * LANES]
        last = x_out[leaf_dev - 1, :, part * LANES : (part + 1) * LANES]
        rows = slice(start + part * vectors, start + (part + 1) * vectors)
        for peer in range(GROUP):
            above = lax.rem(place + 1, GROUP) == peer
            out[peer, rows, :] = jnp.where(above, last, first)


def side_kernel(me_ref, *refs):
    inputs, outputs = refs[:11], refs[11:25]
    held, results = refs[25:36], refs[36:50]
    sems, block_sems, out_sems = refs[50:]
    ids_s, links_s, transfer_v, couple_v, x_v, top_v, lift_v, order_v, far_v, bases_v, blocks_v = held
    (
        up_high,
        up_low,
        path_high,
        path_low,
        inverse_out,
        leaf_high,
        leaf_low,
        lift_high,
        lift_low,
        bases_high,
        bases_low,
        edge_high,
        edge_low,
        near_out,
    ) = results
    leaf_dev, slots, leaf_size, _ = blocks_v.shape
    rank = top_v.shape[0]
    pairs = leaf_dev // 2
    me = me_ref[0]
    first = fetch(list(zip(inputs[:8], held[:8])), sems)

    def block(pair):
        two = pl.ds(2 * pair, 2)
        return fetch([(inputs[10].at[two], blocks_v.at[two])], block_sems.at[pl.ds(pair, 1)])

    blocks = block(0)
    second = fetch(list(zip(inputs[8:10], held[8:10])), sems.at[pl.ds(8, 2)])
    for pair in range(1, pairs):
        blocks += block(pair)
    writes = []

    def write(*indices):
        for index in indices:
            writes.extend(fetch([(results[index], outputs[index])], out_sems.at[pl.ds(index, 1)]))

    def couplings(level):
        weights = [
            links_s[level, column].astype(F32) * couple_v[level, column]
            for column in range(len(OFFSETS))
        ]
        return jnp.concatenate(weights, axis=1)

    def chain():
        bits = [lax.shift_right_logical(me, level) & 1 for level in range(DEPTH)]
        up = transfer_v[0].reshape(2 * rank, rank)
        path = transfer_v[0, bits[0]]
        parts = [couplings(0)]
        row = 0
        for level in range(1, DEPTH):
            rows = up.shape[0]
            up_high[row : row + rows], up_low[row : row + rows] = halves(up)
            row += rows
            if level < DEPTH - 1:
                up = jnp.concatenate(
                    [dot3(up, transfer_v[level, side], NN) for side in range(2)], axis=0
                )
            parts.append(dot3(path, couplings(level), NN))
            path = dot3(path, transfer_v[level, bits[level]], NN)
            if level < DEPTH - 1:
                yield
        write(0, 1)
        top = dot3(path, top_v[...], NN)
        yield
        parts = [x[:, k * rank : (k + 1) * rank] for x in parts for k in range(len(OFFSETS))]
        parts += [dot3(top, transfer_v[DEPTH - 1, side], NT) for side in range(2)]
        half = len(parts) // 2
        for index in range(half):
            span = slice(index * rank, (index + 1) * rank)
            both = jnp.concatenate([parts[index], parts[half + index]], axis=0).T
            path_high[span], path_low[span] = halves(both)
        write(2, 3)

    def inverse():
        points_dev = order_v.shape[1]
        tiles = points_dev // LANES
        spot = order_v[...] - me * points_dev
        times = lax.broadcasted_iota(jnp.int32, (1, points_dev), 1)
        shape = (tiles, points_dev)
        match = lax.broadcasted_iota(jnp.int32, shape, 0) == lax.shift_right_logical(spot, 7)
        digits = [
            jnp.where(match, jnp.broadcast_to(digit.astype(F32), shape), 0.0)
            for digit in (lax.shift_right_logical(times, 4), times & 15)
        ]
        shape = (LANES, points_dev)
        match = lax.broadcasted_iota(jnp.int32, shape, 0) == (spot & (LANES - 1))
        both = lax.dot_general(
            jnp.concatenate(digits, axis=0).astype(BF16),
            jnp.where(match, 1.0, 0.0).astype(BF16),
            NT,
            preferred_element_type=F32,
        )
        inverse_out[...] = (both[:tiles] * 16.0 + both[tiles:]).astype(jnp.int32)
        write(4)

    def transposes(pair):
        two = range(2 * pair, 2 * pair + 2)
        for slot in range(far_v.shape[1]):
            span = slice(slot * rank, (slot + 1) * rank)
            both = jnp.concatenate([far_v[leaf, slot] for leaf in two], axis=0).T
            leaf_high[pair, span], leaf_low[pair, span] = halves(both)
        both = jnp.concatenate([lift_v[leaf] for leaf in two], axis=0).T
        lift_high[pair], lift_low[pair] = halves(both)
        bases_high[pair], bases_low[pair] = halves(bases_v[pair])

    def near(leaf):
        total = jnp.zeros(near_out.shape[1:], F32)
        for slot in range(slots):
            local = ids_s[slot, leaf] - me * leaf_dev
            here = (local >= 0) & (local < leaf_dev)
            x_leaf = jnp.where(here, x_v[jnp.clip(local, 0, leaf_dev - 1)], 0.0)
            total = total + dot3(x_leaf, blocks_v[leaf, slot], NT)
        near_out[leaf] = total

    def edge(index, leaf, outside):
        total = jnp.zeros((leaf_size, leaf_size), F32)
        for slot in range(1, slots):
            remote = ids_s[slot, leaf] - me * leaf_dev == outside
            total = total + jnp.where(remote, blocks_v[leaf, slot], 0.0)
        edge_high[index], edge_low[index] = halves(total.T)

    for copy in first:
        copy.wait()
    links = chain()
    next(links)
    for pair in range(pairs):
        blocks[pair].wait()
        if pair == 0:
            for copy in second:
                copy.wait()
        near(2 * pair)
        near(2 * pair + 1)
        transposes(pair)
        next(links, None)
        if pair == 0:
            edge(0, 0, -1)
        if pair == 1:
            inverse()
        if pair == pairs - 1:
            edge(1, leaf_dev - 1, leaf_dev)
    for _ in links:
        pass
    write(*range(5, 14))
    for copy in writes:
        copy.wait()


def middle_kernel(
    leaf_dev,
    me_ref,
    group_hbm,
    up_high_hbm,
    up_low_hbm,
    near_half,
    far_half,
    nodes_out,
    far_out,
    roots_v,
    up_high,
    up_low,
    sems,
    half_sems,
):
    low = lax.rem(me_ref[0], GROUP) < REACH
    copies = fetch(
        [
            (group_hbm.at[:, pl.ds(leaf_dev * TILE, TILE), :], roots_v),
            (up_high_hbm, up_high),
            (up_low_hbm, up_low),
        ],
        sems,
    )
    rows = (leaf_dev + 1) * TILE
    edge_rows = group_hbm.shape[1] - rows
    count = REACH // 2
    moves = [
        (group_hbm.at[first + part, pl.ds(0, rows)], half.at[pl.ds(part * rows, rows)])
        for half, first in (
            (near_half, jnp.where(low, GROUP - count, 0)),
            (far_half, jnp.where(low, count, REACH)),
        )
        for part in range(count)
    ]
    moves.append(
        (
            group_hbm.at[jnp.where(low, GROUP - 1, 0), pl.ds(rows, edge_rows)],
            near_half.at[pl.ds(count * rows, edge_rows)],
        )
    )
    moves = fetch(moves, half_sems)
    for copy in copies:
        copy.wait()
    roots = [roots_v[peer] for peer in range(GROUP)]
    start, tiles = 0, []
    for level in range(1, DEPTH):
        width = 1 << level
        some = GROUP // width
        left = jnp.concatenate(
            [row_of(roots[n * width : (n + 1) * width]) for n in range(some)], axis=0
        )
        size = left.shape[1]
        nodes = dot_halves(left, up_high[start : start + size], up_low[start : start + size], NN)
        start += size
        tiles += [fold(nodes[n * 2 * TILE : (n + 1) * 2 * TILE]) for n in range(some)]
    row = count * rows + edge_rows
    for index, tile in enumerate(tiles):
        near_half[row + index * TILE : row + (index + 1) * TILE, :] = tile
        for peer in range(nodes_out.shape[0]):
            nodes_out[peer, index] = tile
    for index in range(3):
        far_out[index] = tiles[NODES - 3 + index]
    for copy in moves:
        copy.wait()


def down_kernel(parts, me_ref, *refs):
    halves_hbm, node_parts, refs = refs[:2], refs[2 : 2 + parts], refs[2 + parts :]
    count = (len(refs) - 7) // 2
    out_ref = refs[count]
    held = refs[count + 1 : 2 * count + 1]
    nodes_ref, half_ref, y_tree, sems, node_sems, half_sems = refs[2 * count + 1 :]
    me = me_ref[0]
    groups = nodes_ref.shape[0]
    group = lax.shift_right_logical(me, 3)
    place = me & (GROUP - 1)
    low = place < REACH
    if parts > 1:
        near_by, far_by = jnp.where(low, groups - 1, 1), jnp.where(low, 1, groups - 1)
        across = lax.rem(group + 2, groups)
        near_group = lax.rem(group + near_by, groups)
        node_copies = fetch(
            [
                (node_parts[0].at[0], nodes_ref.at[group]),
                (node_parts[1].at[0], nodes_ref.at[lax.rem(group + far_by, groups)]),
                (node_parts[2], nodes_ref.at[across, pl.ds(NODES - 3, 3)]),
            ],
            node_sems,
        )
    else:
        node_copies = fetch([(node_parts[0], nodes_ref)], node_sems)
    quarter = halves_hbm[1].shape[0]
    near_start = pl.multiple_of(jnp.where(low, quarter, 0), TILE)
    rest = halves_hbm[0].shape[0] - quarter
    node_copies += fetch(
        [
            (halves_hbm[0].at[pl.ds(0, quarter)], half_ref.at[pl.ds(near_start, quarter)]),
            (halves_hbm[1], half_ref.at[pl.ds(pl.multiple_of(quarter - near_start, TILE), quarter)]),
            (halves_hbm[0].at[pl.ds(quarter, rest)], half_ref.at[pl.ds(2 * quarter, rest)]),
        ],
        half_sems,
    )
    copies = fetch(list(zip(refs[:count], held)), sems)
    (
        group_ref,
        far_ids_s,
        far_count_s,
        path_high,
        path_low,
        leaf_high,
        leaf_low,
        lift_high,
        lift_low,
        edge_high,
        edge_low,
        bases_high,
        bases_low,
        near_ref,
        inverse_ref,
    ) = held
    leaf_dev, vectors, leaf_size = near_ref.shape
    points_dev = out_ref.shape[1]
    slots = far_ids_s.shape[1]
    per_leaf = leaf_size // LANES
    rank = bases_high.shape[1] // 2
    start = (leaf_dev + 1) * TILE
    edge_rows = group_ref.shape[1] - start

    def tile_of(subtree, index):
        other = subtree & (GROUP - 1)
        inside = lax.shift_right_arithmetic(subtree, 3) == group
        row = pl.multiple_of(index * TILE, TILE)
        near_row = jnp.clip(other - jnp.where(low, REACH, 0), 0, REACH - 1) * start
        here = group_ref[other, pl.ds(row, TILE), :]
        there = half_ref[pl.ds(pl.multiple_of(near_row + row, TILE), TILE), :]
        return jnp.where(inside, here, there)

    for copy in node_copies + copies[:5]:
        copy.wait()
    if parts > 1:
        for index in range(NODES):
            row = half_ref.shape[0] - (NODES - index) * TILE
            tile = half_ref[row : row + TILE, :]
            nodes_ref[near_group, index] = tile
    partners = []
    for level in range(DEPTH):
        node = lax.shift_right_logical(me, level)
        size = (groups * GROUP) >> level
        for offset in OFFSETS:
            other = node + offset
            used = (other >= 0) & (other < size)
            other = jnp.clip(other, 0, size - 1)
            if level == 0:
                tile = tile_of(other, leaf_dev)
            else:
                shift = DEPTH - 1 - level
                first = GROUP - (2 << shift)
                tile = nodes_ref[
                    lax.shift_right_logical(other, shift), first + (other & ((1 << shift) - 1))
                ]
            partners.append(jnp.where(used, tile, 0.0))
    top = lax.shift_right_logical(me, DEPTH)
    for side in range(2):
        blended = jnp.zeros((TILE, LANES), F32)
        for other in range(groups // 2):
            distance = jnp.abs(top - other)
            weight = jnp.where(distance >= 2, 1.0 / jnp.maximum(distance, 1).astype(F32), 0.0)
            blended = blended + weight * nodes_ref[2 * other + side, GROUP - 2]
        partners.append(blended)
    half = len(partners) // 2
    row = row_of(partners)
    first, second = pair_dot(
        row[:, : half * rank], row[:, half * rank :], path_high[...], path_low[...]
    )
    down = first[:, :rank] + second[:, rank:]

    rows = []
    for leaf in range(leaf_dev):
        picked = []
        for slot in range(slots):
            used = slot < far_count_s[leaf]
            spot = far_ids_s[leaf, slot]
            tile = tile_of(lax.shift_right_logical(spot, 3), spot & (leaf_dev - 1))
            picked.append(jnp.where(used, tile, 0.0))
        rows.append(row_of(picked))
    edges = []
    for offset in (-1, 1):
        other = me + offset
        inside = lax.shift_right_arithmetic(other, 3) == group
        here = group_ref[other & (GROUP - 1), start:, :]
        chosen = jnp.where(inside, here, half_ref[REACH * start : REACH * start + edge_rows, :])
        edges.append(
            jnp.concatenate(
                [chosen[part * vectors : (part + 1) * vectors] for part in range(per_leaf)], axis=1
            )
        )

    for copy in copies[5:]:
        copy.wait()
    edge_parts = [
        dot_halves(edges[index], edge_high[index], edge_low[index], NN) for index in range(2)
    ]
    left_half = lax.broadcasted_iota(jnp.int32, (vectors, 2 * rank), 1) < rank
    for pair in range(leaf_dev // 2):
        two = (2 * pair, 2 * pair + 1)
        first, second = pair_dot(rows[two[0]], rows[two[1]], leaf_high[pair], leaf_low[pair])
        lift = dot_halves(down, lift_high[pair], lift_low[pair], NN)
        first = jnp.where(left_half, first + lift, 0.0)
        second = jnp.where(left_half, 0.0, second + lift)
        products = pair_dot(first, second, bases_high[pair], bases_low[pair])
        for leaf, product in zip(two, products):
            y_leaf = near_ref[leaf] + product
            if leaf == 0:
                y_leaf = y_leaf + edge_parts[0]
            if leaf == leaf_dev - 1:
                y_leaf = y_leaf + edge_parts[1]
            y_tree[:, leaf * leaf_size : (leaf + 1) * leaf_size] = y_leaf

    y = y_tree[...]
    for tile in range(points_dev // LANES):
        spot = inverse_ref[tile : tile + 1, :]
        out_ref[:, tile * LANES : (tile + 1) * LANES] = lane_gather(
            y, lax.shift_right_logical(spot, 7), spot & (LANES - 1)
        )


def local(
    devices,
    points,
    order,
    bases,
    lift,
    near_ids,
    near_blocks,
    far_ids,
    far_count,
    far_blocks,
    transfer,
    couple,
    links,
    top_couple,
):
    me = lax.axis_index("leaf").astype(jnp.int32).reshape(1)
    vectors, points_dev = points.shape
    leaf_dev, leaf_size, rank = bases.shape
    slots = near_ids.shape[1]
    far_slots = far_ids.shape[1]
    bases_t = jnp.swapaxes(bases, 1, 2)
    tiles = points_dev // LANES
    edge_rows = vectors * (leaf_size // LANES)
    rows = (leaf_dev + 1) * TILE
    groups = devices // GROUP
    order_tiles = order.reshape(tiles, LANES)
    shape = jax.ShapeDtypeStruct

    group_out, tree_x = pl.pallas_call(
        up_kernel,
        out_shape=[
            shape((GROUP, rows + edge_rows, LANES), F32),
            shape((leaf_dev, vectors, leaf_size), F32),
        ],
        in_specs=[SMEM] + [HBM] * 4,
        out_specs=[VMEM] * 2,
        scratch_shapes=[
            pltpu.VMEM(points.shape, F32),
            pltpu.VMEM((tiles, LANES), jnp.int32),
            pltpu.VMEM(bases_t.shape, F32),
            pltpu.VMEM(lift.shape, F32),
            pltpu.SemaphoreType.DMA((4,)),
        ],
        compiler_params=PARAMS,
        name="up",
    )(me, points, order_tiles, bases_t, lift)

    aligned = [[g * GROUP + i for i in range(GROUP)] for g in range(groups)]
    group_in = lax.all_to_all(group_out, "leaf", 0, 0, axis_index_groups=aligned, tiled=True)

    ids_t = near_ids.T
    both = lambda *size: [shape(size, BF16)] * 2

    links_own = links.reshape(links.shape[1:])
    path_rows = (DEPTH * len(OFFSETS) + 2) // 2 * rank
    operands = (
        ids_t,
        links_own,
        transfer,
        couple,
        tree_x,
        top_couple,
        lift,
        order.reshape(1, points_dev),
        far_blocks,
        bases_t.reshape(leaf_dev // 2, 2 * rank, leaf_size),
        near_blocks,
    )
    results = (
        both(14 * rank, rank)
        + both(path_rows, 2 * rank)
        + [shape((tiles, LANES), jnp.int32)]
        + both(leaf_dev // 2, far_slots * rank, 2 * rank)
        + both(leaf_dev // 2, rank, 2 * rank)
        + both(leaf_dev // 2, 2 * rank, leaf_size)
        + both(2, leaf_size, leaf_size)
        + [shape(tree_x.shape, F32)]
    )
    (
        up_high,
        up_low,
        path_high,
        path_low,
        inverse,
        leaf_high,
        leaf_low,
        lift_high,
        lift_low,
        bases_high,
        bases_low,
        edge_high,
        edge_low,
        near_part,
    ) = pl.pallas_call(
        side_kernel,
        out_shape=results,
        in_specs=[SMEM] + [HBM] * len(operands),
        out_specs=[HBM] * len(results),
        scratch_shapes=[
            (pltpu.SMEM if x is ids_t or x is links_own else pltpu.VMEM)(x.shape, x.dtype)
            for x in operands
        ]
        + [pltpu.VMEM(x.shape, x.dtype) for x in results]
        + [
            pltpu.SemaphoreType.DMA((10,)),
            pltpu.SemaphoreType.DMA((leaf_dev // 2,)),
            pltpu.SemaphoreType.DMA((len(results),)),
        ],
        compiler_params=PARAMS,
        cost_estimate=pl.CostEstimate(
            flops=250 * 12_000_000, bytes_accessed=12_000_000, transcendentals=0
        ),
        name="side",
    )(me, *operands)

    by_permute = groups == 4
    near_half, far_half, nodes_out, far_nodes = pl.pallas_call(
        functools.partial(middle_kernel, leaf_dev),
        out_shape=[
            shape((REACH // 2 * rows + edge_rows + NODES * TILE, LANES), F32),
            shape((REACH // 2 * rows, LANES), F32),
            shape((1 if by_permute else groups, NODES, TILE, LANES), F32),
            shape((3, TILE, LANES), F32),
        ],
        in_specs=[SMEM] + [HBM] * 3,
        out_specs=[VMEM] * 4,
        scratch_shapes=[
            pltpu.VMEM((GROUP, TILE, LANES), F32),
            pltpu.VMEM(up_high.shape, BF16),
            pltpu.VMEM(up_low.shape, BF16),
            pltpu.SemaphoreType.DMA((3,)),
            pltpu.SemaphoreType.DMA((REACH + 1,)),
        ],
        compiler_params=PARAMS,
        name="middle",
    )(me, group_in, up_high, up_low)

    def shifted(x, low, high):
        pairs = []
        for device in range(devices):
            by = low if device % GROUP < REACH else high
            pairs.append(((device + by * GROUP) % devices, device))
        return lax.ppermute(x, "leaf", pairs)

    half_in = shifted(near_half, -1, 1)
    pairs = []
    for device in range(devices):
        side = -1 if device % GROUP < REACH else 1
        if 0 <= device // GROUP + side < groups:
            pairs.append((device + side * (GROUP - REACH), device))
    quarter_in = lax.ppermute(far_half, "leaf", pairs)
    if by_permute:
        node_parts = (nodes_out, shifted(nodes_out, 1, -1), shifted(far_nodes, 2, 2))
    else:
        across = [[g * GROUP + i for g in range(groups)] for i in range(GROUP)]
        node_parts = (lax.all_to_all(nodes_out, "leaf", 0, 0, axis_index_groups=across, tiled=True),)

    operands = (
        group_in,
        far_ids,
        far_count,
        path_high,
        path_low,
        leaf_high,
        leaf_low,
        lift_high,
        lift_low,
        edge_high,
        edge_low,
        bases_high,
        bases_low,
        near_part,
        inverse,
    )
    return pl.pallas_call(
        functools.partial(down_kernel, len(node_parts)),
        out_shape=shape((vectors, points_dev), F32),
        in_specs=[SMEM] + [HBM] * (2 + len(node_parts) + len(operands)),
        out_specs=VMEM,
        scratch_shapes=[
            (pltpu.SMEM if x is far_ids or x is far_count else pltpu.VMEM)(x.shape, x.dtype)
            for x in operands
        ]
        + [
            pltpu.VMEM((groups, NODES, TILE, LANES), F32),
            pltpu.VMEM((half_in.shape[0] + quarter_in.shape[0], LANES), F32),
            pltpu.VMEM((vectors, points_dev), F32),
            pltpu.SemaphoreType.DMA((len(operands),)),
            pltpu.SemaphoreType.DMA((3,)),
            pltpu.SemaphoreType.DMA((3,)),
        ],
        compiler_params=PARAMS,
        name="down",
    )(me, half_in, quarter_in, *node_parts, *operands)


def solution(mesh):
    in_specs = (
        P(None, "leaf"),
        P("leaf"),
        P("leaf", None, None),
        P("leaf", None, None),
        P("leaf", None),
        P("leaf", None, None, None),
        P("leaf", None),
        P("leaf"),
        P("leaf", None, None, None),
        P(),
        P(),
        P("leaf", None, None),
        P(),
    )
    return jax.shard_map(
        functools.partial(local, mesh.shape["leaf"]),
        mesh=mesh,
        in_specs=in_specs,
        out_specs=P(None, "leaf"),
        check_vma=False,
    )
```

```python
import functools

import jax
import jax.numpy as jnp
from jax import lax
from jax.experimental import pallas as pl
from jax.experimental.pallas import tpu as pltpu
from jax.sharding import PartitionSpec as P

REACH = 4
DEPTH = 4
OFFSETS = (-3, -2, 2, 3)
GROUP = 2 * REACH
LANES = 128
TILE = 8
NODES = GROUP - 1
VMEM_LIMIT = 64 * 1024 * 1024

NN = (((1,), (0,)), ((), ()))
NT = (((1,), (1,)), ((), ()))

VMEM = pl.BlockSpec(memory_space=pltpu.VMEM)
SMEM = pl.BlockSpec(memory_space=pltpu.SMEM)
HBM = pl.BlockSpec(memory_space=pltpu.HBM)
PARAMS = pltpu.CompilerParams(vmem_limit_bytes=VMEM_LIMIT)
F32 = jnp.float32
BF16 = jnp.bfloat16


def halves(x):
    high = x.astype(BF16)
    low = (x - high.astype(F32)).astype(BF16)
    return high, low


def dot_halves(a, b_high, b_low, dims):
    a_high, a_low = halves(a)
    rows = a.shape[0]
    both = lax.dot_general(
        jnp.concatenate([a_high, a_low], axis=0), b_high, dims, preferred_element_type=F32
    )
    cross = lax.dot_general(a_high, b_low, dims, preferred_element_type=F32)
    return both[:rows] + (both[rows:] + cross)


def pair_dot(a, b, w_high, w_low):
    a_high, a_low = halves(a)
    b_high, b_low = halves(b)
    rows = a.shape[0]
    both = lax.dot_general(
        jnp.concatenate([a_high, b_high, a_low, b_low], axis=0),
        w_high,
        NN,
        preferred_element_type=F32,
    )
    cross = lax.dot_general(
        jnp.concatenate([a_high, b_high], axis=0), w_low, NN, preferred_element_type=F32
    )
    total = both[: 2 * rows] + (both[2 * rows :] + cross)
    return total[:rows], total[rows:]


def dot3(a, b, dims):
    return dot_halves(a, *halves(b), dims)


def fold(x):
    return jnp.concatenate([x[:TILE], x[TILE:]], axis=1)


def beside(p, q):
    rank = p.shape[1] // 2
    left = lax.broadcasted_iota(jnp.int32, p.shape, 1) < rank
    return jnp.concatenate(
        [
            jnp.where(left, p, pltpu.roll(q, rank, 1)),
            jnp.where(left, pltpu.roll(p, rank, 1), q),
        ],
        axis=0,
    )


def row_of(tiles):
    return jnp.concatenate([beside(*tiles[k : k + 2]) for k in range(0, len(tiles), 2)], axis=1)


def lane_gather(x, high, low):
    rows, columns = x.shape
    high = jnp.broadcast_to(high, (rows, LANES))
    low = jnp.broadcast_to(low, (rows, LANES))
    result = jnp.zeros((rows, LANES), x.dtype)
    for source in range(columns // LANES):
        tile = x[:, source * LANES : (source + 1) * LANES]
        moved = jnp.take_along_axis(tile, low, axis=1, mode="promise_in_bounds")
        result = jnp.where(high == source, moved, result)
    return result


def fetch(pairs, sems):
    copies = [
        pltpu.make_async_copy(source, target, sems.at[index])
        for index, (source, target) in enumerate(pairs)
    ]
    for copy in copies:
        copy.start()
    return copies


def up_kernel(
    me_ref,
    points_hbm,
    order_hbm,
    bases_hbm,
    lift_hbm,
    out_hbm,
    x_hbm,
    points_v,
    order_v,
    bases_v,
    lift_v,
    x_v,
    tiles_v,
    edges_v,
    sems,
    edge_sems,
    tile_sems,
):
    copies = fetch(
        [(order_hbm, order_v), (points_hbm, points_v), (bases_hbm, bases_v), (lift_hbm, lift_v)],
        sems,
    )
    me = me_ref[0]
    leaf_dev, rank, leaf_size = bases_v.shape
    vectors, points_dev = points_v.shape
    copies[0].wait()
    copies[1].wait()
    points = points_v[...]
    per_leaf = leaf_size // LANES
    for t in range(points_dev // LANES):
        spot = order_v[t : t + 1, :] - me * points_dev
        column = t % per_leaf * LANES
        x_v[t // per_leaf, :, column : column + LANES] = lane_gather(
            points, lax.shift_right_logical(spot, 7), spot & (LANES - 1)
        )
    for index, leaf in enumerate((0, leaf_dev - 1)):
        for part in range(per_leaf):
            edges_v[index, part * vectors : (part + 1) * vectors, :] = x_v[
                leaf, :, part * LANES : (part + 1) * LANES
            ]
    rows = tiles_v.shape[0]
    above = lax.rem(me + 1, GROUP)
    writes = fetch([(x_v, x_hbm)], sems.at[pl.ds(4, 1)])
    writes += fetch(
        [
            (
                edges_v.at[jnp.where(above == peer, 1, 0)],
                out_hbm.at[peer, pl.ds(rows, edges_v.shape[1])],
            )
            for peer in range(GROUP)
        ],
        edge_sems,
    )
    copies[2].wait()
    coefs = [dot3(x_v[leaf], bases_v[leaf], NT) for leaf in range(leaf_dev)]
    copies[3].wait()
    weights = lift_v[...].reshape(leaf_dev * rank, rank)
    root = dot3(jnp.concatenate(coefs, axis=1), weights, NN)
    for index, matrix in enumerate(coefs + [root]):
        tiles_v[index * TILE : (index + 1) * TILE, :] = fold(matrix)
    writes += fetch(
        [(tiles_v, out_hbm.at[peer, pl.ds(0, rows)]) for peer in range(GROUP)], tile_sems
    )
    for copy in writes:
        copy.wait()


def side_kernel(me_ref, *refs):
    inputs, outputs = refs[:11], refs[11:25]
    held, results = refs[25:36], refs[36:50]
    sems, block_sems, out_sems = refs[50:]
    ids_s, links_s, transfer_v, couple_v, x_v, top_v, lift_v, order_v, far_v, bases_v, blocks_v = held
    (
        up_high,
        up_low,
        path_high,
        path_low,
        inverse_out,
        leaf_high,
        leaf_low,
        lift_high,
        lift_low,
        bases_high,
        bases_low,
        edge_high,
        edge_low,
        near_out,
    ) = results
    leaf_dev, slots, leaf_size, _ = blocks_v.shape
    rank = top_v.shape[0]
    pairs = leaf_dev // 2
    me = me_ref[0]
    first = fetch(list(zip(inputs[:8], held[:8])), sems)

    def block(pair):
        two = pl.ds(2 * pair, 2)
        return fetch([(inputs[10].at[two], blocks_v.at[two])], block_sems.at[pl.ds(pair, 1)])

    blocks = block(0)
    second = fetch(list(zip(inputs[8:10], held[8:10])), sems.at[pl.ds(8, 2)])
    for pair in range(1, pairs):
        blocks += block(pair)
    writes = []

    def write(*indices):
        for index in indices:
            writes.extend(fetch([(results[index], outputs[index])], out_sems.at[pl.ds(index, 1)]))

    def couplings(level):
        weights = [
            links_s[level, column].astype(F32) * couple_v[level, column]
            for column in range(len(OFFSETS))
        ]
        return jnp.concatenate(weights, axis=1)

    def chain():
        bits = [lax.shift_right_logical(me, level) & 1 for level in range(DEPTH)]
        up = transfer_v[0].reshape(2 * rank, rank)
        path = transfer_v[0, bits[0]]
        parts = [couplings(0)]
        row = 0
        for level in range(1, DEPTH):
            rows = up.shape[0]
            up_high[row : row + rows], up_low[row : row + rows] = halves(up)
            row += rows
            if level < DEPTH - 1:
                up = jnp.concatenate(
                    [dot3(up, transfer_v[level, side], NN) for side in range(2)], axis=0
                )
            parts.append(dot3(path, couplings(level), NN))
            path = dot3(path, transfer_v[level, bits[level]], NN)
            if level < DEPTH - 1:
                yield
        write(0, 1)
        top = dot3(path, top_v[...], NN)
        yield
        parts = [x[:, k * rank : (k + 1) * rank] for x in parts for k in range(len(OFFSETS))]
        parts += [dot3(top, transfer_v[DEPTH - 1, side], NT) for side in range(2)]
        half = len(parts) // 2
        for index in range(half):
            span = slice(index * rank, (index + 1) * rank)
            both = jnp.concatenate([parts[index], parts[half + index]], axis=0).T
            path_high[span], path_low[span] = halves(both)
        write(2, 3)

    def inverse():
        points_dev = order_v.shape[1]
        tiles = points_dev // LANES
        spot = order_v[...] - me * points_dev
        times = lax.broadcasted_iota(jnp.int32, (1, points_dev), 1)
        shape = (tiles, points_dev)
        match = lax.broadcasted_iota(jnp.int32, shape, 0) == lax.shift_right_logical(spot, 7)
        digits = [
            jnp.where(match, jnp.broadcast_to(digit.astype(F32), shape), 0.0)
            for digit in (lax.shift_right_logical(times, 4), times & 15)
        ]
        shape = (LANES, points_dev)
        match = lax.broadcasted_iota(jnp.int32, shape, 0) == (spot & (LANES - 1))
        both = lax.dot_general(
            jnp.concatenate(digits, axis=0).astype(BF16),
            jnp.where(match, 1.0, 0.0).astype(BF16),
            NT,
            preferred_element_type=F32,
        )
        inverse_out[...] = (both[:tiles] * 16.0 + both[tiles:]).astype(jnp.int32)
        write(4)

    def transposes(pair):
        two = range(2 * pair, 2 * pair + 2)
        for slot in range(far_v.shape[1]):
            span = slice(slot * rank, (slot + 1) * rank)
            both = jnp.concatenate([far_v[leaf, slot] for leaf in two], axis=0).T
            leaf_high[pair, span], leaf_low[pair, span] = halves(both)
        both = jnp.concatenate([lift_v[leaf] for leaf in two], axis=0).T
        lift_high[pair], lift_low[pair] = halves(both)
        bases_high[pair], bases_low[pair] = halves(bases_v[pair])

    def near(leaf):
        total = jnp.zeros(near_out.shape[1:], F32)
        for slot in range(slots):
            local = ids_s[slot, leaf] - me * leaf_dev
            here = (local >= 0) & (local < leaf_dev)
            x_leaf = jnp.where(here, x_v[jnp.clip(local, 0, leaf_dev - 1)], 0.0)
            total = total + dot3(x_leaf, blocks_v[leaf, slot], NT)
        near_out[leaf] = total

    def edge(index, leaf, outside):
        total = jnp.zeros((leaf_size, leaf_size), F32)
        for slot in range(1, slots):
            remote = ids_s[slot, leaf] - me * leaf_dev == outside
            total = total + jnp.where(remote, blocks_v[leaf, slot], 0.0)
        edge_high[index], edge_low[index] = halves(total.T)

    for copy in first:
        copy.wait()
    links = chain()
    next(links)
    for pair in range(pairs):
        blocks[pair].wait()
        if pair == 0:
            for copy in second:
                copy.wait()
        near(2 * pair)
        near(2 * pair + 1)
        transposes(pair)
        next(links, None)
        if pair == 0:
            edge(0, 0, -1)
        if pair == 1:
            inverse()
        if pair == pairs - 1:
            edge(1, leaf_dev - 1, leaf_dev)
    for _ in links:
        pass
    write(*range(5, 14))
    for copy in writes:
        copy.wait()


def middle_kernel(
    leaf_dev,
    me_ref,
    group_hbm,
    up_high_hbm,
    up_low_hbm,
    half_hbm,
    nodes_out,
    far_out,
    roots_v,
    up_high,
    up_low,
    half_out,
    sems,
    half_sems,
    out_sems,
):
    low = lax.rem(me_ref[0], GROUP) < REACH
    copies = fetch(
        [
            (group_hbm.at[:, pl.ds(leaf_dev * TILE, TILE), :], roots_v),
            (up_high_hbm, up_high),
            (up_low_hbm, up_low),
        ],
        sems,
    )
    rows = (leaf_dev + 1) * TILE
    edge_rows = group_hbm.shape[1] - rows
    first = jnp.where(low, REACH, 0)
    moves = [
        (group_hbm.at[first + part, pl.ds(0, rows)], half_out.at[pl.ds(part * rows, rows)])
        for part in range(REACH)
    ]
    moves.append(
        (
            group_hbm.at[jnp.where(low, GROUP - 1, 0), pl.ds(rows, edge_rows)],
            half_out.at[pl.ds(REACH * rows, edge_rows)],
        )
    )
    moves = fetch(moves, half_sems)
    for copy in moves + copies:
        copy.wait()
    row = REACH * rows + edge_rows
    writes = fetch([(half_out.at[pl.ds(0, row)], half_hbm.at[pl.ds(0, row)])], out_sems)
    roots = [roots_v[peer] for peer in range(GROUP)]
    start, tiles = 0, []
    for level in range(1, DEPTH):
        width = 1 << level
        count = GROUP // width
        left = jnp.concatenate(
            [row_of(roots[n * width : (n + 1) * width]) for n in range(count)], axis=0
        )
        size = left.shape[1]
        nodes = dot_halves(left, up_high[start : start + size], up_low[start : start + size], NN)
        start += size
        tiles += [fold(nodes[n * 2 * TILE : (n + 1) * 2 * TILE]) for n in range(count)]
    for index, tile in enumerate(tiles):
        half_out[row + index * TILE : row + (index + 1) * TILE, :] = tile
        for peer in range(nodes_out.shape[0]):
            nodes_out[peer, index] = tile
    for index in range(3):
        far_out[index] = tiles[NODES - 3 + index]
    span = pl.ds(row, NODES * TILE)
    writes += fetch([(half_out.at[span], half_hbm.at[span])], out_sems.at[pl.ds(1, 1)])
    for copy in writes:
        copy.wait()


def down_kernel(parts, me_ref, *refs):
    node_parts, refs = refs[:parts], refs[parts:]
    count = (len(refs) - 7) // 2
    out_ref = refs[count]
    held = refs[count + 1 : 2 * count + 1]
    nodes_ref, y_tree, out_v, sems, node_sems, out_sems = refs[2 * count + 1 :]
    me = me_ref[0]
    groups = nodes_ref.shape[0]
    group = lax.shift_right_logical(me, 3)
    place = me & (GROUP - 1)
    low = place < REACH
    if parts > 1:
        near_by, far_by = jnp.where(low, groups - 1, 1), jnp.where(low, 1, groups - 1)
        across = lax.rem(group + 2, groups)
        near_group = lax.rem(group + near_by, groups)
        node_copies = fetch(
            [
                (node_parts[0].at[0], nodes_ref.at[group]),
                (node_parts[1].at[0], nodes_ref.at[lax.rem(group + far_by, groups)]),
                (node_parts[2], nodes_ref.at[across, pl.ds(NODES - 3, 3)]),
            ],
            node_sems,
        )
    else:
        node_copies = fetch([(node_parts[0], nodes_ref)], node_sems)
    copies = fetch(list(zip(refs[:count], held)), sems)
    (
        group_ref,
        half_ref,
        far_ids_s,
        far_count_s,
        path_high,
        path_low,
        leaf_high,
        leaf_low,
        lift_high,
        lift_low,
        edge_high,
        edge_low,
        bases_high,
        bases_low,
        near_ref,
        inverse_ref,
    ) = held
    leaf_dev, vectors, leaf_size = near_ref.shape
    points_dev = out_ref.shape[1]
    slots = far_ids_s.shape[1]
    per_leaf = leaf_size // LANES
    rank = bases_high.shape[1] // 2
    start = (leaf_dev + 1) * TILE
    edge_rows = group_ref.shape[1] - start

    def tile_of(subtree, index):
        other = subtree & (GROUP - 1)
        inside = lax.shift_right_arithmetic(subtree, 3) == group
        row = pl.multiple_of(index * TILE, TILE)
        near_row = jnp.clip(other - jnp.where(low, REACH, 0), 0, REACH - 1) * start
        here = group_ref[other, pl.ds(row, TILE), :]
        there = half_ref[pl.ds(pl.multiple_of(near_row + row, TILE), TILE), :]
        return jnp.where(inside, here, there)

    for copy in node_copies + copies[:6]:
        copy.wait()
    if parts > 1:
        for index in range(NODES):
            row = half_ref.shape[0] - (NODES - index) * TILE
            tile = half_ref[row : row + TILE, :]
            nodes_ref[near_group, index] = tile
    partners = []
    for level in range(DEPTH):
        node = lax.shift_right_logical(me, level)
        size = (groups * GROUP) >> level
        for offset in OFFSETS:
            other = node + offset
            used = (other >= 0) & (other < size)
            other = jnp.clip(other, 0, size - 1)
            if level == 0:
                tile = tile_of(other, leaf_dev)
            else:
                shift = DEPTH - 1 - level
                first = GROUP - (2 << shift)
                tile = nodes_ref[
                    lax.shift_right_logical(other, shift), first + (other & ((1 << shift) - 1))
                ]
            partners.append(jnp.where(used, tile, 0.0))
    top = lax.shift_right_logical(me, DEPTH)
    for side in range(2):
        blended = jnp.zeros((TILE, LANES), F32)
        for other in range(groups // 2):
            distance = jnp.abs(top - other)
            weight = jnp.where(distance >= 2, 1.0 / jnp.maximum(distance, 1).astype(F32), 0.0)
            blended = blended + weight * nodes_ref[2 * other + side, GROUP - 2]
        partners.append(blended)
    half = len(partners) // 2
    row = row_of(partners)
    first, second = pair_dot(
        row[:, : half * rank], row[:, half * rank :], path_high[...], path_low[...]
    )
    down = first[:, :rank] + second[:, rank:]

    rows = []
    for leaf in range(leaf_dev):
        picked = []
        for slot in range(slots):
            used = slot < far_count_s[leaf]
            spot = far_ids_s[leaf, slot]
            tile = tile_of(lax.shift_right_logical(spot, 3), spot & (leaf_dev - 1))
            picked.append(jnp.where(used, tile, 0.0))
        rows.append(row_of(picked))
    edges = []
    for offset in (-1, 1):
        other = me + offset
        inside = lax.shift_right_arithmetic(other, 3) == group
        here = group_ref[other & (GROUP - 1), start:, :]
        chosen = jnp.where(inside, here, half_ref[REACH * start : REACH * start + edge_rows, :])
        edges.append(
            jnp.concatenate(
                [chosen[part * vectors : (part + 1) * vectors] for part in range(per_leaf)], axis=1
            )
        )

    for copy in copies[6:]:
        copy.wait()
    edge_parts = [
        dot_halves(edges[index], edge_high[index], edge_low[index], NN) for index in range(2)
    ]
    left_half = lax.broadcasted_iota(jnp.int32, (vectors, 2 * rank), 1) < rank
    for pair in range(leaf_dev // 2):
        two = (2 * pair, 2 * pair + 1)
        first, second = pair_dot(rows[two[0]], rows[two[1]], leaf_high[pair], leaf_low[pair])
        lift = dot_halves(down, lift_high[pair], lift_low[pair], NN)
        first = jnp.where(left_half, first + lift, 0.0)
        second = jnp.where(left_half, 0.0, second + lift)
        products = pair_dot(first, second, bases_high[pair], bases_low[pair])
        for leaf, product in zip(two, products):
            y_leaf = near_ref[leaf] + product
            if leaf == 0:
                y_leaf = y_leaf + edge_parts[0]
            if leaf == leaf_dev - 1:
                y_leaf = y_leaf + edge_parts[1]
            y_tree[:, leaf * leaf_size : (leaf + 1) * leaf_size] = y_leaf

    y = y_tree[...]
    writes = []
    tiles = points_dev // LANES
    for tile in range(tiles):
        spot = inverse_ref[tile : tile + 1, :]
        out_v[:, tile * LANES : (tile + 1) * LANES] = lane_gather(
            y, lax.shift_right_logical(spot, 7), spot & (LANES - 1)
        )
        if (tile + 1) % (tiles // 4) == 0:
            span = pl.ds((tile + 1 - tiles // 4) * LANES, tiles // 4 * LANES)
            sem = out_sems.at[pl.ds(len(writes), 1)]
            writes += fetch([(out_v.at[:, span], out_ref.at[:, span])], sem)
    for copy in writes:
        copy.wait()


def local(
    devices,
    points,
    order,
    bases,
    lift,
    near_ids,
    near_blocks,
    far_ids,
    far_count,
    far_blocks,
    transfer,
    couple,
    links,
    top_couple,
):
    me = lax.axis_index("leaf").astype(jnp.int32).reshape(1)
    vectors, points_dev = points.shape
    leaf_dev, leaf_size, rank = bases.shape
    slots = near_ids.shape[1]
    far_slots = far_ids.shape[1]
    bases_t = jnp.swapaxes(bases, 1, 2)
    tiles = points_dev // LANES
    edge_rows = vectors * (leaf_size // LANES)
    rows = (leaf_dev + 1) * TILE
    groups = devices // GROUP
    order_tiles = order.reshape(tiles, LANES)
    shape = jax.ShapeDtypeStruct

    group_out, tree_x = pl.pallas_call(
        up_kernel,
        out_shape=[
            shape((GROUP, rows + edge_rows, LANES), F32),
            shape((leaf_dev, vectors, leaf_size), F32),
        ],
        in_specs=[SMEM] + [HBM] * 4,
        out_specs=[HBM] * 2,
        scratch_shapes=[
            pltpu.VMEM(points.shape, F32),
            pltpu.VMEM((tiles, LANES), jnp.int32),
            pltpu.VMEM(bases_t.shape, F32),
            pltpu.VMEM(lift.shape, F32),
            pltpu.VMEM((leaf_dev, vectors, leaf_size), F32),
            pltpu.VMEM((rows, LANES), F32),
            pltpu.VMEM((2, edge_rows, LANES), F32),
            pltpu.SemaphoreType.DMA((5,)),
            pltpu.SemaphoreType.DMA((GROUP,)),
            pltpu.SemaphoreType.DMA((GROUP,)),
        ],
        compiler_params=PARAMS,
        name="up",
    )(me, points, order_tiles, bases_t, lift)

    aligned = [[g * GROUP + i for i in range(GROUP)] for g in range(groups)]
    group_in = lax.all_to_all(group_out, "leaf", 0, 0, axis_index_groups=aligned, tiled=True)

    ids_t = near_ids.T
    both = lambda *size: [shape(size, BF16)] * 2

    links_own = links.reshape(links.shape[1:])
    path_rows = (DEPTH * len(OFFSETS) + 2) // 2 * rank
    operands = (
        ids_t,
        links_own,
        transfer,
        couple,
        tree_x,
        top_couple,
        lift,
        order.reshape(1, points_dev),
        far_blocks,
        bases_t.reshape(leaf_dev // 2, 2 * rank, leaf_size),
        near_blocks,
    )
    results = (
        both(14 * rank, rank)
        + both(path_rows, 2 * rank)
        + [shape((tiles, LANES), jnp.int32)]
        + both(leaf_dev // 2, far_slots * rank, 2 * rank)
        + both(leaf_dev // 2, rank, 2 * rank)
        + both(leaf_dev // 2, 2 * rank, leaf_size)
        + both(2, leaf_size, leaf_size)
        + [shape(tree_x.shape, F32)]
    )
    (
        up_high,
        up_low,
        path_high,
        path_low,
        inverse,
        leaf_high,
        leaf_low,
        lift_high,
        lift_low,
        bases_high,
        bases_low,
        edge_high,
        edge_low,
        near_part,
    ) = pl.pallas_call(
        side_kernel,
        out_shape=results,
        in_specs=[SMEM] + [HBM] * len(operands),
        out_specs=[HBM] * len(results),
        scratch_shapes=[
            (pltpu.SMEM if x is ids_t or x is links_own else pltpu.VMEM)(x.shape, x.dtype)
            for x in operands
        ]
        + [pltpu.VMEM(x.shape, x.dtype) for x in results]
        + [
            pltpu.SemaphoreType.DMA((10,)),
            pltpu.SemaphoreType.DMA((leaf_dev // 2,)),
            pltpu.SemaphoreType.DMA((len(results),)),
        ],
        compiler_params=PARAMS,
        cost_estimate=pl.CostEstimate(
            flops=250 * 12_000_000, bytes_accessed=12_000_000, transcendentals=0
        ),
        name="side",
    )(me, *operands)

    by_permute = groups == 4
    half_out, nodes_out, far_nodes = pl.pallas_call(
        functools.partial(middle_kernel, leaf_dev),
        out_shape=[
            shape((REACH * rows + edge_rows + NODES * TILE, LANES), F32),
            shape((1 if by_permute else groups, NODES, TILE, LANES), F32),
            shape((3, TILE, LANES), F32),
        ],
        in_specs=[SMEM] + [HBM] * 3,
        out_specs=[HBM, VMEM, VMEM],
        scratch_shapes=[
            pltpu.VMEM((GROUP, TILE, LANES), F32),
            pltpu.VMEM(up_high.shape, BF16),
            pltpu.VMEM(up_low.shape, BF16),
            pltpu.VMEM((REACH * rows + edge_rows + NODES * TILE, LANES), F32),
            pltpu.SemaphoreType.DMA((3,)),
            pltpu.SemaphoreType.DMA((REACH + 1,)),
            pltpu.SemaphoreType.DMA((2,)),
        ],
        compiler_params=PARAMS,
        name="middle",
    )(me, group_in, up_high, up_low)

    def shifted(x, low, high):
        pairs = []
        for device in range(devices):
            by = low if device % GROUP < REACH else high
            pairs.append(((device + by * GROUP) % devices, device))
        return lax.ppermute(x, "leaf", pairs)

    half_in = shifted(half_out, -1, 1)
    if by_permute:
        node_parts = (nodes_out, shifted(nodes_out, 1, -1), shifted(far_nodes, 2, 2))
    else:
        across = [[g * GROUP + i for g in range(groups)] for i in range(GROUP)]
        node_parts = (lax.all_to_all(nodes_out, "leaf", 0, 0, axis_index_groups=across, tiled=True),)

    operands = (
        group_in,
        half_in,
        far_ids,
        far_count,
        path_high,
        path_low,
        leaf_high,
        leaf_low,
        lift_high,
        lift_low,
        edge_high,
        edge_low,
        bases_high,
        bases_low,
        near_part,
        inverse,
    )
    return pl.pallas_call(
        functools.partial(down_kernel, len(node_parts)),
        out_shape=shape((vectors, points_dev), F32),
        in_specs=[SMEM] + [HBM] * (len(node_parts) + len(operands)),
        out_specs=HBM,
        scratch_shapes=[
            (pltpu.SMEM if x is far_ids or x is far_count else pltpu.VMEM)(x.shape, x.dtype)
            for x in operands
        ]
        + [
            pltpu.VMEM((groups, NODES, TILE, LANES), F32),
            pltpu.VMEM((vectors, points_dev), F32),
            pltpu.VMEM((vectors, points_dev), F32),
            pltpu.SemaphoreType.DMA((len(operands),)),
            pltpu.SemaphoreType.DMA((3,)),
            pltpu.SemaphoreType.DMA((4,)),
        ],
        compiler_params=PARAMS,
        name="down",
    )(me, *node_parts, *operands)


def solution(mesh):
    in_specs = (
        P(None, "leaf"),
        P("leaf"),
        P("leaf", None, None),
        P("leaf", None, None),
        P("leaf", None),
        P("leaf", None, None, None),
        P("leaf", None),
        P("leaf"),
        P("leaf", None, None, None),
        P(),
        P(),
        P("leaf", None, None),
        P(),
    )
    return jax.shard_map(
        functools.partial(local, mesh.shape["leaf"]),
        mesh=mesh,
        in_specs=in_specs,
        out_specs=P(None, "leaf"),
        check_vma=False,
    )
```

```python
import functools

import jax
import jax.numpy as jnp
from jax import lax
from jax.experimental import pallas as pl
from jax.experimental.pallas import tpu as pltpu
from jax.sharding import PartitionSpec as P

REACH = 4
DEPTH = 4
OFFSETS = (-3, -2, 2, 3)
GROUP = 2 * REACH
LANES = 128
TILE = 8
NODES = GROUP - 1
VMEM_LIMIT = 64 * 1024 * 1024

NN = (((1,), (0,)), ((), ()))
NT = (((1,), (1,)), ((), ()))

VMEM = pl.BlockSpec(memory_space=pltpu.VMEM)
SMEM = pl.BlockSpec(memory_space=pltpu.SMEM)
HBM = pl.BlockSpec(memory_space=pltpu.HBM)
PARAMS = pltpu.CompilerParams(vmem_limit_bytes=VMEM_LIMIT)
F32 = jnp.float32
BF16 = jnp.bfloat16


def halves(x):
    high = x.astype(BF16)
    low = (x - high.astype(F32)).astype(BF16)
    return high, low


def dot_halves(a, b_high, b_low, dims):
    a_high, a_low = halves(a)
    rows = a.shape[0]
    both = lax.dot_general(
        jnp.concatenate([a_high, a_low], axis=0), b_high, dims, preferred_element_type=F32
    )
    cross = lax.dot_general(a_high, b_low, dims, preferred_element_type=F32)
    return both[:rows] + (both[rows:] + cross)


def pair_dot(a, b, w_high, w_low):
    a_high, a_low = halves(a)
    b_high, b_low = halves(b)
    rows = a.shape[0]
    both = lax.dot_general(
        jnp.concatenate([a_high, b_high, a_low, b_low], axis=0),
        w_high,
        NN,
        preferred_element_type=F32,
    )
    cross = lax.dot_general(
        jnp.concatenate([a_high, b_high], axis=0), w_low, NN, preferred_element_type=F32
    )
    total = both[: 2 * rows] + (both[2 * rows :] + cross)
    return total[:rows], total[rows:]


def dot3(a, b, dims):
    return dot_halves(a, *halves(b), dims)


def fold(x):
    return jnp.concatenate([x[:TILE], x[TILE:]], axis=1)


def beside(p, q):
    rank = p.shape[1] // 2
    left = lax.broadcasted_iota(jnp.int32, p.shape, 1) < rank
    return jnp.concatenate(
        [
            jnp.where(left, p, pltpu.roll(q, rank, 1)),
            jnp.where(left, pltpu.roll(p, rank, 1), q),
        ],
        axis=0,
    )


def row_of(tiles):
    return jnp.concatenate([beside(*tiles[k : k + 2]) for k in range(0, len(tiles), 2)], axis=1)


def lane_gather(x, high, low):
    rows, columns = x.shape
    high = jnp.broadcast_to(high, (rows, LANES))
    low = jnp.broadcast_to(low, (rows, LANES))
    result = jnp.zeros((rows, LANES), x.dtype)
    for source in range(columns // LANES):
        tile = x[:, source * LANES : (source + 1) * LANES]
        moved = jnp.take_along_axis(tile, low, axis=1, mode="promise_in_bounds")
        result = jnp.where(high == source, moved, result)
    return result


def fetch(pairs, sems):
    copies = [
        pltpu.make_async_copy(source, target, sems.at[index])
        for index, (source, target) in enumerate(pairs)
    ]
    for copy in copies:
        copy.start()
    return copies


def up_kernel(
    me_ref,
    points_hbm,
    order_hbm,
    bases_hbm,
    lift_hbm,
    out_hbm,
    x_hbm,
    points_v,
    order_v,
    bases_v,
    lift_v,
    x_v,
    tiles_v,
    edges_v,
    sems,
    edge_sems,
    tile_sems,
):
    copies = fetch(
        [(order_hbm, order_v), (points_hbm, points_v), (bases_hbm, bases_v), (lift_hbm, lift_v)],
        sems,
    )
    me = me_ref[0]
    leaf_dev, rank, leaf_size = bases_v.shape
    vectors, points_dev = points_v.shape
    copies[0].wait()
    copies[1].wait()
    points = points_v[...]
    per_leaf = leaf_size // LANES
    for t in range(points_dev // LANES):
        spot = order_v[t : t + 1, :] - me * points_dev
        column = t % per_leaf * LANES
        x_v[t // per_leaf, :, column : column + LANES] = lane_gather(
            points, lax.shift_right_logical(spot, 7), spot & (LANES - 1)
        )
    for index, leaf in enumerate((0, leaf_dev - 1)):
        for part in range(per_leaf):
            edges_v[index, part * vectors : (part + 1) * vectors, :] = x_v[
                leaf, :, part * LANES : (part + 1) * LANES
            ]
    rows = tiles_v.shape[0]
    above = lax.rem(me + 1, GROUP)
    writes = fetch([(x_v, x_hbm)], sems.at[pl.ds(4, 1)])
    writes += fetch(
        [
            (
                edges_v.at[jnp.where(above == peer, 1, 0)],
                out_hbm.at[peer, pl.ds(rows, edges_v.shape[1])],
            )
            for peer in range(GROUP)
        ],
        edge_sems,
    )
    copies[2].wait()
    coefs = [dot3(x_v[leaf], bases_v[leaf], NT) for leaf in range(leaf_dev)]
    copies[3].wait()
    weights = lift_v[...].reshape(leaf_dev * rank, rank)
    root = dot3(jnp.concatenate(coefs, axis=1), weights, NN)
    for index, matrix in enumerate(coefs + [root]):
        tiles_v[index * TILE : (index + 1) * TILE, :] = fold(matrix)
    writes += fetch(
        [(tiles_v, out_hbm.at[peer, pl.ds(0, rows)]) for peer in range(GROUP)], tile_sems
    )
    for copy in writes:
        copy.wait()


def side_kernel(me_ref, *refs):
    inputs, outputs = refs[:11], refs[11:25]
    held, results = refs[25:36], refs[36:50]
    sems, block_sems, out_sems = refs[50:]
    ids_s, links_s, transfer_v, couple_v, x_v, top_v, lift_v, order_v, far_v, bases_v, blocks_v = held
    (
        up_high,
        up_low,
        path_high,
        path_low,
        inverse_out,
        leaf_high,
        leaf_low,
        lift_high,
        lift_low,
        bases_high,
        bases_low,
        edge_high,
        edge_low,
        near_out,
    ) = results
    leaf_dev, slots, leaf_size, _ = blocks_v.shape
    rank = top_v.shape[0]
    pairs = leaf_dev // 2
    me = me_ref[0]
    first = fetch(list(zip(inputs[:8], held[:8])), sems)

    def block(pair):
        two = pl.ds(2 * pair, 2)
        return fetch([(inputs[10].at[two], blocks_v.at[two])], block_sems.at[pl.ds(pair, 1)])

    blocks = block(0)
    second = fetch(list(zip(inputs[8:10], held[8:10])), sems.at[pl.ds(8, 2)])
    for pair in range(1, pairs):
        blocks += block(pair)
    writes = []

    def write(*indices):
        for index in indices:
            writes.extend(fetch([(results[index], outputs[index])], out_sems.at[pl.ds(index, 1)]))

    def couplings(level):
        weights = [
            links_s[level, column].astype(F32) * couple_v[level, column]
            for column in range(len(OFFSETS))
        ]
        return jnp.concatenate(weights, axis=1)

    def chain():
        bits = [lax.shift_right_logical(me, level) & 1 for level in range(DEPTH)]
        up = transfer_v[0].reshape(2 * rank, rank)
        path = transfer_v[0, bits[0]]
        parts = [couplings(0)]
        row = 0
        for level in range(1, DEPTH):
            rows = up.shape[0]
            up_high[row : row + rows], up_low[row : row + rows] = halves(up)
            row += rows
            if level < DEPTH - 1:
                up = jnp.concatenate(
                    [dot3(up, transfer_v[level, side], NN) for side in range(2)], axis=0
                )
            parts.append(dot3(path, couplings(level), NN))
            path = dot3(path, transfer_v[level, bits[level]], NN)
            if level < DEPTH - 1:
                yield
        write(0, 1)
        top = dot3(path, top_v[...], NN)
        yield
        parts = [x[:, k * rank : (k + 1) * rank] for x in parts for k in range(len(OFFSETS))]
        parts += [dot3(top, transfer_v[DEPTH - 1, side], NT) for side in range(2)]
        half = len(parts) // 2
        for index in range(half):
            span = slice(index * rank, (index + 1) * rank)
            both = jnp.concatenate([parts[index], parts[half + index]], axis=0).T
            path_high[span], path_low[span] = halves(both)
        write(2, 3)

    def inverse():
        points_dev = order_v.shape[1]
        tiles = points_dev // LANES
        spot = order_v[...] - me * points_dev
        times = lax.broadcasted_iota(jnp.int32, (1, points_dev), 1)
        shape = (tiles, points_dev)
        match = lax.broadcasted_iota(jnp.int32, shape, 0) == lax.shift_right_logical(spot, 7)
        digits = [
            jnp.where(match, jnp.broadcast_to(digit.astype(F32), shape), 0.0)
            for digit in (lax.shift_right_logical(times, 4), times & 15)
        ]
        shape = (LANES, points_dev)
        match = lax.broadcasted_iota(jnp.int32, shape, 0) == (spot & (LANES - 1))
        both = lax.dot_general(
            jnp.concatenate(digits, axis=0).astype(BF16),
            jnp.where(match, 1.0, 0.0).astype(BF16),
            NT,
            preferred_element_type=F32,
        )
        inverse_out[...] = (both[:tiles] * 16.0 + both[tiles:]).astype(jnp.int32)
        write(4)

    def transposes(pair):
        two = range(2 * pair, 2 * pair + 2)
        for slot in range(far_v.shape[1]):
            span = slice(slot * rank, (slot + 1) * rank)
            both = jnp.concatenate([far_v[leaf, slot] for leaf in two], axis=0).T
            leaf_high[pair, span], leaf_low[pair, span] = halves(both)
        both = jnp.concatenate([lift_v[leaf] for leaf in two], axis=0).T
        lift_high[pair], lift_low[pair] = halves(both)
        bases_high[pair], bases_low[pair] = halves(bases_v[pair])

    def near(leaf):
        total = jnp.zeros(near_out.shape[1:], F32)
        for slot in range(slots):
            local = ids_s[slot, leaf] - me * leaf_dev
            here = (local >= 0) & (local < leaf_dev)
            x_leaf = jnp.where(here, x_v[jnp.clip(local, 0, leaf_dev - 1)], 0.0)
            total = total + dot3(x_leaf, blocks_v[leaf, slot], NT)
        near_out[leaf] = total

    def edge(index, leaf, outside):
        total = jnp.zeros((leaf_size, leaf_size), F32)
        for slot in range(1, slots):
            remote = ids_s[slot, leaf] - me * leaf_dev == outside
            total = total + jnp.where(remote, blocks_v[leaf, slot], 0.0)
        edge_high[index], edge_low[index] = halves(total.T)

    for copy in first:
        copy.wait()
    links = chain()
    next(links)
    for pair in range(pairs):
        blocks[pair].wait()
        if pair == 0:
            for copy in second:
                copy.wait()
        near(2 * pair)
        near(2 * pair + 1)
        transposes(pair)
        next(links, None)
        if pair == 0:
            edge(0, 0, -1)
        if pair == 1:
            inverse()
        if pair == pairs - 1:
            edge(1, leaf_dev - 1, leaf_dev)
    for _ in links:
        pass
    write(*range(5, 14))
    for copy in writes:
        copy.wait()


def middle_kernel(
    leaf_dev,
    me_ref,
    group_hbm,
    up_high_hbm,
    up_low_hbm,
    half_out,
    nodes_out,
    far_out,
    roots_v,
    up_high,
    up_low,
    sems,
    half_sems,
):
    low = lax.rem(me_ref[0], GROUP) < REACH
    copies = fetch(
        [
            (group_hbm.at[:, pl.ds(leaf_dev * TILE, TILE), :], roots_v),
            (up_high_hbm, up_high),
            (up_low_hbm, up_low),
        ],
        sems,
    )
    rows = (leaf_dev + 1) * TILE
    edge_rows = group_hbm.shape[1] - rows
    first = jnp.where(low, REACH, 0)
    moves = [
        (group_hbm.at[first + part, pl.ds(0, rows)], half_out.at[pl.ds(part * rows, rows)])
        for part in range(REACH)
    ]
    moves.append(
        (
            group_hbm.at[jnp.where(low, GROUP - 1, 0), pl.ds(rows, edge_rows)],
            half_out.at[pl.ds(REACH * rows, edge_rows)],
        )
    )
    moves = fetch(moves, half_sems)
    for copy in copies:
        copy.wait()
    roots = [roots_v[peer] for peer in range(GROUP)]
    start, tiles = 0, []
    for level in range(1, DEPTH):
        width = 1 << level
        count = GROUP // width
        left = jnp.concatenate(
            [row_of(roots[n * width : (n + 1) * width]) for n in range(count)], axis=0
        )
        size = left.shape[1]
        nodes = dot_halves(left, up_high[start : start + size], up_low[start : start + size], NN)
        start += size
        tiles += [fold(nodes[n * 2 * TILE : (n + 1) * 2 * TILE]) for n in range(count)]
    row = REACH * rows + edge_rows
    for index, tile in enumerate(tiles):
        half_out[row + index * TILE : row + (index + 1) * TILE, :] = tile
        for peer in range(nodes_out.shape[0]):
            nodes_out[peer, index] = tile
    for index in range(3):
        far_out[index] = tiles[NODES - 3 + index]
    for copy in moves:
        copy.wait()


def down_kernel(parts, me_ref, *refs):
    node_parts, refs = refs[:parts], refs[parts:]
    count = (len(refs) - 7) // 2
    out_ref = refs[count]
    held = refs[count + 1 : 2 * count + 1]
    nodes_ref, y_tree, out_v, sems, node_sems, out_sems = refs[2 * count + 1 :]
    me = me_ref[0]
    groups = nodes_ref.shape[0]
    group = lax.shift_right_logical(me, 3)
    place = me & (GROUP - 1)
    low = place < REACH
    if parts > 1:
        near_by, far_by = jnp.where(low, groups - 1, 1), jnp.where(low, 1, groups - 1)
        across = lax.rem(group + 2, groups)
        near_group = lax.rem(group + near_by, groups)
        node_copies = fetch(
            [
                (node_parts[0].at[0], nodes_ref.at[group]),
                (node_parts[1].at[0], nodes_ref.at[lax.rem(group + far_by, groups)]),
                (node_parts[2], nodes_ref.at[across, pl.ds(NODES - 3, 3)]),
            ],
            node_sems,
        )
    else:
        node_copies = fetch([(node_parts[0], nodes_ref)], node_sems)
    copies = fetch(list(zip(refs[:count], held)), sems)
    (
        group_ref,
        half_ref,
        far_ids_s,
        far_count_s,
        path_high,
        path_low,
        leaf_high,
        leaf_low,
        lift_high,
        lift_low,
        edge_high,
        edge_low,
        bases_high,
        bases_low,
        near_ref,
        inverse_ref,
    ) = held
    leaf_dev, vectors, leaf_size = near_ref.shape
    points_dev = out_ref.shape[1]
    slots = far_ids_s.shape[1]
    per_leaf = leaf_size // LANES
    rank = bases_high.shape[1] // 2
    start = (leaf_dev + 1) * TILE
    edge_rows = group_ref.shape[1] - start

    def tile_of(subtree, index):
        other = subtree & (GROUP - 1)
        inside = lax.shift_right_arithmetic(subtree, 3) == group
        row = pl.multiple_of(index * TILE, TILE)
        near_row = jnp.clip(other - jnp.where(low, REACH, 0), 0, REACH - 1) * start
        here = group_ref[other, pl.ds(row, TILE), :]
        there = half_ref[pl.ds(pl.multiple_of(near_row + row, TILE), TILE), :]
        return jnp.where(inside, here, there)

    for copy in node_copies + copies[:6]:
        copy.wait()
    if parts > 1:
        for index in range(NODES):
            row = half_ref.shape[0] - (NODES - index) * TILE
            tile = half_ref[row : row + TILE, :]
            nodes_ref[near_group, index] = tile
    partners = []
    for level in range(DEPTH):
        node = lax.shift_right_logical(me, level)
        size = (groups * GROUP) >> level
        for offset in OFFSETS:
            other = node + offset
            used = (other >= 0) & (other < size)
            other = jnp.clip(other, 0, size - 1)
            if level == 0:
                tile = tile_of(other, leaf_dev)
            else:
                shift = DEPTH - 1 - level
                first = GROUP - (2 << shift)
                tile = nodes_ref[
                    lax.shift_right_logical(other, shift), first + (other & ((1 << shift) - 1))
                ]
            partners.append(jnp.where(used, tile, 0.0))
    top = lax.shift_right_logical(me, DEPTH)
    for side in range(2):
        blended = jnp.zeros((TILE, LANES), F32)
        for other in range(groups // 2):
            distance = jnp.abs(top - other)
            weight = jnp.where(distance >= 2, 1.0 / jnp.maximum(distance, 1).astype(F32), 0.0)
            blended = blended + weight * nodes_ref[2 * other + side, GROUP - 2]
        partners.append(blended)
    half = len(partners) // 2
    row = row_of(partners)
    first, second = pair_dot(
        row[:, : half * rank], row[:, half * rank :], path_high[...], path_low[...]
    )
    down = first[:, :rank] + second[:, rank:]

    rows = []
    for leaf in range(leaf_dev):
        picked = []
        for slot in range(slots):
            used = slot < far_count_s[leaf]
            spot = far_ids_s[leaf, slot]
            tile = tile_of(lax.shift_right_logical(spot, 3), spot & (leaf_dev - 1))
            picked.append(jnp.where(used, tile, 0.0))
        rows.append(row_of(picked))
    edges = []
    for offset in (-1, 1):
        other = me + offset
        inside = lax.shift_right_arithmetic(other, 3) == group
        here = group_ref[other & (GROUP - 1), start:, :]
        chosen = jnp.where(inside, here, half_ref[REACH * start : REACH * start + edge_rows, :])
        edges.append(
            jnp.concatenate(
                [chosen[part * vectors : (part + 1) * vectors] for part in range(per_leaf)], axis=1
            )
        )

    for copy in copies[6:]:
        copy.wait()
    edge_parts = [
        dot_halves(edges[index], edge_high[index], edge_low[index], NN) for index in range(2)
    ]
    left_half = lax.broadcasted_iota(jnp.int32, (vectors, 2 * rank), 1) < rank
    for pair in range(leaf_dev // 2):
        two = (2 * pair, 2 * pair + 1)
        first, second = pair_dot(rows[two[0]], rows[two[1]], leaf_high[pair], leaf_low[pair])
        lift = dot_halves(down, lift_high[pair], lift_low[pair], NN)
        first = jnp.where(left_half, first + lift, 0.0)
        second = jnp.where(left_half, 0.0, second + lift)
        products = pair_dot(first, second, bases_high[pair], bases_low[pair])
        for leaf, product in zip(two, products):
            y_leaf = near_ref[leaf] + product
            if leaf == 0:
                y_leaf = y_leaf + edge_parts[0]
            if leaf == leaf_dev - 1:
                y_leaf = y_leaf + edge_parts[1]
            y_tree[:, leaf * leaf_size : (leaf + 1) * leaf_size] = y_leaf

    y = y_tree[...]
    writes = []
    tiles = points_dev // LANES
    for tile in range(tiles):
        spot = inverse_ref[tile : tile + 1, :]
        out_v[:, tile * LANES : (tile + 1) * LANES] = lane_gather(
            y, lax.shift_right_logical(spot, 7), spot & (LANES - 1)
        )
        if (tile + 1) % (tiles // 4) == 0:
            span = pl.ds((tile + 1 - tiles // 4) * LANES, tiles // 4 * LANES)
            sem = out_sems.at[pl.ds(len(writes), 1)]
            writes += fetch([(out_v.at[:, span], out_ref.at[:, span])], sem)
    for copy in writes:
        copy.wait()


def local(
    devices,
    points,
    order,
    bases,
    lift,
    near_ids,
    near_blocks,
    far_ids,
    far_count,
    far_blocks,
    transfer,
    couple,
    links,
    top_couple,
):
    me = lax.axis_index("leaf").astype(jnp.int32).reshape(1)
    vectors, points_dev = points.shape
    leaf_dev, leaf_size, rank = bases.shape
    slots = near_ids.shape[1]
    far_slots = far_ids.shape[1]
    bases_t = jnp.swapaxes(bases, 1, 2)
    tiles = points_dev // LANES
    edge_rows = vectors * (leaf_size // LANES)
    rows = (leaf_dev + 1) * TILE
    groups = devices // GROUP
    order_tiles = order.reshape(tiles, LANES)
    shape = jax.ShapeDtypeStruct

    group_out, tree_x = pl.pallas_call(
        up_kernel,
        out_shape=[
            shape((GROUP, rows + edge_rows, LANES), F32),
            shape((leaf_dev, vectors, leaf_size), F32),
        ],
        in_specs=[SMEM] + [HBM] * 4,
        out_specs=[HBM] * 2,
        scratch_shapes=[
            pltpu.VMEM(points.shape, F32),
            pltpu.VMEM((tiles, LANES), jnp.int32),
            pltpu.VMEM(bases_t.shape, F32),
            pltpu.VMEM(lift.shape, F32),
            pltpu.VMEM((leaf_dev, vectors, leaf_size), F32),
            pltpu.VMEM((rows, LANES), F32),
            pltpu.VMEM((2, edge_rows, LANES), F32),
            pltpu.SemaphoreType.DMA((5,)),
            pltpu.SemaphoreType.DMA((GROUP,)),
            pltpu.SemaphoreType.DMA((GROUP,)),
        ],
        compiler_params=PARAMS,
        name="up",
    )(me, points, order_tiles, bases_t, lift)

    aligned = [[g * GROUP + i for i in range(GROUP)] for g in range(groups)]
    group_in = lax.all_to_all(group_out, "leaf", 0, 0, axis_index_groups=aligned, tiled=True)

    ids_t = near_ids.T
    both = lambda *size: [shape(size, BF16)] * 2

    links_own = links.reshape(links.shape[1:])
    path_rows = (DEPTH * len(OFFSETS) + 2) // 2 * rank
    operands = (
        ids_t,
        links_own,
        transfer,
        couple,
        tree_x,
        top_couple,
        lift,
        order.reshape(1, points_dev),
        far_blocks,
        bases_t.reshape(leaf_dev // 2, 2 * rank, leaf_size),
        near_blocks,
    )
    results = (
        both(14 * rank, rank)
        + both(path_rows, 2 * rank)
        + [shape((tiles, LANES), jnp.int32)]
        + both(leaf_dev // 2, far_slots * rank, 2 * rank)
        + both(leaf_dev // 2, rank, 2 * rank)
        + both(leaf_dev // 2, 2 * rank, leaf_size)
        + both(2, leaf_size, leaf_size)
        + [shape(tree_x.shape, F32)]
    )
    (
        up_high,
        up_low,
        path_high,
        path_low,
        inverse,
        leaf_high,
        leaf_low,
        lift_high,
        lift_low,
        bases_high,
        bases_low,
        edge_high,
        edge_low,
        near_part,
    ) = pl.pallas_call(
        side_kernel,
        out_shape=results,
        in_specs=[SMEM] + [HBM] * len(operands),
        out_specs=[HBM] * len(results),
        scratch_shapes=[
            (pltpu.SMEM if x is ids_t or x is links_own else pltpu.VMEM)(x.shape, x.dtype)
            for x in operands
        ]
        + [pltpu.VMEM(x.shape, x.dtype) for x in results]
        + [
            pltpu.SemaphoreType.DMA((10,)),
            pltpu.SemaphoreType.DMA((leaf_dev // 2,)),
            pltpu.SemaphoreType.DMA((len(results),)),
        ],
        compiler_params=PARAMS,
        cost_estimate=pl.CostEstimate(
            flops=250 * 12_000_000, bytes_accessed=12_000_000, transcendentals=0
        ),
        name="side",
    )(me, *operands)

    by_permute = groups == 4
    half_out, nodes_out, far_nodes = pl.pallas_call(
        functools.partial(middle_kernel, leaf_dev),
        out_shape=[
            shape((REACH * rows + edge_rows + NODES * TILE, LANES), F32),
            shape((1 if by_permute else groups, NODES, TILE, LANES), F32),
            shape((3, TILE, LANES), F32),
        ],
        in_specs=[SMEM] + [HBM] * 3,
        out_specs=[VMEM] * 3,
        scratch_shapes=[
            pltpu.VMEM((GROUP, TILE, LANES), F32),
            pltpu.VMEM(up_high.shape, BF16),
            pltpu.VMEM(up_low.shape, BF16),
            pltpu.SemaphoreType.DMA((3,)),
            pltpu.SemaphoreType.DMA((REACH + 1,)),
        ],
        compiler_params=PARAMS,
        name="middle",
    )(me, group_in, up_high, up_low)

    def shifted(x, low, high):
        pairs = []
        for device in range(devices):
            by = low if device % GROUP < REACH else high
            pairs.append(((device + by * GROUP) % devices, device))
        return lax.ppermute(x, "leaf", pairs)

    half_in = shifted(half_out, -1, 1)
    if by_permute:
        node_parts = (nodes_out, shifted(nodes_out, 1, -1), shifted(far_nodes, 2, 2))
    else:
        across = [[g * GROUP + i for g in range(groups)] for i in range(GROUP)]
        node_parts = (lax.all_to_all(nodes_out, "leaf", 0, 0, axis_index_groups=across, tiled=True),)

    operands = (
        group_in,
        half_in,
        far_ids,
        far_count,
        path_high,
        path_low,
        leaf_high,
        leaf_low,
        lift_high,
        lift_low,
        edge_high,
        edge_low,
        bases_high,
        bases_low,
        near_part,
        inverse,
    )
    return pl.pallas_call(
        functools.partial(down_kernel, len(node_parts)),
        out_shape=shape((vectors, points_dev), F32),
        in_specs=[SMEM] + [HBM] * (len(node_parts) + len(operands)),
        out_specs=HBM,
        scratch_shapes=[
            (pltpu.SMEM if x is far_ids or x is far_count else pltpu.VMEM)(x.shape, x.dtype)
            for x in operands
        ]
        + [
            pltpu.VMEM((groups, NODES, TILE, LANES), F32),
            pltpu.VMEM((vectors, points_dev), F32),
            pltpu.VMEM((vectors, points_dev), F32),
            pltpu.SemaphoreType.DMA((len(operands),)),
            pltpu.SemaphoreType.DMA((3,)),
            pltpu.SemaphoreType.DMA((4,)),
        ],
        compiler_params=PARAMS,
        name="down",
    )(me, *node_parts, *operands)


def solution(mesh):
    in_specs = (
        P(None, "leaf"),
        P("leaf"),
        P("leaf", None, None),
        P("leaf", None, None),
        P("leaf", None),
        P("leaf", None, None, None),
        P("leaf", None),
        P("leaf"),
        P("leaf", None, None, None),
        P(),
        P(),
        P("leaf", None, None),
        P(),
    )
    return jax.shard_map(
        functools.partial(local, mesh.shape["leaf"]),
        mesh=mesh,
        in_specs=in_specs,
        out_specs=P(None, "leaf"),
        check_vma=False,
    )
```

```python
import functools

import jax
import jax.numpy as jnp
from jax import lax
from jax.experimental import pallas as pl
from jax.experimental.pallas import tpu as pltpu
from jax.sharding import PartitionSpec as P

REACH = 4
DEPTH = 4
OFFSETS = (-3, -2, 2, 3)
GROUP = 2 * REACH
LANES = 128
TILE = 8
NODES = GROUP - 1
VMEM_LIMIT = 64 * 1024 * 1024

NN = (((1,), (0,)), ((), ()))
NT = (((1,), (1,)), ((), ()))

VMEM = pl.BlockSpec(memory_space=pltpu.VMEM)
SMEM = pl.BlockSpec(memory_space=pltpu.SMEM)
HBM = pl.BlockSpec(memory_space=pltpu.HBM)
PARAMS = pltpu.CompilerParams(vmem_limit_bytes=VMEM_LIMIT)
F32 = jnp.float32
BF16 = jnp.bfloat16


def halves(x):
    high = x.astype(BF16)
    low = (x - high.astype(F32)).astype(BF16)
    return high, low


def dot_halves(a, b_high, b_low, dims):
    a_high, a_low = halves(a)
    rows = a.shape[0]
    both = lax.dot_general(
        jnp.concatenate([a_high, a_low], axis=0), b_high, dims, preferred_element_type=F32
    )
    cross = lax.dot_general(a_high, b_low, dims, preferred_element_type=F32)
    return both[:rows] + (both[rows:] + cross)


def pair_dot(a, b, w_high, w_low):
    a_high, a_low = halves(a)
    b_high, b_low = halves(b)
    rows = a.shape[0]
    both = lax.dot_general(
        jnp.concatenate([a_high, b_high, a_low, b_low], axis=0),
        w_high,
        NN,
        preferred_element_type=F32,
    )
    cross = lax.dot_general(
        jnp.concatenate([a_high, b_high], axis=0), w_low, NN, preferred_element_type=F32
    )
    total = both[: 2 * rows] + (both[2 * rows :] + cross)
    return total[:rows], total[rows:]


def dot3(a, b, dims):
    return dot_halves(a, *halves(b), dims)


def fold(x):
    return jnp.concatenate([x[:TILE], x[TILE:]], axis=1)


def beside(p, q):
    rank = p.shape[1] // 2
    left = lax.broadcasted_iota(jnp.int32, p.shape, 1) < rank
    return jnp.concatenate(
        [
            jnp.where(left, p, pltpu.roll(q, rank, 1)),
            jnp.where(left, pltpu.roll(p, rank, 1), q),
        ],
        axis=0,
    )


def row_of(tiles):
    return jnp.concatenate([beside(*tiles[k : k + 2]) for k in range(0, len(tiles), 2)], axis=1)


def lane_gather(x, high, low):
    rows, columns = x.shape
    high = jnp.broadcast_to(high, (rows, LANES))
    low = jnp.broadcast_to(low, (rows, LANES))
    result = jnp.zeros((rows, LANES), x.dtype)
    for source in range(columns // LANES):
        tile = x[:, source * LANES : (source + 1) * LANES]
        moved = jnp.take_along_axis(tile, low, axis=1, mode="promise_in_bounds")
        result = jnp.where(high == source, moved, result)
    return result


def fetch(pairs, sems):
    copies = [
        pltpu.make_async_copy(source, target, sems.at[index])
        for index, (source, target) in enumerate(pairs)
    ]
    for copy in copies:
        copy.start()
    return copies


def up_kernel(
    me_ref, points_hbm, order_hbm, bases_hbm, lift_hbm, out, x_out, points_v, order_v, bases_v, lift_v, sems
):
    copies = fetch(
        [(order_hbm, order_v), (points_hbm, points_v), (bases_hbm, bases_v), (lift_hbm, lift_v)], sems
    )
    me = me_ref[0]
    leaf_dev, rank, leaf_size = bases_v.shape
    vectors, points_dev = points_v.shape
    copies[0].wait()
    copies[1].wait()
    points = points_v[...]
    per_leaf = leaf_size // LANES
    for t in range(points_dev // LANES):
        spot = order_v[t : t + 1, :] - me * points_dev
        column = t % per_leaf * LANES
        x_out[t // per_leaf, :, column : column + LANES] = lane_gather(
            points, lax.shift_right_logical(spot, 7), spot & (LANES - 1)
        )
    copies[2].wait()
    coefs = [dot3(x_out[leaf], bases_v[leaf], NT) for leaf in range(leaf_dev)]
    tiles = [fold(coef) for coef in coefs]
    copies[3].wait()
    weights = lift_v[...].reshape(leaf_dev * rank, rank)
    tiles.append(fold(dot3(jnp.concatenate(coefs, axis=1), weights, NN)))
    for peer in range(GROUP):
        for index, tile in enumerate(tiles):
            out[peer, index * TILE : (index + 1) * TILE, :] = tile
    place = lax.rem(me, GROUP)
    start = len(tiles) * TILE
    for part in range(per_leaf):
        first = x_out[0, :, part * LANES : (part + 1) * LANES]
        last = x_out[leaf_dev - 1, :, part * LANES : (part + 1) * LANES]
        rows = slice(start + part * vectors, start + (part + 1) * vectors)
        for peer in range(GROUP):
            above = lax.rem(place + 1, GROUP) == peer
            out[peer, rows, :] = jnp.where(above, last, first)


def side_kernel(me_ref, *refs):
    inputs, outputs = refs[:11], refs[11:25]
    held, results = refs[25:36], refs[36:50]
    sems, block_sems, out_sems = refs[50:]
    ids_s, links_s, transfer_v, couple_v, x_v, top_v, lift_v, order_v, far_v, bases_v, blocks_v = held
    (
        up_high,
        up_low,
        path_high,
        path_low,
        inverse_out,
        leaf_high,
        leaf_low,
        lift_high,
        lift_low,
        bases_high,
        bases_low,
        edge_high,
        edge_low,
        near_out,
    ) = results
    leaf_dev, slots, leaf_size, _ = blocks_v.shape
    rank = top_v.shape[0]
    pairs = leaf_dev // 2
    me = me_ref[0]
    first = fetch(list(zip(inputs[:8], held[:8])), sems)

    def block(pair):
        two = pl.ds(2 * pair, 2)
        return fetch([(inputs[10].at[two], blocks_v.at[two])], block_sems.at[pl.ds(pair, 1)])

    blocks = block(0)
    second = fetch(list(zip(inputs[8:10], held[8:10])), sems.at[pl.ds(8, 2)])
    for pair in range(1, pairs):
        blocks += block(pair)
    writes = []

    def write(*indices):
        for index in indices:
            writes.extend(fetch([(results[index], outputs[index])], out_sems.at[pl.ds(index, 1)]))

    def couplings(level):
        weights = [
            links_s[level, column].astype(F32) * couple_v[level, column]
            for column in range(len(OFFSETS))
        ]
        return jnp.concatenate(weights, axis=1)

    def chain():
        bits = [lax.shift_right_logical(me, level) & 1 for level in range(DEPTH)]
        up = transfer_v[0].reshape(2 * rank, rank)
        path = transfer_v[0, bits[0]]
        parts = [couplings(0)]
        row = 0
        for level in range(1, DEPTH):
            rows = up.shape[0]
            up_high[row : row + rows], up_low[row : row + rows] = halves(up)
            row += rows
            if level < DEPTH - 1:
                up = jnp.concatenate(
                    [dot3(up, transfer_v[level, side], NN) for side in range(2)], axis=0
                )
            parts.append(dot3(path, couplings(level), NN))
            path = dot3(path, transfer_v[level, bits[level]], NN)
            if level < DEPTH - 1:
                yield
        write(0, 1)
        top = dot3(path, top_v[...], NN)
        yield
        parts = [x[:, k * rank : (k + 1) * rank] for x in parts for k in range(len(OFFSETS))]
        parts += [dot3(top, transfer_v[DEPTH - 1, side], NT) for side in range(2)]
        half = len(parts) // 2
        for index in range(half):
            span = slice(index * rank, (index + 1) * rank)
            both = jnp.concatenate([parts[index], parts[half + index]], axis=0).T
            path_high[span], path_low[span] = halves(both)
        write(2, 3)

    def inverse():
        points_dev = order_v.shape[1]
        tiles = points_dev // LANES
        spot = order_v[...] - me * points_dev
        times = lax.broadcasted_iota(jnp.int32, (1, points_dev), 1)
        shape = (tiles, points_dev)
        match = lax.broadcasted_iota(jnp.int32, shape, 0) == lax.shift_right_logical(spot, 7)
        digits = [
            jnp.where(match, jnp.broadcast_to(digit.astype(F32), shape), 0.0)
            for digit in (lax.shift_right_logical(times, 4), times & 15)
        ]
        shape = (LANES, points_dev)
        match = lax.broadcasted_iota(jnp.int32, shape, 0) == (spot & (LANES - 1))
        both = lax.dot_general(
            jnp.concatenate(digits, axis=0).astype(BF16),
            jnp.where(match, 1.0, 0.0).astype(BF16),
            NT,
            preferred_element_type=F32,
        )
        inverse_out[...] = (both[:tiles] * 16.0 + both[tiles:]).astype(jnp.int32)
        write(4)

    def transposes(pair):
        two = range(2 * pair, 2 * pair + 2)
        for slot in range(far_v.shape[1]):
            span = slice(slot * rank, (slot + 1) * rank)
            both = jnp.concatenate([far_v[leaf, slot] for leaf in two], axis=0).T
            leaf_high[pair, span], leaf_low[pair, span] = halves(both)
        both = jnp.concatenate([lift_v[leaf] for leaf in two], axis=0).T
        lift_high[pair], lift_low[pair] = halves(both)
        bases_high[pair], bases_low[pair] = halves(bases_v[pair])

    def near(leaf):
        total = jnp.zeros(near_out.shape[1:], F32)
        for slot in range(slots):
            local = ids_s[slot, leaf] - me * leaf_dev
            here = (local >= 0) & (local < leaf_dev)
            x_leaf = jnp.where(here, x_v[jnp.clip(local, 0, leaf_dev - 1)], 0.0)
            total = total + dot3(x_leaf, blocks_v[leaf, slot], NT)
        near_out[leaf] = total

    def edge(index, leaf, outside):
        total = jnp.zeros((leaf_size, leaf_size), F32)
        for slot in range(1, slots):
            remote = ids_s[slot, leaf] - me * leaf_dev == outside
            total = total + jnp.where(remote, blocks_v[leaf, slot], 0.0)
        edge_high[index], edge_low[index] = halves(total.T)

    for copy in first:
        copy.wait()
    links = chain()
    next(links)
    for pair in range(pairs):
        blocks[pair].wait()
        if pair == 0:
            for copy in second:
                copy.wait()
        near(2 * pair)
        near(2 * pair + 1)
        transposes(pair)
        next(links, None)
        if pair == 0:
            edge(0, 0, -1)
        if pair == 1:
            inverse()
        if pair == pairs - 1:
            edge(1, leaf_dev - 1, leaf_dev)
    for _ in links:
        pass
    write(*range(5, 14))
    for copy in writes:
        copy.wait()


def middle_kernel(
    leaf_dev,
    me_ref,
    group_hbm,
    up_high_hbm,
    up_low_hbm,
    half_out,
    nodes_out,
    far_out,
    side_out,
    roots_v,
    up_high,
    up_low,
    sems,
    half_sems,
):
    low = lax.rem(me_ref[0], GROUP) < REACH
    copies = fetch(
        [
            (group_hbm.at[:, pl.ds(leaf_dev * TILE, TILE), :], roots_v),
            (up_high_hbm, up_high),
            (up_low_hbm, up_low),
        ],
        sems,
    )
    rows = (leaf_dev + 1) * TILE
    edge_rows = group_hbm.shape[1] - rows
    first = jnp.where(low, REACH, 0)
    moves = [
        (group_hbm.at[first + part, pl.ds(0, rows)], half_out.at[pl.ds(part * rows, rows)])
        for part in range(REACH)
    ]
    moves.append(
        (
            group_hbm.at[jnp.where(low, GROUP - 1, 0), pl.ds(rows, edge_rows)],
            half_out.at[pl.ds(REACH * rows, edge_rows)],
        )
    )
    moves = fetch(moves, half_sems)
    for copy in copies:
        copy.wait()
    roots = [roots_v[peer] for peer in range(GROUP)]
    start, tiles = 0, []
    for level in range(1, DEPTH):
        width = 1 << level
        count = GROUP // width
        left = jnp.concatenate(
            [row_of(roots[n * width : (n + 1) * width]) for n in range(count)], axis=0
        )
        size = left.shape[1]
        nodes = dot_halves(left, up_high[start : start + size], up_low[start : start + size], NN)
        start += size
        tiles += [fold(nodes[n * 2 * TILE : (n + 1) * 2 * TILE]) for n in range(count)]
    row = REACH * rows + edge_rows
    for index, tile in enumerate(tiles):
        half_out[row + index * TILE : row + (index + 1) * TILE, :] = tile
        for peer in range(nodes_out.shape[0]):
            nodes_out[peer, index] = tile
    for index in range(3):
        far_out[index] = tiles[NODES - 3 + index]
        side_out[1 + index] = tiles[NODES - 3 + index]
    side_out[0] = jnp.where(low, tiles[0], tiles[3])
    for copy in moves:
        copy.wait()


def down_kernel(parts, me_ref, *refs):
    node_parts, refs = refs[:parts], refs[parts:]
    count = (len(refs) - 5) // 2
    out_ref = refs[count]
    held = refs[count + 1 : 2 * count + 1]
    nodes_ref, y_tree, sems, node_sems = refs[2 * count + 1 :]
    me = me_ref[0]
    groups = nodes_ref.shape[0]
    group = lax.shift_right_logical(me, 3)
    place = me & (GROUP - 1)
    low = place < REACH
    if parts > 1:
        near_by, far_by = jnp.where(low, groups - 1, 1), jnp.where(low, 1, groups - 1)
        across = lax.rem(group + 2, groups)
        near_group = lax.rem(group + near_by, groups)
        far_group = lax.rem(group + far_by, groups)
        node_copies = fetch(
            [
                (node_parts[0].at[0], nodes_ref.at[group]),
                (node_parts[1].at[0], nodes_ref.at[far_group, jnp.where(low, 0, 3)]),
                (node_parts[1].at[pl.ds(1, 3)], nodes_ref.at[far_group, pl.ds(NODES - 3, 3)]),
                (node_parts[2], nodes_ref.at[across, pl.ds(NODES - 3, 3)]),
            ],
            node_sems,
        )
    else:
        node_copies = fetch([(node_parts[0], nodes_ref)], node_sems)
    copies = fetch(list(zip(refs[:count], held)), sems)
    (
        group_ref,
        half_ref,
        far_ids_s,
        far_count_s,
        path_high,
        path_low,
        leaf_high,
        leaf_low,
        lift_high,
        lift_low,
        edge_high,
        edge_low,
        bases_high,
        bases_low,
        near_ref,
        inverse_ref,
    ) = held
    leaf_dev, vectors, leaf_size = near_ref.shape
    points_dev = out_ref.shape[1]
    slots = far_ids_s.shape[1]
    per_leaf = leaf_size // LANES
    rank = bases_high.shape[1] // 2
    start = (leaf_dev + 1) * TILE
    edge_rows = group_ref.shape[1] - start

    def tile_of(subtree, index):
        other = subtree & (GROUP - 1)
        inside = lax.shift_right_arithmetic(subtree, 3) == group
        row = pl.multiple_of(index * TILE, TILE)
        near_row = jnp.clip(other - jnp.where(low, REACH, 0), 0, REACH - 1) * start
        here = group_ref[other, pl.ds(row, TILE), :]
        there = half_ref[pl.ds(pl.multiple_of(near_row + row, TILE), TILE), :]
        return jnp.where(inside, here, there)

    for copy in node_copies + copies[:6]:
        copy.wait()
    if parts > 1:
        for index in range(NODES):
            row = half_ref.shape[0] - (NODES - index) * TILE
            tile = half_ref[row : row + TILE, :]
            nodes_ref[near_group, index] = tile
    partners = []
    for level in range(DEPTH):
        node = lax.shift_right_logical(me, level)
        size = (groups * GROUP) >> level
        for offset in OFFSETS:
            other = node + offset
            used = (other >= 0) & (other < size)
            other = jnp.clip(other, 0, size - 1)
            if level == 0:
                tile = tile_of(other, leaf_dev)
            else:
                shift = DEPTH - 1 - level
                first = GROUP - (2 << shift)
                tile = nodes_ref[
                    lax.shift_right_logical(other, shift), first + (other & ((1 << shift) - 1))
                ]
            partners.append(jnp.where(used, tile, 0.0))
    top = lax.shift_right_logical(me, DEPTH)
    for side in range(2):
        blended = jnp.zeros((TILE, LANES), F32)
        for other in range(groups // 2):
            distance = jnp.abs(top - other)
            weight = jnp.where(distance >= 2, 1.0 / jnp.maximum(distance, 1).astype(F32), 0.0)
            blended = blended + weight * nodes_ref[2 * other + side, GROUP - 2]
        partners.append(blended)
    half = len(partners) // 2
    row = row_of(partners)
    first, second = pair_dot(
        row[:, : half * rank], row[:, half * rank :], path_high[...], path_low[...]
    )
    down = first[:, :rank] + second[:, rank:]

    rows = []
    for leaf in range(leaf_dev):
        picked = []
        for slot in range(slots):
            used = slot < far_count_s[leaf]
            spot = far_ids_s[leaf, slot]
            tile = tile_of(lax.shift_right_logical(spot, 3), spot & (leaf_dev - 1))
            picked.append(jnp.where(used, tile, 0.0))
        rows.append(row_of(picked))
    edges = []
    for offset in (-1, 1):
        other = me + offset
        inside = lax.shift_right_arithmetic(other, 3) == group
        here = group_ref[other & (GROUP - 1), start:, :]
        chosen = jnp.where(inside, here, half_ref[REACH * start : REACH * start + edge_rows, :])
        edges.append(
            jnp.concatenate(
                [chosen[part * vectors : (part + 1) * vectors] for part in range(per_leaf)], axis=1
            )
        )

    for copy in copies[6:]:
        copy.wait()
    edge_parts = [
        dot_halves(edges[index], edge_high[index], edge_low[index], NN) for index in range(2)
    ]
    left_half = lax.broadcasted_iota(jnp.int32, (vectors, 2 * rank), 1) < rank
    for pair in range(leaf_dev // 2):
        two = (2 * pair, 2 * pair + 1)
        first, second = pair_dot(rows[two[0]], rows[two[1]], leaf_high[pair], leaf_low[pair])
        lift = dot_halves(down, lift_high[pair], lift_low[pair], NN)
        first = jnp.where(left_half, first + lift, 0.0)
        second = jnp.where(left_half, 0.0, second + lift)
        products = pair_dot(first, second, bases_high[pair], bases_low[pair])
        for leaf, product in zip(two, products):
            y_leaf = near_ref[leaf] + product
            if leaf == 0:
                y_leaf = y_leaf + edge_parts[0]
            if leaf == leaf_dev - 1:
                y_leaf = y_leaf + edge_parts[1]
            y_tree[:, leaf * leaf_size : (leaf + 1) * leaf_size] = y_leaf

    y = y_tree[...]
    for tile in range(points_dev // LANES):
        spot = inverse_ref[tile : tile + 1, :]
        out_ref[:, tile * LANES : (tile + 1) * LANES] = lane_gather(
            y, lax.shift_right_logical(spot, 7), spot & (LANES - 1)
        )


def local(
    devices,
    points,
    order,
    bases,
    lift,
    near_ids,
    near_blocks,
    far_ids,
    far_count,
    far_blocks,
    transfer,
    couple,
    links,
    top_couple,
):
    me = lax.axis_index("leaf").astype(jnp.int32).reshape(1)
    vectors, points_dev = points.shape
    leaf_dev, leaf_size, rank = bases.shape
    slots = near_ids.shape[1]
    far_slots = far_ids.shape[1]
    bases_t = jnp.swapaxes(bases, 1, 2)
    tiles = points_dev // LANES
    edge_rows = vectors * (leaf_size // LANES)
    rows = (leaf_dev + 1) * TILE
    groups = devices // GROUP
    order_tiles = order.reshape(tiles, LANES)
    shape = jax.ShapeDtypeStruct

    group_out, tree_x = pl.pallas_call(
        up_kernel,
        out_shape=[
            shape((GROUP, rows + edge_rows, LANES), F32),
            shape((leaf_dev, vectors, leaf_size), F32),
        ],
        in_specs=[SMEM] + [HBM] * 4,
        out_specs=[VMEM] * 2,
        scratch_shapes=[
            pltpu.VMEM(points.shape, F32),
            pltpu.VMEM((tiles, LANES), jnp.int32),
            pltpu.VMEM(bases_t.shape, F32),
            pltpu.VMEM(lift.shape, F32),
            pltpu.SemaphoreType.DMA((4,)),
        ],
        compiler_params=PARAMS,
        name="up",
    )(me, points, order_tiles, bases_t, lift)

    aligned = [[g * GROUP + i for i in range(GROUP)] for g in range(groups)]
    group_in = lax.all_to_all(group_out, "leaf", 0, 0, axis_index_groups=aligned, tiled=True)

    ids_t = near_ids.T
    both = lambda *size: [shape(size, BF16)] * 2

    links_own = links.reshape(links.shape[1:])
    path_rows = (DEPTH * len(OFFSETS) + 2) // 2 * rank
    operands = (
        ids_t,
        links_own,
        transfer,
        couple,
        tree_x,
        top_couple,
        lift,
        order.reshape(1, points_dev),
        far_blocks,
        bases_t.reshape(leaf_dev // 2, 2 * rank, leaf_size),
        near_blocks,
    )
    results = (
        both(14 * rank, rank)
        + both(path_rows, 2 * rank)
        + [shape((tiles, LANES), jnp.int32)]
        + both(leaf_dev // 2, far_slots * rank, 2 * rank)
        + both(leaf_dev // 2, rank, 2 * rank)
        + both(leaf_dev // 2, 2 * rank, leaf_size)
        + both(2, leaf_size, leaf_size)
        + [shape(tree_x.shape, F32)]
    )
    (
        up_high,
        up_low,
        path_high,
        path_low,
        inverse,
        leaf_high,
        leaf_low,
        lift_high,
        lift_low,
        bases_high,
        bases_low,
        edge_high,
        edge_low,
        near_part,
    ) = pl.pallas_call(
        side_kernel,
        out_shape=results,
        in_specs=[SMEM] + [HBM] * len(operands),
        out_specs=[HBM] * len(results),
        scratch_shapes=[
            (pltpu.SMEM if x is ids_t or x is links_own else pltpu.VMEM)(x.shape, x.dtype)
            for x in operands
        ]
        + [pltpu.VMEM(x.shape, x.dtype) for x in results]
        + [
            pltpu.SemaphoreType.DMA((10,)),
            pltpu.SemaphoreType.DMA((leaf_dev // 2,)),
            pltpu.SemaphoreType.DMA((len(results),)),
        ],
        compiler_params=PARAMS,
        cost_estimate=pl.CostEstimate(
            flops=250 * 12_000_000, bytes_accessed=12_000_000, transcendentals=0
        ),
        name="side",
    )(me, *operands)

    by_permute = groups == 4
    half_out, nodes_out, far_nodes, side_nodes = pl.pallas_call(
        functools.partial(middle_kernel, leaf_dev),
        out_shape=[
            shape((REACH * rows + edge_rows + NODES * TILE, LANES), F32),
            shape((1 if by_permute else groups, NODES, TILE, LANES), F32),
            shape((3, TILE, LANES), F32),
            shape((4, TILE, LANES), F32),
        ],
        in_specs=[SMEM] + [HBM] * 3,
        out_specs=[VMEM] * 4,
        scratch_shapes=[
            pltpu.VMEM((GROUP, TILE, LANES), F32),
            pltpu.VMEM(up_high.shape, BF16),
            pltpu.VMEM(up_low.shape, BF16),
            pltpu.SemaphoreType.DMA((3,)),
            pltpu.SemaphoreType.DMA((REACH + 1,)),
        ],
        compiler_params=PARAMS,
        name="middle",
    )(me, group_in, up_high, up_low)

    def shifted(x, low, high):
        pairs = []
        for device in range(devices):
            by = low if device % GROUP < REACH else high
            pairs.append(((device + by * GROUP) % devices, device))
        return lax.ppermute(x, "leaf", pairs)

    half_in = shifted(half_out, -1, 1)
    if by_permute:
        node_parts = (nodes_out, shifted(side_nodes, 1, -1), shifted(far_nodes, 2, 2))
    else:
        across = [[g * GROUP + i for g in range(groups)] for i in range(GROUP)]
        node_parts = (lax.all_to_all(nodes_out, "leaf", 0, 0, axis_index_groups=across, tiled=True),)

    operands = (
        group_in,
        half_in,
        far_ids,
        far_count,
        path_high,
        path_low,
        leaf_high,
        leaf_low,
        lift_high,
        lift_low,
        edge_high,
        edge_low,
        bases_high,
        bases_low,
        near_part,
        inverse,
    )
    return pl.pallas_call(
        functools.partial(down_kernel, len(node_parts)),
        out_shape=shape((vectors, points_dev), F32),
        in_specs=[SMEM] + [HBM] * (len(node_parts) + len(operands)),
        out_specs=VMEM,
        scratch_shapes=[
            (pltpu.SMEM if x is far_ids or x is far_count else pltpu.VMEM)(x.shape, x.dtype)
            for x in operands
        ]
        + [
            pltpu.VMEM((groups, NODES, TILE, LANES), F32),
            pltpu.VMEM((vectors, points_dev), F32),
            pltpu.SemaphoreType.DMA((len(operands),)),
            pltpu.SemaphoreType.DMA((4,)),
        ],
        compiler_params=PARAMS,
        name="down",
    )(me, *node_parts, *operands)


def solution(mesh):
    in_specs = (
        P(None, "leaf"),
        P("leaf"),
        P("leaf", None, None),
        P("leaf", None, None),
        P("leaf", None),
        P("leaf", None, None, None),
        P("leaf", None),
        P("leaf"),
        P("leaf", None, None, None),
        P(),
        P(),
        P("leaf", None, None),
        P(),
    )
    return jax.shard_map(
        functools.partial(local, mesh.shape["leaf"]),
        mesh=mesh,
        in_specs=in_specs,
        out_specs=P(None, "leaf"),
        check_vma=False,
    )
```

```python
import functools

import jax
import jax.numpy as jnp
from jax import lax
from jax.experimental import pallas as pl
from jax.experimental.pallas import tpu as pltpu
from jax.sharding import PartitionSpec as P

REACH = 4
DEPTH = 4
OFFSETS = (-3, -2, 2, 3)
GROUP = 2 * REACH
LANES = 128
TILE = 8
NODES = GROUP - 1
VMEM_LIMIT = 64 * 1024 * 1024

NN = (((1,), (0,)), ((), ()))
NT = (((1,), (1,)), ((), ()))

VMEM = pl.BlockSpec(memory_space=pltpu.VMEM)
SMEM = pl.BlockSpec(memory_space=pltpu.SMEM)
HBM = pl.BlockSpec(memory_space=pltpu.HBM)
PARAMS = pltpu.CompilerParams(vmem_limit_bytes=VMEM_LIMIT)
F32 = jnp.float32
BF16 = jnp.bfloat16


def halves(x):
    high = x.astype(BF16)
    low = (x - high.astype(F32)).astype(BF16)
    return high, low


def dot_halves(a, b_high, b_low, dims):
    a_high, a_low = halves(a)
    rows = a.shape[0]
    both = lax.dot_general(
        jnp.concatenate([a_high, a_low], axis=0), b_high, dims, preferred_element_type=F32
    )
    cross = lax.dot_general(a_high, b_low, dims, preferred_element_type=F32)
    return both[:rows] + (both[rows:] + cross)


def pair_dot(a, b, w_high, w_low):
    a_high, a_low = halves(a)
    b_high, b_low = halves(b)
    rows = a.shape[0]
    both = lax.dot_general(
        jnp.concatenate([a_high, b_high, a_low, b_low], axis=0),
        w_high,
        NN,
        preferred_element_type=F32,
    )
    cross = lax.dot_general(
        jnp.concatenate([a_high, b_high], axis=0), w_low, NN, preferred_element_type=F32
    )
    total = both[: 2 * rows] + (both[2 * rows :] + cross)
    return total[:rows], total[rows:]


def dot3(a, b, dims):
    return dot_halves(a, *halves(b), dims)


def fold(x):
    return jnp.concatenate([x[:TILE], x[TILE:]], axis=1)


def beside(p, q):
    rank = p.shape[1] // 2
    left = lax.broadcasted_iota(jnp.int32, p.shape, 1) < rank
    return jnp.concatenate(
        [
            jnp.where(left, p, pltpu.roll(q, rank, 1)),
            jnp.where(left, pltpu.roll(p, rank, 1), q),
        ],
        axis=0,
    )


def row_of(tiles):
    return jnp.concatenate([beside(*tiles[k : k + 2]) for k in range(0, len(tiles), 2)], axis=1)


def lane_gather(x, high, low):
    rows, columns = x.shape
    high = jnp.broadcast_to(high, (rows, LANES))
    low = jnp.broadcast_to(low, (rows, LANES))
    result = jnp.zeros((rows, LANES), x.dtype)
    for source in range(columns // LANES):
        tile = x[:, source * LANES : (source + 1) * LANES]
        moved = jnp.take_along_axis(tile, low, axis=1, mode="promise_in_bounds")
        result = jnp.where(high == source, moved, result)
    return result


def fetch(pairs, sems):
    copies = [
        pltpu.make_async_copy(source, target, sems.at[index])
        for index, (source, target) in enumerate(pairs)
    ]
    for copy in copies:
        copy.start()
    return copies


def up_kernel(
    me_ref, points_hbm, order_hbm, bases_hbm, lift_hbm, out, x_out, points_v, order_v, bases_v, lift_v, sems
):
    copies = fetch(
        [(order_hbm, order_v), (points_hbm, points_v), (bases_hbm, bases_v), (lift_hbm, lift_v)], sems
    )
    me = me_ref[0]
    leaf_dev, rank, leaf_size = bases_v.shape
    vectors, points_dev = points_v.shape
    copies[0].wait()
    copies[1].wait()
    points = points_v[...]
    per_leaf = leaf_size // LANES
    for t in range(points_dev // LANES):
        spot = order_v[t : t + 1, :] - me * points_dev
        column = t % per_leaf * LANES
        x_out[t // per_leaf, :, column : column + LANES] = lane_gather(
            points, lax.shift_right_logical(spot, 7), spot & (LANES - 1)
        )
    copies[2].wait()
    coefs = [dot3(x_out[leaf], bases_v[leaf], NT) for leaf in range(leaf_dev)]
    tiles = [fold(coef) for coef in coefs]
    copies[3].wait()
    weights = lift_v[...].reshape(leaf_dev * rank, rank)
    tiles.append(fold(dot3(jnp.concatenate(coefs, axis=1), weights, NN)))
    for peer in range(GROUP):
        for index, tile in enumerate(tiles):
            out[peer, index * TILE : (index + 1) * TILE, :] = tile
    place = lax.rem(me, GROUP)
    start = len(tiles) * TILE
    for part in range(per_leaf):
        first = x_out[0, :, part * LANES : (part + 1) * LANES]
        last = x_out[leaf_dev - 1, :, part * LANES : (part + 1) * LANES]
        rows = slice(start + part * vectors, start + (part + 1) * vectors)
        for peer in range(GROUP):
            above = lax.rem(place + 1, GROUP) == peer
            out[peer, rows, :] = jnp.where(above, last, first)


def side_kernel(me_ref, *refs):
    inputs, outputs = refs[:11], refs[11:25]
    held, results = refs[25:36], refs[36:50]
    sems, block_sems, out_sems = refs[50:]
    ids_s, links_s, transfer_v, couple_v, x_v, top_v, lift_v, order_v, far_v, bases_v, blocks_v = held
    (
        up_high,
        up_low,
        path_high,
        path_low,
        inverse_out,
        leaf_high,
        leaf_low,
        lift_high,
        lift_low,
        bases_high,
        bases_low,
        edge_high,
        edge_low,
        near_out,
    ) = results
    leaf_dev, slots, leaf_size, _ = blocks_v.shape
    rank = top_v.shape[0]
    pairs = leaf_dev // 2
    me = me_ref[0]
    first = fetch(list(zip(inputs[:8], held[:8])), sems)

    def block(pair):
        two = pl.ds(2 * pair, 2)
        return fetch([(inputs[10].at[two], blocks_v.at[two])], block_sems.at[pl.ds(pair, 1)])

    blocks = block(0)
    second = fetch(list(zip(inputs[8:10], held[8:10])), sems.at[pl.ds(8, 2)])
    for pair in range(1, pairs):
        blocks += block(pair)
    writes = []

    def write(*indices):
        for index in indices:
            writes.extend(fetch([(results[index], outputs[index])], out_sems.at[pl.ds(index, 1)]))

    def couplings(level):
        weights = [
            links_s[level, column].astype(F32) * couple_v[level, column]
            for column in range(len(OFFSETS))
        ]
        return jnp.concatenate(weights, axis=1)

    def chain():
        bits = [lax.shift_right_logical(me, level) & 1 for level in range(DEPTH)]
        up = transfer_v[0].reshape(2 * rank, rank)
        path = transfer_v[0, bits[0]]
        parts = [couplings(0)]
        row = 0
        for level in range(1, DEPTH):
            rows = up.shape[0]
            up_high[row : row + rows], up_low[row : row + rows] = halves(up)
            row += rows
            if level < DEPTH - 1:
                up = jnp.concatenate(
                    [dot3(up, transfer_v[level, side], NN) for side in range(2)], axis=0
                )
            parts.append(dot3(path, couplings(level), NN))
            path = dot3(path, transfer_v[level, bits[level]], NN)
            if level < DEPTH - 1:
                yield
        write(0, 1)
        top = dot3(path, top_v[...], NN)
        yield
        parts = [x[:, k * rank : (k + 1) * rank] for x in parts for k in range(len(OFFSETS))]
        parts += [dot3(top, transfer_v[DEPTH - 1, side], NT) for side in range(2)]
        half = len(parts) // 2
        for index in range(half):
            span = slice(index * rank, (index + 1) * rank)
            both = jnp.concatenate([parts[index], parts[half + index]], axis=0).T
            path_high[span], path_low[span] = halves(both)
        write(2, 3)

    def inverse():
        points_dev = order_v.shape[1]
        tiles = points_dev // LANES
        spot = order_v[...] - me * points_dev
        times = lax.broadcasted_iota(jnp.int32, (1, points_dev), 1)
        shape = (tiles, points_dev)
        match = lax.broadcasted_iota(jnp.int32, shape, 0) == lax.shift_right_logical(spot, 7)
        digits = [
            jnp.where(match, jnp.broadcast_to(digit.astype(F32), shape), 0.0)
            for digit in (lax.shift_right_logical(times, 4), times & 15)
        ]
        shape = (LANES, points_dev)
        match = lax.broadcasted_iota(jnp.int32, shape, 0) == (spot & (LANES - 1))
        both = lax.dot_general(
            jnp.concatenate(digits, axis=0).astype(BF16),
            jnp.where(match, 1.0, 0.0).astype(BF16),
            NT,
            preferred_element_type=F32,
        )
        inverse_out[...] = (both[:tiles] * 16.0 + both[tiles:]).astype(jnp.int32)
        write(4)

    def transposes(pair):
        two = range(2 * pair, 2 * pair + 2)
        for slot in range(far_v.shape[1]):
            span = slice(slot * rank, (slot + 1) * rank)
            both = jnp.concatenate([far_v[leaf, slot] for leaf in two], axis=0).T
            leaf_high[pair, span], leaf_low[pair, span] = halves(both)
        both = jnp.concatenate([lift_v[leaf] for leaf in two], axis=0).T
        lift_high[pair], lift_low[pair] = halves(both)
        bases_high[pair], bases_low[pair] = halves(bases_v[pair])

    def near(leaf):
        total = jnp.zeros(near_out.shape[1:], F32)
        for slot in range(slots):
            local = ids_s[slot, leaf] - me * leaf_dev
            here = (local >= 0) & (local < leaf_dev)
            x_leaf = jnp.where(here, x_v[jnp.clip(local, 0, leaf_dev - 1)], 0.0)
            total = total + dot3(x_leaf, blocks_v[leaf, slot], NT)
        near_out[leaf] = total

    def edge(index, leaf, outside):
        total = jnp.zeros((leaf_size, leaf_size), F32)
        for slot in range(1, slots):
            remote = ids_s[slot, leaf] - me * leaf_dev == outside
            total = total + jnp.where(remote, blocks_v[leaf, slot], 0.0)
        edge_high[index], edge_low[index] = halves(total.T)

    for copy in first:
        copy.wait()
    links = chain()
    next(links)
    for pair in range(pairs):
        blocks[pair].wait()
        if pair == 0:
            for copy in second:
                copy.wait()
        near(2 * pair)
        near(2 * pair + 1)
        transposes(pair)
        next(links, None)
        if pair == 0:
            edge(0, 0, -1)
        if pair == 1:
            inverse()
        if pair == pairs - 1:
            edge(1, leaf_dev - 1, leaf_dev)
    for _ in links:
        pass
    write(*range(5, 14))
    for copy in writes:
        copy.wait()


def middle_kernel(
    leaf_dev,
    me_ref,
    group_hbm,
    up_high_hbm,
    up_low_hbm,
    half_out,
    nodes_out,
    far_out,
    side_out,
    roots_v,
    up_high,
    up_low,
    sems,
    half_sems,
):
    low = lax.rem(me_ref[0], GROUP) < REACH
    copies = fetch(
        [
            (group_hbm.at[:, pl.ds(leaf_dev * TILE, TILE), :], roots_v),
            (up_high_hbm, up_high),
            (up_low_hbm, up_low),
        ],
        sems,
    )
    rows = (leaf_dev + 1) * TILE
    edge_rows = group_hbm.shape[1] - rows
    first = jnp.where(low, REACH, 0)
    moves = [
        (group_hbm.at[first + part, pl.ds(0, rows)], half_out.at[pl.ds(part * rows, rows)])
        for part in range(REACH)
    ]
    moves.append(
        (
            group_hbm.at[jnp.where(low, GROUP - 1, 0), pl.ds(rows, edge_rows)],
            half_out.at[pl.ds(REACH * rows, edge_rows)],
        )
    )
    moves = fetch(moves, half_sems)
    for copy in copies:
        copy.wait()
    roots = [roots_v[peer] for peer in range(GROUP)]
    start, tiles = 0, []
    for level in range(1, DEPTH):
        width = 1 << level
        count = GROUP // width
        left = jnp.concatenate(
            [row_of(roots[n * width : (n + 1) * width]) for n in range(count)], axis=0
        )
        size = left.shape[1]
        nodes = dot_halves(left, up_high[start : start + size], up_low[start : start + size], NN)
        start += size
        tiles += [fold(nodes[n * 2 * TILE : (n + 1) * 2 * TILE]) for n in range(count)]
    row = REACH * rows + edge_rows
    for index, tile in enumerate(tiles):
        half_out[row + index * TILE : row + (index + 1) * TILE, :] = tile
        for peer in range(nodes_out.shape[0]):
            nodes_out[peer, index] = tile
    for index in range(3):
        side_out[1 + index] = tiles[NODES - 3 + index]
    side_out[0] = jnp.where(low, tiles[0], tiles[3])
    far_out[0] = jnp.where(low, tiles[5], tiles[4])
    far_out[1] = tiles[6]
    for copy in moves:
        copy.wait()


def down_kernel(parts, me_ref, *refs):
    node_parts, refs = refs[:parts], refs[parts:]
    count = (len(refs) - 5) // 2
    out_ref = refs[count]
    held = refs[count + 1 : 2 * count + 1]
    nodes_ref, y_tree, sems, node_sems = refs[2 * count + 1 :]
    me = me_ref[0]
    groups = nodes_ref.shape[0]
    group = lax.shift_right_logical(me, 3)
    place = me & (GROUP - 1)
    low = place < REACH
    if parts > 1:
        near_by, far_by = jnp.where(low, groups - 1, 1), jnp.where(low, 1, groups - 1)
        across = lax.rem(group + 2, groups)
        near_group = lax.rem(group + near_by, groups)
        far_group = lax.rem(group + far_by, groups)
        node_copies = fetch(
            [
                (node_parts[0].at[0], nodes_ref.at[group]),
                (node_parts[1].at[0], nodes_ref.at[far_group, jnp.where(low, 0, 3)]),
                (node_parts[1].at[pl.ds(1, 3)], nodes_ref.at[far_group, pl.ds(NODES - 3, 3)]),
                (node_parts[2].at[0], nodes_ref.at[across, jnp.where(low, 5, 4)]),
                (node_parts[2].at[1], nodes_ref.at[across, NODES - 1]),
            ],
            node_sems,
        )
    else:
        node_copies = fetch([(node_parts[0], nodes_ref)], node_sems)
    copies = fetch(list(zip(refs[:count], held)), sems)
    (
        group_ref,
        half_ref,
        far_ids_s,
        far_count_s,
        path_high,
        path_low,
        leaf_high,
        leaf_low,
        lift_high,
        lift_low,
        edge_high,
        edge_low,
        bases_high,
        bases_low,
        near_ref,
        inverse_ref,
    ) = held
    leaf_dev, vectors, leaf_size = near_ref.shape
    points_dev = out_ref.shape[1]
    slots = far_ids_s.shape[1]
    per_leaf = leaf_size // LANES
    rank = bases_high.shape[1] // 2
    start = (leaf_dev + 1) * TILE
    edge_rows = group_ref.shape[1] - start

    def tile_of(subtree, index):
        other = subtree & (GROUP - 1)
        inside = lax.shift_right_arithmetic(subtree, 3) == group
        row = pl.multiple_of(index * TILE, TILE)
        near_row = jnp.clip(other - jnp.where(low, REACH, 0), 0, REACH - 1) * start
        here = group_ref[other, pl.ds(row, TILE), :]
        there = half_ref[pl.ds(pl.multiple_of(near_row + row, TILE), TILE), :]
        return jnp.where(inside, here, there)

    for copy in node_copies + copies[:6]:
        copy.wait()
    if parts > 1:
        for index in range(NODES):
            row = half_ref.shape[0] - (NODES - index) * TILE
            tile = half_ref[row : row + TILE, :]
            nodes_ref[near_group, index] = tile
    partners = []
    for level in range(DEPTH):
        node = lax.shift_right_logical(me, level)
        size = (groups * GROUP) >> level
        for offset in OFFSETS:
            other = node + offset
            used = (other >= 0) & (other < size)
            other = jnp.clip(other, 0, size - 1)
            if level == 0:
                tile = tile_of(other, leaf_dev)
            else:
                shift = DEPTH - 1 - level
                first = GROUP - (2 << shift)
                tile = nodes_ref[
                    lax.shift_right_logical(other, shift), first + (other & ((1 << shift) - 1))
                ]
            partners.append(jnp.where(used, tile, 0.0))
    top = lax.shift_right_logical(me, DEPTH)
    for side in range(2):
        blended = jnp.zeros((TILE, LANES), F32)
        for other in range(groups // 2):
            distance = jnp.abs(top - other)
            weight = jnp.where(distance >= 2, 1.0 / jnp.maximum(distance, 1).astype(F32), 0.0)
            blended = blended + weight * nodes_ref[2 * other + side, GROUP - 2]
        partners.append(blended)
    half = len(partners) // 2
    row = row_of(partners)
    first, second = pair_dot(
        row[:, : half * rank], row[:, half * rank :], path_high[...], path_low[...]
    )
    down = first[:, :rank] + second[:, rank:]

    rows = []
    for leaf in range(leaf_dev):
        picked = []
        for slot in range(slots):
            used = slot < far_count_s[leaf]
            spot = far_ids_s[leaf, slot]
            tile = tile_of(lax.shift_right_logical(spot, 3), spot & (leaf_dev - 1))
            picked.append(jnp.where(used, tile, 0.0))
        rows.append(row_of(picked))
    edges = []
    for offset in (-1, 1):
        other = me + offset
        inside = lax.shift_right_arithmetic(other, 3) == group
        here = group_ref[other & (GROUP - 1), start:, :]
        chosen = jnp.where(inside, here, half_ref[REACH * start : REACH * start + edge_rows, :])
        edges.append(
            jnp.concatenate(
                [chosen[part * vectors : (part + 1) * vectors] for part in range(per_leaf)], axis=1
            )
        )

    for copy in copies[6:]:
        copy.wait()
    edge_parts = [
        dot_halves(edges[index], edge_high[index], edge_low[index], NN) for index in range(2)
    ]
    left_half = lax.broadcasted_iota(jnp.int32, (vectors, 2 * rank), 1) < rank
    for pair in range(leaf_dev // 2):
        two = (2 * pair, 2 * pair + 1)
        first, second = pair_dot(rows[two[0]], rows[two[1]], leaf_high[pair], leaf_low[pair])
        lift = dot_halves(down, lift_high[pair], lift_low[pair], NN)
        first = jnp.where(left_half, first + lift, 0.0)
        second = jnp.where(left_half, 0.0, second + lift)
        products = pair_dot(first, second, bases_high[pair], bases_low[pair])
        for leaf, product in zip(two, products):
            y_leaf = near_ref[leaf] + product
            if leaf == 0:
                y_leaf = y_leaf + edge_parts[0]
            if leaf == leaf_dev - 1:
                y_leaf = y_leaf + edge_parts[1]
            y_tree[:, leaf * leaf_size : (leaf + 1) * leaf_size] = y_leaf

    y = y_tree[...]
    for tile in range(points_dev // LANES):
        spot = inverse_ref[tile : tile + 1, :]
        out_ref[:, tile * LANES : (tile + 1) * LANES] = lane_gather(
            y, lax.shift_right_logical(spot, 7), spot & (LANES - 1)
        )


def local(
    devices,
    points,
    order,
    bases,
    lift,
    near_ids,
    near_blocks,
    far_ids,
    far_count,
    far_blocks,
    transfer,
    couple,
    links,
    top_couple,
):
    me = lax.axis_index("leaf").astype(jnp.int32).reshape(1)
    vectors, points_dev = points.shape
    leaf_dev, leaf_size, rank = bases.shape
    slots = near_ids.shape[1]
    far_slots = far_ids.shape[1]
    bases_t = jnp.swapaxes(bases, 1, 2)
    tiles = points_dev // LANES
    edge_rows = vectors * (leaf_size // LANES)
    rows = (leaf_dev + 1) * TILE
    groups = devices // GROUP
    order_tiles = order.reshape(tiles, LANES)
    shape = jax.ShapeDtypeStruct

    group_out, tree_x = pl.pallas_call(
        up_kernel,
        out_shape=[
            shape((GROUP, rows + edge_rows, LANES), F32),
            shape((leaf_dev, vectors, leaf_size), F32),
        ],
        in_specs=[SMEM] + [HBM] * 4,
        out_specs=[VMEM] * 2,
        scratch_shapes=[
            pltpu.VMEM(points.shape, F32),
            pltpu.VMEM((tiles, LANES), jnp.int32),
            pltpu.VMEM(bases_t.shape, F32),
            pltpu.VMEM(lift.shape, F32),
            pltpu.SemaphoreType.DMA((4,)),
        ],
        compiler_params=PARAMS,
        name="up",
    )(me, points, order_tiles, bases_t, lift)

    aligned = [[g * GROUP + i for i in range(GROUP)] for g in range(groups)]
    group_in = lax.all_to_all(group_out, "leaf", 0, 0, axis_index_groups=aligned, tiled=True)

    ids_t = near_ids.T
    both = lambda *size: [shape(size, BF16)] * 2

    links_own = links.reshape(links.shape[1:])
    path_rows = (DEPTH * len(OFFSETS) + 2) // 2 * rank
    operands = (
        ids_t,
        links_own,
        transfer,
        couple,
        tree_x,
        top_couple,
        lift,
        order.reshape(1, points_dev),
        far_blocks,
        bases_t.reshape(leaf_dev // 2, 2 * rank, leaf_size),
        near_blocks,
    )
    results = (
        both(14 * rank, rank)
        + both(path_rows, 2 * rank)
        + [shape((tiles, LANES), jnp.int32)]
        + both(leaf_dev // 2, far_slots * rank, 2 * rank)
        + both(leaf_dev // 2, rank, 2 * rank)
        + both(leaf_dev // 2, 2 * rank, leaf_size)
        + both(2, leaf_size, leaf_size)
        + [shape(tree_x.shape, F32)]
    )
    (
        up_high,
        up_low,
        path_high,
        path_low,
        inverse,
        leaf_high,
        leaf_low,
        lift_high,
        lift_low,
        bases_high,
        bases_low,
        edge_high,
        edge_low,
        near_part,
    ) = pl.pallas_call(
        side_kernel,
        out_shape=results,
        in_specs=[SMEM] + [HBM] * len(operands),
        out_specs=[HBM] * len(results),
        scratch_shapes=[
            (pltpu.SMEM if x is ids_t or x is links_own else pltpu.VMEM)(x.shape, x.dtype)
            for x in operands
        ]
        + [pltpu.VMEM(x.shape, x.dtype) for x in results]
        + [
            pltpu.SemaphoreType.DMA((10,)),
            pltpu.SemaphoreType.DMA((leaf_dev // 2,)),
            pltpu.SemaphoreType.DMA((len(results),)),
        ],
        compiler_params=PARAMS,
        cost_estimate=pl.CostEstimate(
            flops=250 * 12_000_000, bytes_accessed=12_000_000, transcendentals=0
        ),
        name="side",
    )(me, *operands)

    by_permute = groups == 4
    half_out, nodes_out, far_nodes, side_nodes = pl.pallas_call(
        functools.partial(middle_kernel, leaf_dev),
        out_shape=[
            shape((REACH * rows + edge_rows + NODES * TILE, LANES), F32),
            shape((1 if by_permute else groups, NODES, TILE, LANES), F32),
            shape((2, TILE, LANES), F32),
            shape((4, TILE, LANES), F32),
        ],
        in_specs=[SMEM] + [HBM] * 3,
        out_specs=[VMEM] * 4,
        scratch_shapes=[
            pltpu.VMEM((GROUP, TILE, LANES), F32),
            pltpu.VMEM(up_high.shape, BF16),
            pltpu.VMEM(up_low.shape, BF16),
            pltpu.SemaphoreType.DMA((3,)),
            pltpu.SemaphoreType.DMA((REACH + 1,)),
        ],
        compiler_params=PARAMS,
        name="middle",
    )(me, group_in, up_high, up_low)

    def shifted(x, low, high):
        pairs = []
        for device in range(devices):
            by = low if device % GROUP < REACH else high
            pairs.append(((device + by * GROUP) % devices, device))
        return lax.ppermute(x, "leaf", pairs)

    half_in = shifted(half_out, -1, 1)
    if by_permute:
        node_parts = (nodes_out, shifted(side_nodes, 1, -1), shifted(far_nodes, 2, 2))
    else:
        across = [[g * GROUP + i for g in range(groups)] for i in range(GROUP)]
        node_parts = (lax.all_to_all(nodes_out, "leaf", 0, 0, axis_index_groups=across, tiled=True),)

    operands = (
        group_in,
        half_in,
        far_ids,
        far_count,
        path_high,
        path_low,
        leaf_high,
        leaf_low,
        lift_high,
        lift_low,
        edge_high,
        edge_low,
        bases_high,
        bases_low,
        near_part,
        inverse,
    )
    return pl.pallas_call(
        functools.partial(down_kernel, len(node_parts)),
        out_shape=shape((vectors, points_dev), F32),
        in_specs=[SMEM] + [HBM] * (len(node_parts) + len(operands)),
        out_specs=VMEM,
        scratch_shapes=[
            (pltpu.SMEM if x is far_ids or x is far_count else pltpu.VMEM)(x.shape, x.dtype)
            for x in operands
        ]
        + [
            pltpu.VMEM((groups, NODES, TILE, LANES), F32),
            pltpu.VMEM((vectors, points_dev), F32),
            pltpu.SemaphoreType.DMA((len(operands),)),
            pltpu.SemaphoreType.DMA((5,)),
        ],
        compiler_params=PARAMS,
        name="down",
    )(me, *node_parts, *operands)


def solution(mesh):
    in_specs = (
        P(None, "leaf"),
        P("leaf"),
        P("leaf", None, None),
        P("leaf", None, None),
        P("leaf", None),
        P("leaf", None, None, None),
        P("leaf", None),
        P("leaf"),
        P("leaf", None, None, None),
        P(),
        P(),
        P("leaf", None, None),
        P(),
    )
    return jax.shard_map(
        functools.partial(local, mesh.shape["leaf"]),
        mesh=mesh,
        in_specs=in_specs,
        out_specs=P(None, "leaf"),
        check_vma=False,
    )
```
